32 devices in a mesh: ctx: 8 (over y, x, core), shard: 4 (over z).
Axes of the slice: x: 2, y: 2, z: 4, core: 2. Of those that a mesh axis runs over, the one named last changes fastest.
Arguments:
- layer_input: bfloat16 [2, 4096, 768], P(None, ('ctx', 'shard')), may hold values from -6 to 6
- attn_gain: bfloat16 [768], P('shard'), may hold values from 0.099609375 to 1.8984375
- attn_shift: bfloat16 [768], P('shard'), may hold values from -3 to 3
- qkv_weight: bfloat16 [768, 2304], P('shard'), may hold values from -0.3125 to 0.3125
- query_bias: bfloat16 [768], P('shard'), may hold values from -3 to 3
- value_bias: bfloat16 [768], P('shard'), may hold values from -3 to 3
- proj_weight: bfloat16 [768, 768], P('shard'), may hold values from -3.5 to 3.5
- proj_bias: bfloat16 [768], P('shard'), may hold values from -1.75 to 1.75
- mlp_gain: bfloat16 [768], P('shard'), may hold values from 0.099609375 to 1.8984375
- mlp_shift: bfloat16 [768], P('shard'), may hold values from -3 to 3
- fc_weight: bfloat16 [768, 3072], P('shard'), may hold values from -0.21875 to 0.21875
- fc_bias: bfloat16 [3072], P('shard'), may hold values from -3 to 3
- out_weight: bfloat16 [3072, 768], P('shard'), may hold values from -0.109375 to 0.109375
- out_bias: bfloat16 [768], P('shard'), may hold values from -1.75 to 1.75
- grad_output: bfloat16 [2, 4096, 768], P(None, ('ctx', 'shard')), may hold values from -6 to 6
Outputs:
- layer_output: bfloat16 [2, 4096, 768], P(None, ('ctx', 'shard'))
- input_grad: bfloat16 [2, 4096, 768], P(None, ('ctx', 'shard'))
- attn_gain_grad: float32 [768], P('shard')
- attn_shift_grad: float32 [768], P('shard')
- qkv_weight_grad: float32 [768, 2304], P('shard')
- query_bias_grad: float32 [768], P('shard')
- value_bias_grad: float32 [768], P('shard')
- proj_weight_grad: float32 [768, 768], P('shard')
- proj_bias_grad: float32 [768], P('shard')
- mlp_gain_grad: float32 [768], P('shard')
- mlp_shift_grad: float32 [768], P('shard')
- fc_weight_grad: float32 [768, 3072], P('shard')
- fc_bias_grad: float32 [3072], P('shard')
- out_weight_grad: float32 [3072, 768], P('shard')
- out_bias_grad: float32 [768], P('shard')
The draws below stay inside these ranges and needn't reach their ends.
All inputs are finite; a program needn't handle non-finite values.
Results may differ from the reference program's by a relative error of at most 0.014.
The reference program's roundings to bfloat16 on the way count: a program that leaves them out, or rounds other values in their place, can miss the bound.
Values may be sent and summed in bfloat16 or wider, within the bound.
No kernel may reach another device: no remote copies, remote signals or barrier semaphores. Data moves between devices by JAX's collectives and lax.ppermute only.
A program may use at most 256 MiB of HBM per device.

```python
import jax
import jax.numpy as jnp
from jax import lax

D = 768
HEADS = 12
HEAD = 64
FF = 3072
SEQS = 2
LENGTH = 4096


def block_levels(key, extent, pieces, smallest, top_value):
    def one(axis_at, parts):
        heights = jax.random.uniform(jax.random.fold_in(jax.random.fold_in(key, 6), axis_at), (parts,), jnp.float32, smallest / len(pieces), top_value / len(pieces))
        return jnp.repeat(jnp.exp(heights), extent[axis_at] // parts).reshape((-1,) + (1,) * (len(extent) - axis_at - 1))

    level = one(*pieces[0])
    for cut in pieces[1:]:
        level = level * one(*cut)
    return level


def centred(key, shape, spread, most, cuts=(), held_as=jnp.bfloat16):
    level = block_levels(key, shape, cuts, -0.22, 0.18) if cuts else 1.0
    values = jax.random.normal(key, shape, jnp.float32) * spread * level
    return jnp.minimum(jnp.maximum(values, -most), most).astype(held_as)


def setup_inputs(seed: int = 0) -> dict:
    key_of = jax.random.split(jax.random.key(seed), 16)
    layer_input = centred(key_of[0], (SEQS, LENGTH, D), 1.0, 6.0, ((1, 32),))
    attn_gain = jnp.clip(1.0 + 0.18 * jax.random.normal(key_of[1], (D,), jnp.float32), 0.099609375, 1.8984375).astype(jnp.bfloat16)
    attn_shift = centred(key_of[2], (D,), 0.5, 3.0, ((0, 4),))
    qkv_weight = centred(key_of[3], (D, 3 * D), (D // 2) ** -0.5, 0.3125, ((0, 4),))
    query_bias = centred(key_of[4], (D,), 0.5, 3.0, ((0, 4),))
    value_bias = centred(key_of[5], (D,), 0.5, 3.0, ((0, 4),))
    proj_weight = centred(key_of[6], (D, D), (max(D // 256, 1)) ** -0.5, 3.5, ((0, 4),))
    proj_bias = centred(key_of[7], (D,), 0.3, 1.75, ((0, 4),))
    mlp_gain = jnp.clip(1.0 + 0.18 * jax.random.normal(key_of[8], (D,), jnp.float32), 0.099609375, 1.8984375).astype(jnp.bfloat16)
    mlp_shift = centred(key_of[9], (D,), 0.5, 3.0, ((0, 4),))
    fc_weight = centred(key_of[10], (D, FF), D ** -0.5, 0.21875, ((0, 4),))
    fc_bias = centred(key_of[11], (FF,), 0.5, 3.0, ((0, 4),))
    out_weight = centred(key_of[12], (FF, D), FF ** -0.5, 0.109375, ((0, 4),))
    out_bias = centred(key_of[13], (D,), 0.3, 1.75, ((0, 4),))
    grad_output = centred(key_of[14], (SEQS, LENGTH, D), 1.0, 6.0, ((1, 32),))
    return {"layer_input": layer_input, "attn_gain": attn_gain, "attn_shift": attn_shift, "qkv_weight": qkv_weight, "query_bias": query_bias, "value_bias": value_bias, "proj_weight": proj_weight, "proj_bias": proj_bias, "mlp_gain": mlp_gain, "mlp_shift": mlp_shift, "fc_weight": fc_weight, "fc_bias": fc_bias, "out_weight": out_weight, "out_bias": out_bias, "grad_output": grad_output}


@jax.custom_vjp
def low(v):
    return lax.optimization_barrier(v.astype(jnp.bfloat16)).astype(jnp.float32)

@jax.custom_vjp
def low_back(v):
    return v

def low_keep(v):
    return (low(v), None)

def low_pass(kept, grad):
    return (grad,)

def back_keep(v):
    return (v, None)

def back_low(kept, grad):
    return (low(grad),)
low.defvjp(low_keep, low_pass)
low_back.defvjp(back_keep, back_low)
highest_precision = lax.Precision.HIGHEST

def layer_norm(values, gain, shift):
    centered = values - lax.optimization_barrier(jnp.mean(values, axis=-1, keepdims=True))
    variance = lax.optimization_barrier(jnp.mean(centered * centered, axis=-1, keepdims=True))
    return centered * lax.rsqrt(variance + 1e-05) * gain + shift

def attend_sequence(queries, keys, values):
    length = queries.shape[0]
    block_rows = min(512, length)
    block_count = length // block_rows
    key_places = jnp.arange(length).astype(jnp.int32)

    def one_block(start):
        picked = lax.dynamic_slice_in_dim(queries, start, block_rows, 0)
        scores = jnp.einsum('qhd,khd->hqk', picked, keys, precision=highest_precision) * 0.125
        scores = low_back(scores)
        query_places = start + jnp.arange(block_rows).astype(jnp.int32)
        allowed = key_places[None, :] <= query_places[:, None]
        scores = jnp.where(allowed[None], scores, -1e+30)
        largest = lax.optimization_barrier(jnp.max(scores, axis=-1, keepdims=True))
        weights = jnp.exp(scores - largest)
        weights = weights / lax.optimization_barrier(jnp.sum(weights, axis=-1, keepdims=True))
        return jnp.einsum('hqk,khd->qhd', low(weights), values, precision=highest_precision)
    starts = (jnp.arange(block_count) * block_rows).astype(jnp.int32)
    outputs = lax.map(jax.checkpoint(one_block), starts)
    return outputs.reshape(length, queries.shape[1], queries.shape[2])

def forward(inputs, gain_one, shift_one, query_key_value_full, query_add, value_add, projection_full_weight, projection_bias_added, gain_two, shift_two, feedforward_full_weight, feedforward_bias_added, output_full_weight, output_bias_added):
    seqs_count, length, width = inputs.shape
    first_normed_input = low(layer_norm(inputs, gain_one, shift_one))
    projected_output = jnp.einsum('axp,pc->axc', first_normed_input, query_key_value_full, precision=highest_precision)
    queries = low_back(low(projected_output[..., :D] + query_add))
    keys = low_back(low(projected_output[..., D:2 * D]))
    values = low_back(low(projected_output[..., 2 * D:] + value_add))
    shape_four = (seqs_count, length, HEADS, HEAD)

    def per_sequence(triple):
        return attend_sequence(triple[0], triple[1], triple[2])
    attention_output = lax.map(per_sequence, (queries.reshape(shape_four), keys.reshape(shape_four), values.reshape(shape_four)))
    attention_output = low_back(low(attention_output.reshape(seqs_count, length, width)))
    residual_branch = low_back(jnp.einsum('axp,pc->axc', attention_output, projection_full_weight, precision=highest_precision) + projection_bias_added)
    middle_state = inputs + residual_branch
    second_normed_input = low(layer_norm(middle_state, gain_two, shift_two))
    preactivation_values = low_back(jnp.einsum('nry,yv->nrv', second_normed_input, feedforward_full_weight, precision=highest_precision) + feedforward_bias_added)
    hidden_state = low(jax.nn.gelu(preactivation_values, approximate=True))
    return middle_state + jnp.einsum('gyh,hp->gyp', hidden_state, output_full_weight, precision=highest_precision) + output_bias_added

def reference(layer_input, attn_gain, attn_shift, qkv_weight, query_bias, value_bias, proj_weight, proj_bias, mlp_gain, mlp_shift, fc_weight, fc_bias, out_weight, out_bias, grad_output):
    floats = [item.astype(jnp.float32) for item in (layer_input, attn_gain, attn_shift, qkv_weight, query_bias, value_bias, proj_weight, proj_bias, mlp_gain, mlp_shift, fc_weight, fc_bias, out_weight, out_bias)]
    result, pullback = jax.vjp(forward, *floats)
    grads = pullback(grad_output.astype(jnp.float32))
    return (result.astype(jnp.bfloat16), grads[0].astype(jnp.bfloat16), grads[1], grads[2], grads[3], grads[4], grads[5], grads[6], grads[7], grads[8], grads[9], grads[10], grads[11], grads[12], grads[13])
```

```python
import functools

import jax
import jax.numpy as jnp
from jax import lax
from jax.experimental import pallas as pl
from jax.experimental.pallas import tpu as pltpu
from jax.sharding import PartitionSpec as P

HEADS = 12
HEAD = 64
TILE = 512
EXP2_SCALE = 0.125 * 1.4426950408889634
f32 = jnp.float32
bf16 = jnp.bfloat16
VMEM_LIMIT = 56 * 1024 * 1024


def layer_norm(values, gain, shift):
    centered = values - jnp.mean(values, axis=-1, keepdims=True)
    variance = jnp.mean(centered * centered, axis=-1, keepdims=True)
    return centered * lax.rsqrt(variance + 1e-05) * gain + shift


def gelu_tanh(values):
    return jax.nn.gelu(values, approximate=True)


def swapped(block, bit):
    n = lax.axis_size("ctx")
    return lax.ppermute(block, "ctx", [(i, i ^ (1 << bit)) for i in range(n)])


def mirrored(block):
    n = lax.axis_size("ctx")
    return lax.ppermute(block, "ctx", [(i, n - 1 - i) for i in range(n)])


def shifted(block, distance):
    n = lax.axis_size("shard")
    return lax.ppermute(block, "shard", [(i, (i + distance) % n) for i in range(n)])


def dot(a, b, contract):
    return lax.dot_general(a, b, ((contract[0], contract[1]), ((), ())), preferred_element_type=f32)


def gather_small(block):
    n = lax.axis_size("shard")
    me = lax.axis_index("shard")
    held = jnp.stack([block] + [shifted(block, d) for d in range(1, n)])
    return jnp.take(held, (me - jnp.arange(n)) % n, axis=0)


def reduce_small(parts):
    n = lax.axis_size("shard")
    me = lax.axis_index("shard")
    total = lax.dynamic_index_in_dim(parts, me, 0, False)
    for d in range(1, n):
        total = total + shifted(lax.dynamic_index_in_dim(parts, (me + d) % n, 0, False), d)
    for bit in range(lax.axis_size("ctx").bit_length() - 1):
        total = total + swapped(total, bit)
    return total


def summed_over_chips(part, bits):
    for bit in bits:
        low = part.astype(bf16)
        part = low.astype(f32) + swapped(low, bit).astype(f32)
    return part


def pair_joined(half, odd):
    other = swapped(half, 0)
    return jnp.stack([jnp.where(odd, other, half), jnp.where(odd, half, other)])


def causal_tile(shape):
    return lax.broadcasted_iota(jnp.int32, shape, 0) <= lax.broadcasted_iota(jnp.int32, shape, 1)


def forward_kernel(heads, slots, block, q_ref, kv_ref, att_ref, out_ref, lse_ref, m_ref, l_ref, acc_ref):
    shards, piece, width = q_ref.shape
    rows = shards * piece
    tile = min(TILE, rows)
    per = rows // tile
    queries = q_ref[...].reshape(rows, width)
    for part in range(per):
        first = block[0] * per + part

        def step(j, masked):
            slot = slots[j // per]
            base = pl.multiple_of((j % per) * tile, tile)
            for h in range(heads):
                q = queries[part * tile : (part + 1) * tile, h * HEAD : (h + 1) * HEAD]
                k = kv_ref[slot, pl.ds(base, tile), h * HEAD : (h + 1) * HEAD]
                v = kv_ref[slot, pl.ds(base, tile), width + h * HEAD : width + (h + 1) * HEAD]
                s = dot(k, q, ((1,), (1,))) * EXP2_SCALE
                if masked:
                    s = jnp.where(causal_tile(s.shape), s, -1e30)
                    m = jnp.max(s, axis=0, keepdims=True)
                    p = jnp.exp2(s - m)
                    l_ref[h] = jnp.sum(p, axis=0, keepdims=True)
                    acc_ref[h] = dot(v, p.astype(bf16), ((0,), (0,)))
                else:
                    old = m_ref[h]
                    m = jnp.maximum(old, jnp.max(s, axis=0, keepdims=True))
                    p = jnp.exp2(s - m)
                    factor = jnp.exp2(old - m)
                    l_ref[h] = l_ref[h] * factor + jnp.sum(p, axis=0, keepdims=True)
                    acc_ref[h] = acc_ref[h] * factor + dot(v, p.astype(bf16), ((0,), (0,)))
                m_ref[h] = m

        step(first, True)

        @pl.loop(0, first)
        def _(j):
            step(j, False)

        for h in range(heads):
            total = l_ref[h]
            done = acc_ref[h] / total
            out_ref[h * HEAD : (h + 1) * HEAD, part * tile : (part + 1) * tile] = done
            lse_ref[h, :, part * tile : (part + 1) * tile] = m_ref[h] + jnp.log2(total)
            low = done.astype(bf16)
            for z in range(tile // piece):
                att_ref[part * (tile // piece) + z, h * HEAD : (h + 1) * HEAD, :] = low[
                    :, z * piece : (z + 1) * piece
                ]


def backward_kernel(heads, slots, block, q_ref, kv_ref, go_ref, out_ref, lse_ref, dq_ref, dkv_ref, acc_ref):
    shards, piece, width = q_ref.shape
    rows = shards * piece
    tile = min(TILE, rows)
    per = rows // tile
    blocks = kv_ref.shape[0] * per
    queries = q_ref[...].reshape(rows, width)
    for part in range(per):
        first = block[0] * per + part
        pieces = range(part * (tile // piece), (part + 1) * (tile // piece))
        span = slice(part * tile, (part + 1) * tile)
        go_all = jnp.concatenate([go_ref[z] for z in pieces], axis=1)

        def step(j, masked):
            slot = slots[j // per]
            base = pl.multiple_of((j % per) * tile, tile)
            keys_at = pl.ds(base, tile)
            for h in range(heads):
                lanes = slice(h * HEAD, (h + 1) * HEAD)
                lanes_v = slice(width + h * HEAD, width + (h + 1) * HEAD)
                q = queries[span, lanes]
                go = go_all[lanes]
                delta = jnp.sum(go.astype(f32) * out_ref[lanes, span], axis=0, keepdims=True)
                k = kv_ref[slot, keys_at, lanes]
                v = kv_ref[slot, keys_at, lanes_v]
                p = jnp.exp2(dot(k, q, ((1,), (1,))) * EXP2_SCALE - lse_ref[h, :, span])
                if masked:
                    p = jnp.where(causal_tile(p.shape), p, 0.0)
                pulled = dot(v, go, ((1,), (0,)))
                slopes = (p * (pulled - delta)).astype(bf16)
                dv = dot(p.astype(bf16), go, ((1,), (1,)))
                dk = dot(slopes, q, ((1,), (0,))) * 0.125
                if part:
                    dk = dk + dkv_ref[slot, keys_at, lanes].astype(f32)
                    dv = dv + dkv_ref[slot, keys_at, lanes_v].astype(f32)
                dkv_ref[slot, keys_at, lanes] = dk.astype(bf16)
                dkv_ref[slot, keys_at, lanes_v] = dv.astype(bf16)
                dq = dot(k, slopes, ((0,), (0,)))
                if masked:
                    acc_ref[h] = dq
                else:
                    acc_ref[h] += dq

        if part == 0:

            @pl.loop(first + 1, blocks)
            def _(j):
                base = pl.multiple_of((j % per) * tile, tile)
                dkv_ref[slots[j // per], pl.ds(base, tile), :] = jnp.zeros((tile, 2 * width), bf16)

        elif part:
            pass
        step(first, True)

        @pl.loop(0, first)
        def _(j):
            step(j, False)

        for h in range(heads):
            low = (acc_ref[h] * 0.125).T.astype(bf16)
            for z in pieces:
                at = (z - part * (tile // piece)) * piece
                dq_ref[z, :, h * HEAD : (h + 1) * HEAD] = low[at : at + piece]


def attend(slots, block, queries, kv):
    shards, piece, width = queries.shape
    rows = shards * piece
    heads = width // HEAD
    tile = min(TILE, rows)
    scores = heads * rows * rows * (kv.shape[0] + 1) // 2
    smem = pl.BlockSpec(memory_space=pltpu.SMEM)
    vmem = pl.BlockSpec(memory_space=pltpu.VMEM)
    return pl.pallas_call(
        functools.partial(forward_kernel, heads),
        out_shape=(
            jax.ShapeDtypeStruct((shards, width, piece), bf16),
            jax.ShapeDtypeStruct((width, rows), f32),
            jax.ShapeDtypeStruct((heads, 1, rows), f32),
        ),
        in_specs=[smem, smem, vmem, vmem],
        out_specs=(vmem, vmem, vmem),
        scratch_shapes=[
            pltpu.VMEM((heads, 1, tile), f32),
            pltpu.VMEM((heads, 1, tile), f32),
            pltpu.VMEM((heads, HEAD, tile), f32),
        ],
        compiler_params=pltpu.CompilerParams(vmem_limit_bytes=VMEM_LIMIT),
        cost_estimate=pl.CostEstimate(
            flops=scores * 16 * HEAD, bytes_accessed=2 * kv.size, transcendentals=scores
        ),
        name="attention_forward",
    )(slots, block, queries, kv)


def attend_back(slots, block, queries, kv, grads, out, lse):
    shards, piece, width = queries.shape
    rows = shards * piece
    heads = width // HEAD
    tile = min(TILE, rows)
    scores = heads * rows * rows * (kv.shape[0] + 1) // 2
    smem = pl.BlockSpec(memory_space=pltpu.SMEM)
    vmem = pl.BlockSpec(memory_space=pltpu.VMEM)
    return pl.pallas_call(
        functools.partial(backward_kernel, heads),
        out_shape=(
            jax.ShapeDtypeStruct((shards, piece, width), bf16),
            jax.ShapeDtypeStruct(kv.shape, bf16),
        ),
        in_specs=[smem, smem, vmem, vmem, vmem, vmem, vmem],
        out_specs=(vmem, vmem),
        scratch_shapes=[pltpu.VMEM((heads, HEAD, tile), f32)],
        compiler_params=pltpu.CompilerParams(vmem_limit_bytes=VMEM_LIMIT),
        cost_estimate=pl.CostEstimate(
            flops=scores * 40 * HEAD, bytes_accessed=4 * kv.size, transcendentals=scores
        ),
        name="attention_backward",
    )(slots, block, queries, kv, grads, out, lse)


def body(
    layer_input,
    attn_gain,
    attn_shift,
    qkv_weight,
    query_bias,
    value_bias,
    proj_weight,
    proj_bias,
    mlp_gain,
    mlp_shift,
    fc_weight,
    fc_bias,
    out_weight,
    out_bias,
    grad_output,
):
    seqs, piece, width = layer_input.shape
    cycle = lax.axis_size("ctx")
    shards = lax.axis_size("shard")
    here = lax.axis_index("ctx")
    shard_at = lax.axis_index("shard")
    odd = here % 2
    bits = cycle.bit_length() - 1
    chip_bits = list(range(1, bits))
    orders = (chip_bits + [0], chip_bits[::-1] + [0])
    rows = shards * piece
    local_width = qkv_weight.shape[0]
    local_hidden = out_weight.shape[0]
    half_hidden = local_hidden // 2
    heads = -(-HEADS // shards)
    group = heads * HEAD
    padded = group * shards
    straight = (seqs + 1) // 2

    def mirror_late(rows_held):
        return jnp.concatenate([rows_held[:straight], mirrored(rows_held[straight:])])

    inputs = mirror_late(layer_input)
    grads = mirror_late(grad_output)
    gathered_inputs = lax.all_gather(inputs, "shard", axis=0)

    packed = jnp.concatenate(
        [
            jnp.stack(
                [attn_gain, attn_shift, query_bias, value_bias, proj_bias, mlp_gain, mlp_shift, out_bias]
            ),
            fc_bias.reshape(-1, local_width),
        ]
    )
    small = gather_small(packed).astype(f32)
    vectors = [small[:, i].reshape(-1) for i in range(8)]
    gain_one, shift_one, query_add, value_add, proj_add, gain_two, shift_two, out_add = vectors
    fc_add = lax.dynamic_index_in_dim(
        small[:, 8:].reshape(shards, 2, half_hidden), odd, 1, False
    ).reshape(-1)

    def own_heads(vector):
        return lax.dynamic_slice_in_dim(
            jnp.pad(vector, (0, padded - width)), shard_at * group, group, 0
        )

    def by_heads(weight):
        parts = jnp.pad(
            weight.reshape(local_width, 3, width), ((0, 0), (0, 0), (0, padded - width))
        ).reshape(local_width, 3, shards, group)
        return parts.transpose(2, 0, 1, 3).reshape(shards, local_width, 3 * group)

    qkv_own = lax.all_to_all(by_heads(qkv_weight), "shard", 0, 0, tiled=True).reshape(
        width, 3 * group
    )
    q_weight = qkv_own[:, :group]
    kv_weight = qkv_own[:, group:]

    proj_full = lax.all_gather(proj_weight, "shard", axis=0, tiled=True)
    fc_half = lax.all_gather(
        lax.dynamic_index_in_dim(
            fc_weight.reshape(local_width, shards, 2, half_hidden), odd, 2, False
        ).reshape(local_width, shards * half_hidden),
        "shard",
        axis=0,
        tiled=True,
    )
    out_half = lax.all_gather(
        lax.dynamic_index_in_dim(out_weight.reshape(2, half_hidden, width), odd, 0, False),
        "shard",
        axis=0,
        tiled=True,
    )

    normed_one = layer_norm(gathered_inputs.astype(f32), gain_one, shift_one).astype(bf16)
    queries = (dot(normed_one, q_weight, ((3,), (0,))) + own_heads(query_add)).astype(bf16)
    kv_add = jnp.concatenate([jnp.zeros((group,), f32), own_heads(value_add)])
    kv_own = (dot(normed_one, kv_weight, ((3,), (0,))) + kv_add).astype(bf16)

    attended_parts = []
    saved = []
    for seq in range(seqs):
        order = orders[seq % 2]
        late = seq >= straight
        held = kv_own[:, seq].reshape(1, rows, 2 * group)
        for bit in order:
            held = jnp.concatenate([held, swapped(held, bit)])
        owners = jnp.arange(cycle)
        if late:
            owners = cycle - 1 - owners
        apart = owners ^ here
        slots = sum(((apart >> bit) & 1) << k for k, bit in enumerate(order)).astype(jnp.int32)
        block = (cycle - 1 - here if late else here).astype(jnp.int32).reshape(1)
        att, out, lse = attend(slots, block, queries[:, seq], held)
        attended_parts.append(att)
        saved.append((order, slots, block, held, out, lse))
    attended = lax.all_to_all(
        jnp.concatenate(attended_parts, axis=2), "shard", 0, 0, tiled=True
    ).reshape(padded, seqs * piece)[:width]

    inputs32 = inputs.astype(f32).reshape(seqs * piece, width)
    grads_own = grads.reshape(seqs * piece, width)
    grads32 = grads_own.astype(f32)
    middle = inputs32 + dot(attended, proj_full, ((0,), (0,))) + proj_add
    normed_two = layer_norm(middle, gain_two, shift_two).astype(bf16)

    normed_pair = jnp.stack([normed_two, swapped(normed_two, 0)])
    grads_pair = jnp.stack([grads_own, swapped(grads_own, 0)])
    preactivation = dot(normed_pair, fc_half, ((2,), (0,))) + fc_add
    hidden = gelu_tanh(preactivation).astype(bf16)
    out_part = dot(hidden, out_half, ((2,), (0,)))
    layer_output = (middle + (out_part[0] + swapped(out_part[1], 0)) + out_add).astype(bf16)
    grad_hidden = dot(grads_pair, out_half, ((2,), (1,)))
    grad_pre = jax.vjp(gelu_tanh, preactivation)[1](grad_hidden)[0].astype(bf16)
    normed_part = dot(grad_pre, fc_half, ((2,), (1,)))
    grad_normed_two = normed_part[0] + swapped(normed_part[1], 0)
    grad_mid_part, gain_two_grad, shift_two_grad = jax.vjp(
        layer_norm, middle, gain_two, shift_two
    )[1](grad_normed_two)
    grad_middle = grads32 + grad_mid_part
    grad_branch = grad_middle.astype(bf16)

    grad_attended = jnp.pad(
        dot(proj_full, grad_branch, ((1,), (1,))).astype(bf16), ((0, padded - width), (0, 0))
    ).reshape(shards, group, seqs * piece)
    grad_heads = lax.all_to_all(grad_attended, "shard", 0, 0, tiled=True)
    query_grads = []
    kv_grads = []
    for seq in range(seqs):
        order, slots, block, held, out, lse = saved[seq]
        dq, dkv = attend_back(
            slots,
            block,
            queries[:, seq],
            held,
            grad_heads[:, :, seq * piece : (seq + 1) * piece],
            out,
            lse,
        )
        query_grads.append(dq)
        for bit in order[::-1]:
            split = dkv.shape[0] // 2
            received = swapped(dkv[split:], bit)
            dkv = (dkv[:split].astype(f32) + received.astype(f32)).astype(bf16)
        kv_grads.append(dkv.reshape(shards, piece, 2 * group))
    query_low = jnp.stack(query_grads, axis=1)
    kv_low = jnp.stack(kv_grads, axis=1)

    normed_part_one = dot(query_low, q_weight, ((3,), (1,))) + dot(kv_low, kv_weight, ((3,), (1,)))
    grad_normed_one = lax.psum_scatter(
        normed_part_one.astype(bf16), "shard", scatter_dimension=0, tiled=False
    ).astype(f32).reshape(seqs * piece, width)
    grad_in_part, gain_one_grad, shift_one_grad = jax.vjp(
        layer_norm, inputs32, gain_one, shift_one
    )[1](grad_normed_one)
    input_grad = (grad_middle + grad_in_part).astype(bf16)
    layer_output = mirror_late(layer_output.reshape(seqs, piece, width))
    input_grad = mirror_late(input_grad.reshape(seqs, piece, width))

    def pair_split(grad):
        parts = grad.astype(bf16).reshape(shards, 2, local_width // 2, -1)
        mine = lax.dynamic_index_in_dim(parts, odd, 1, False)
        sent = lax.dynamic_index_in_dim(parts, 1 - odd, 1, False)
        return (mine.astype(f32) + swapped(sent, 0).astype(f32)).astype(bf16)

    flat_tokens = ((0, 1), (0, 1))
    out_grad = dot(hidden, grads_pair, flat_tokens).astype(bf16)
    out_grad = lax.psum_scatter(
        out_grad.reshape(shards, half_hidden, width), "shard", scatter_dimension=0, tiled=False
    )
    out_grad = pair_joined(summed_over_chips(out_grad, chip_bits[::-1]), odd).reshape(
        local_hidden, width
    )
    fc_grad = dot(normed_pair, grad_pre, flat_tokens).astype(bf16)
    fc_grad = lax.psum_scatter(
        fc_grad.reshape(shards, local_width, -1), "shard", scatter_dimension=0, tiled=False
    )
    fc_grad = pair_joined(summed_over_chips(fc_grad, chip_bits), odd)
    fc_grad = (
        fc_grad.reshape(2, local_width, shards, half_hidden)
        .transpose(1, 2, 0, 3)
        .reshape(local_width, shards * local_hidden)
    )
    proj_grad = lax.psum_scatter(
        pair_split(dot(attended, grad_branch, ((1,), (0,)))), "shard", scatter_dimension=0, tiled=False
    )
    proj_grad = pair_joined(summed_over_chips(proj_grad, chip_bits), odd).reshape(local_width, width)
    tokens3 = ((0, 1, 2), (0, 1, 2))
    qkv_grad = jnp.concatenate(
        [dot(normed_one, query_low, tokens3), dot(normed_one, kv_low, tokens3)], axis=1
    )
    qkv_grad = lax.all_to_all(pair_split(qkv_grad), "shard", 0, 0, tiled=True)
    qkv_grad = pair_joined(summed_over_chips(qkv_grad, chip_bits), odd)
    qkv_grad = (
        qkv_grad.reshape(2, shards, local_width // 2, 3, group)
        .transpose(0, 2, 3, 1, 4)
        .reshape(local_width, 3, padded)[:, :, :width]
        .reshape(local_width, 3 * width)
    )

    fc_add_part = jnp.sum(grad_pre.astype(f32), axis=(0, 1)).reshape(shards, 1, half_hidden)
    fc_add_part = jnp.where(jnp.arange(2)[None, :, None] == odd, fc_add_part, 0.0)
    early = reduce_small(
        jnp.concatenate(
            [
                v.reshape(shards, -1)
                for v in (
                    gain_two_grad,
                    shift_two_grad,
                    jnp.sum(grad_branch.astype(f32), axis=0),
                    jnp.sum(grads32, axis=0),
                    fc_add_part,
                )
            ],
            axis=1,
        )
    )

    def all_heads(vector):
        return lax.dynamic_update_slice_in_dim(
            jnp.zeros((padded,), f32), vector, shard_at * group, 0
        )[:width]

    late_sums = reduce_small(
        jnp.concatenate(
            [
                v.reshape(shards, -1)
                for v in (
                    gain_one_grad,
                    shift_one_grad,
                    all_heads(jnp.sum(query_low.astype(f32), axis=(0, 1, 2))),
                    all_heads(jnp.sum(kv_low[..., group:].astype(f32), axis=(0, 1, 2))),
                )
            ],
            axis=1,
        )
    )
    early_parts = [early[i * local_width : (i + 1) * local_width] for i in range(4)]
    late_parts = [late_sums[i * local_width : (i + 1) * local_width] for i in range(4)]
    return (
        layer_output,
        input_grad,
        late_parts[0],
        late_parts[1],
        qkv_grad,
        late_parts[2],
        late_parts[3],
        proj_grad,
        early_parts[2],
        early_parts[0],
        early_parts[1],
        fc_grad,
        early[4 * local_width :],
        out_grad,
        early_parts[3],
    )


def solution(mesh):
    tokens = P(None, ("ctx", "shard"), None)
    vector = P("shard")
    matrix = P("shard", None)
    return jax.shard_map(
        body,
        mesh=mesh,
        in_specs=(
            tokens,
            vector,
            vector,
            matrix,
            vector,
            vector,
            matrix,
            vector,
            vector,
            vector,
            matrix,
            vector,
            matrix,
            vector,
            tokens,
        ),
        out_specs=(
            tokens,
            tokens,
            vector,
            vector,
            matrix,
            vector,
            vector,
            matrix,
            vector,
            vector,
            vector,
            matrix,
            vector,
            matrix,
            vector,
        ),
        check_vma=False,
    )
```

```python
import functools

import jax
import jax.numpy as jnp
from jax import lax
from jax.experimental import pallas as pl
from jax.experimental.pallas import tpu as pltpu
from jax.sharding import PartitionSpec as P

HEADS = 12
HEAD = 64
TILE = 512
EXP2_SCALE = 0.125 * 1.4426950408889634
f32 = jnp.float32
bf16 = jnp.bfloat16
VMEM_LIMIT = 56 * 1024 * 1024


def normalized(values):
    centered = values - jnp.mean(values, axis=-1, keepdims=True)
    variance = jnp.mean(centered * centered, axis=-1, keepdims=True)
    return centered * lax.rsqrt(variance + 1e-05)


def layer_norm(values, gain, shift):
    return normalized(values) * gain + shift


def gelu_tanh(values):
    return jax.nn.gelu(values, approximate=True)


def swapped(block, bit):
    n = lax.axis_size("ctx")
    return lax.ppermute(block, "ctx", [(i, i ^ (1 << bit)) for i in range(n)])


def sent_up(block, apart, up):
    n = lax.axis_size("ctx")
    pairs = [(i, i ^ apart) for i in range(n) if (i < i ^ apart) == up]
    return lax.ppermute(block, "ctx", pairs)


def mirrored(block):
    n = lax.axis_size("ctx")
    return lax.ppermute(block, "ctx", [(i, n - 1 - i) for i in range(n)])


def shifted(block, distance):
    n = lax.axis_size("shard")
    return lax.ppermute(block, "shard", [(i, (i + distance) % n) for i in range(n)])


def dot(a, b, contract):
    return lax.dot_general(a, b, ((contract[0], contract[1]), ((), ())), preferred_element_type=f32)


def rolled(block, start):
    return lax.dynamic_slice_in_dim(jnp.concatenate([block, block]), start, block.shape[0], 0)


def gather_small(block):
    n = lax.axis_size("shard")
    me = lax.axis_index("shard")
    held = jnp.stack([shifted(block, d) for d in range(n - 1, 0, -1)] + [block])
    return rolled(held, n - 1 - me)


def reduce_small(parts):
    n = lax.axis_size("shard")
    me = lax.axis_index("shard")
    total = lax.dynamic_index_in_dim(parts, me, 0, False)
    for d in range(1, n):
        total = total + shifted(lax.dynamic_index_in_dim(parts, (me + d) % n, 0, False), d)
    for bit in range(lax.axis_size("ctx").bit_length() - 1):
        total = total + swapped(total, bit)
    return total


def summed_over_chips(part, bits):
    for bit in bits:
        low = part.astype(bf16)
        part = low.astype(f32) + swapped(low, bit).astype(f32)
    return part


def pair_joined(half, odd):
    other = swapped(half, 0)
    return jnp.where(odd, other, half), jnp.where(odd, half, other)


def places(count, piece, shards, shard_at, axis):
    shape = (count, 1) if axis == 0 else (1, count)
    index = lax.broadcasted_iota(jnp.int32, shape, axis)
    owner = shard_at - index // piece
    owner = jnp.where(owner < 0, owner + shards, owner)
    return owner * piece + index % piece


def load_blocks(refs, held, sems):
    copies = [pltpu.make_async_copy(ref, held.at[i], sems.at[i]) for i, ref in enumerate(refs)]
    for copy in copies:
        copy.start()
    return copies


def forward_kernel(heads, shards, count, slots, info, q_ref, *refs):
    kv_refs = refs[:count]
    att_ref, out_ref, lse_ref, held, sems, m_ref, l_ref, acc_ref = refs[count:]
    rows, width = q_ref.shape
    piece = rows // shards
    tile = min(TILE, rows)
    per = rows // tile
    copies = load_blocks(kv_refs, held, sems)
    key_places = places(rows, piece, shards, info[1], 0)
    query_places = places(rows, piece, shards, info[1], 1)
    for copy in copies:
        copy.wait()
    for part in range(per):
        span = slice(part * tile, (part + 1) * tile)

        def step(slot, key_part, masked, start):
            keys_at = slice(key_part * tile, (key_part + 1) * tile)
            allowed = key_places[keys_at] <= query_places[:, span] if masked else None
            for h in range(heads):
                lanes = slice(h * HEAD, (h + 1) * HEAD)
                lanes_v = slice(width + h * HEAD, width + (h + 1) * HEAD)
                q = q_ref[span, lanes]
                k = held[slot, keys_at, lanes]
                v = held[slot, keys_at, lanes_v]
                s = dot(k, q, ((1,), (1,))) * EXP2_SCALE
                if masked:
                    s = jnp.where(allowed, s, -1e30)
                m = jnp.max(s, axis=0, keepdims=True)
                if start:
                    p = jnp.exp2(s - m)
                    l_ref[h] = jnp.sum(p, axis=0, keepdims=True)
                    acc_ref[h] = dot(v, p.astype(bf16), ((0,), (0,)))
                else:
                    old = m_ref[h]
                    m = jnp.maximum(old, m)
                    p = jnp.exp2(s - m)
                    factor = jnp.exp2(old - m)
                    l_ref[h] = l_ref[h] * factor + jnp.sum(p, axis=0, keepdims=True)
                    acc_ref[h] = acc_ref[h] * factor + dot(v, p.astype(bf16), ((0,), (0,)))
                m_ref[h] = m

        for key_part in range(per):
            step(slots[info[0]], key_part, True, key_part == 0)

        @pl.loop(0, info[0])
        def _(j):
            for key_part in range(per):
                step(slots[j], key_part, False, False)

        for h in range(heads):
            total = l_ref[h]
            done = acc_ref[h] / total
            out_ref[h * HEAD : (h + 1) * HEAD, span] = done
            lse_ref[h, :, span] = m_ref[h] + jnp.log2(total)
            low = done.astype(bf16)
            for z in range(tile // piece):
                att_ref[part * (tile // piece) + z, h * HEAD : (h + 1) * HEAD, :] = low[
                    :, z * piece : (z + 1) * piece
                ]


def backward_kernel(heads, shards, count, slots, info, q_ref, out_ref, lse_ref, *refs):
    go_refs = refs[:shards]
    kv_refs = refs[shards : shards + count]
    dq_ref, near_ref, far_ref, held, sums, sems, end_sems, acc_ref = refs[shards + count :]
    rows, width = q_ref.shape
    piece = rows // shards
    tile = min(TILE, rows)
    per = rows // tile
    copies = load_blocks(kv_refs, held, sems)
    key_places = places(rows, piece, shards, info[1], 0)
    query_places = places(rows, piece, shards, info[1], 1)

    @pl.loop(info[0] + 1, count)
    def _(j):
        sums[slots[j]] = jnp.zeros((rows, 2 * width), bf16)

    for copy in copies:
        copy.wait()
    for part in range(per):
        span = slice(part * tile, (part + 1) * tile)
        pieces = range(part * (tile // piece), (part + 1) * (tile // piece))
        go_all = jnp.concatenate([go_refs[z][...] for z in pieces], axis=1)
        deltas = []
        for h in range(heads):
            lanes = slice(h * HEAD, (h + 1) * HEAD)
            deltas.append(
                jnp.sum(go_all[lanes].astype(f32) * out_ref[lanes, span], axis=0, keepdims=True)
            )

        def step(slot, key_part, masked, start):
            keys_at = slice(key_part * tile, (key_part + 1) * tile)
            allowed = key_places[keys_at] <= query_places[:, span] if masked else None
            for h in range(heads):
                lanes = slice(h * HEAD, (h + 1) * HEAD)
                lanes_v = slice(width + h * HEAD, width + (h + 1) * HEAD)
                q = q_ref[span, lanes]
                go = go_all[lanes]
                k = held[slot, keys_at, lanes]
                v = held[slot, keys_at, lanes_v]
                p = jnp.exp2(dot(k, q, ((1,), (1,))) * EXP2_SCALE - lse_ref[h, :, span])
                if masked:
                    p = jnp.where(allowed, p, 0.0)
                pulled = dot(v, go, ((1,), (0,)))
                slopes = (p * (pulled - deltas[h])).astype(bf16)
                dv = dot(p.astype(bf16), go, ((1,), (1,)))
                dk = dot(slopes, q, ((1,), (0,))) * 0.125
                if part:
                    dk = dk + sums[slot, keys_at, lanes].astype(f32)
                    dv = dv + sums[slot, keys_at, lanes_v].astype(f32)
                sums[slot, keys_at, lanes] = dk.astype(bf16)
                sums[slot, keys_at, lanes_v] = dv.astype(bf16)
                dq = dot(k, slopes, ((0,), (0,)))
                if start:
                    acc_ref[h] = dq
                else:
                    acc_ref[h] += dq

        for key_part in range(per):
            step(slots[info[0]], key_part, True, key_part == 0)

        @pl.loop(0, info[0])
        def _(j):
            for key_part in range(per):
                step(slots[j], key_part, False, False)

        for h in range(heads):
            dq_ref[span, h * HEAD : (h + 1) * HEAD] = (acc_ref[h] * 0.125).T.astype(bf16)
    half = count // 2
    out_near = pltpu.make_async_copy(sums.at[pl.ds(0, half)], near_ref, end_sems.at[0])
    out_far = pltpu.make_async_copy(sums.at[pl.ds(half, half)], far_ref, end_sems.at[1])
    out_near.start()
    out_far.start()
    out_near.wait()
    out_far.wait()


SMEM = pl.BlockSpec(memory_space=pltpu.SMEM)
VMEM = pl.BlockSpec(memory_space=pltpu.VMEM)
ANY = pl.BlockSpec(memory_space=pl.ANY)


def attend(shards, slots, info, queries, blocks):
    rows, width = queries.shape
    heads = width // HEAD
    count = len(blocks)
    tile = min(TILE, rows)
    scores = heads * rows * rows * (count + 1) // 2
    return pl.pallas_call(
        functools.partial(forward_kernel, heads, shards, count),
        out_shape=(
            jax.ShapeDtypeStruct((shards, width, rows // shards), bf16),
            jax.ShapeDtypeStruct((width, rows), f32),
            jax.ShapeDtypeStruct((heads, 1, rows), f32),
        ),
        in_specs=[SMEM, SMEM, VMEM] + [ANY] * count,
        out_specs=(VMEM, VMEM, VMEM),
        scratch_shapes=[
            pltpu.VMEM((count, rows, 2 * width), bf16),
            pltpu.SemaphoreType.DMA((count,)),
            pltpu.VMEM((heads, 1, tile), f32),
            pltpu.VMEM((heads, 1, tile), f32),
            pltpu.VMEM((heads, HEAD, tile), f32),
        ],
        compiler_params=pltpu.CompilerParams(vmem_limit_bytes=VMEM_LIMIT),
        cost_estimate=pl.CostEstimate(
            flops=scores * 16 * HEAD,
            bytes_accessed=4 * rows * width * (count + 2),
            transcendentals=scores,
        ),
        name="attention_forward",
    )(slots, info, queries, *blocks)


def attend_back(shards, slots, info, queries, out, lse, grads, blocks):
    rows, width = queries.shape
    heads = width // HEAD
    count = len(blocks)
    tile = min(TILE, rows)
    scores = heads * rows * rows * (count + 1) // 2
    part = jax.ShapeDtypeStruct((count // 2, rows, 2 * width), bf16)
    return pl.pallas_call(
        functools.partial(backward_kernel, heads, shards, count),
        out_shape=(jax.ShapeDtypeStruct((rows, width), bf16), part, part),
        in_specs=[SMEM, SMEM, VMEM, VMEM, VMEM] + [VMEM] * shards + [ANY] * count,
        out_specs=(VMEM, ANY, ANY),
        scratch_shapes=[
            pltpu.VMEM((count, rows, 2 * width), bf16),
            pltpu.VMEM((count, rows, 2 * width), bf16),
            pltpu.SemaphoreType.DMA((count,)),
            pltpu.SemaphoreType.DMA((2,)),
            pltpu.VMEM((heads, HEAD, tile), f32),
        ],
        compiler_params=pltpu.CompilerParams(vmem_limit_bytes=VMEM_LIMIT),
        cost_estimate=pl.CostEstimate(
            flops=scores * 40 * HEAD,
            bytes_accessed=8 * rows * width * (count + 2),
            transcendentals=scores,
        ),
        name="attention_backward",
    )(slots, info, queries, out, lse, *grads, *blocks)


def body(
    layer_input,
    attn_gain,
    attn_shift,
    qkv_weight,
    query_bias,
    value_bias,
    proj_weight,
    proj_bias,
    mlp_gain,
    mlp_shift,
    fc_weight,
    fc_bias,
    out_weight,
    out_bias,
    grad_output,
):
    seqs, piece, width = layer_input.shape
    cycle = lax.axis_size("ctx")
    shards = lax.axis_size("shard")
    here = lax.axis_index("ctx")
    shard_at = lax.axis_index("shard")
    odd = here % 2
    chip_bits = list(range(1, cycle.bit_length() - 1))
    rows = shards * piece
    local_width = qkv_weight.shape[0]
    local_hidden = out_weight.shape[0]
    half_width = local_width // 2
    half_hidden = local_hidden // 2
    group = -(-HEADS // shards) * HEAD
    padded = group * shards
    late = [seq >= (seqs + 1) // 2 for seq in range(seqs)]
    tokens = seqs * piece

    def by_heads(weight):
        parts = []
        for third in range(3):
            part = weight[:, third * width : (third + 1) * width]
            parts.append(jnp.pad(part, ((0, 0), (0, padded - width))))
        return jnp.stack(
            [
                jnp.concatenate([part[:, z * group : (z + 1) * group] for part in parts], axis=1)
                for z in range(shards)
            ]
        )

    weight_half = lax.dynamic_slice_in_dim(qkv_weight, odd * half_width, half_width, 0)
    moved = lax.all_to_all(by_heads(weight_half), "shard", 0, 0, tiled=True)
    qkv_own = jnp.stack(pair_joined(moved, odd), axis=1).reshape(width, 3 * group)
    q_weight = qkv_own[:, :group]
    kv_weight = qkv_own[:, group:]

    packed = jnp.concatenate(
        [
            jnp.stack(
                [attn_gain, attn_shift, query_bias, value_bias, proj_bias, mlp_gain, mlp_shift, out_bias]
            ),
            fc_bias.reshape(-1, local_width),
        ]
    )
    small = gather_small(packed).astype(f32)
    vectors = [small[:, i].reshape(-1) for i in range(8)]
    gain_one, shift_one, query_add, value_add, proj_add, gain_two, shift_two, out_add = vectors
    fc_add = lax.dynamic_index_in_dim(
        small[:, 8:].reshape(shards, 2, half_hidden), odd, 1, False
    ).reshape(-1)

    def own_heads(vector):
        return lax.dynamic_slice_in_dim(
            jnp.pad(vector, (0, padded - width)), shard_at * group, group, 0
        )

    kv_add = jnp.concatenate([jnp.zeros((group,), f32), own_heads(value_add)])
    query_add = own_heads(query_add)

    proj_full = lax.all_gather(proj_weight, "shard", axis=0, tiled=True)
    fc_half = lax.all_gather(
        jnp.concatenate(
            [
                lax.dynamic_slice_in_dim(
                    fc_weight, z * local_hidden + odd * half_hidden, half_hidden, 1
                )
                for z in range(shards)
            ],
            axis=1,
        ),
        "shard",
        axis=0,
        tiled=True,
    )
    out_half = lax.all_gather(
        lax.dynamic_slice_in_dim(out_weight, odd * half_hidden, half_hidden, 0),
        "shard",
        axis=0,
        tiled=True,
    )
    proj_heads = rolled(
        jnp.pad(proj_full, ((0, padded - width), (0, 0))).reshape(shards, group, width), shard_at
    ).reshape(padded, width)

    inputs = [mirrored(layer_input[s]) if late[s] else layer_input[s] for s in range(seqs)]
    block_index = [cycle - 1 - here if late[s] else here for s in range(seqs)]
    group_norms, normed_one, queries, blocks, slots, infos = [], [], [], [], [], []
    for s in range(seqs):
        held = jnp.concatenate([inputs[s]] + [shifted(inputs[s], d) for d in range(1, shards)])
        norm = normalized(held.astype(f32))
        normed = (norm * gain_one + shift_one).astype(bf16)
        group_norms.append(norm)
        normed_one.append(normed)
        queries.append((dot(normed, q_weight, ((1,), (0,))) + query_add).astype(bf16))
        own = (dot(normed, kv_weight, ((1,), (0,))) + kv_add).astype(bf16)
        near = [own] + [sent_up(own, 2 * i, not late[s]) for i in range(1, cycle // 2)]
        blocks.append(near + [swapped(block, 0) for block in near])
        owners = jnp.arange(cycle)
        apart = (cycle - 1 - owners if late[s] else owners) ^ here
        slots.append(((apart >> 1) + (apart & 1) * (cycle // 2)).astype(jnp.int32))
        infos.append(jnp.stack([block_index[s], shard_at]).astype(jnp.int32))
    saved = []
    attended_parts = []
    for s in range(seqs):
        att, out, lse = attend(shards, slots[s], infos[s], queries[s], blocks[s])
        saved.append((out, lse))
        attended_parts.append(
            jnp.concatenate([att[0]] + [shifted(att[d], -d) for d in range(1, shards)])
        )
    attended = jnp.concatenate(attended_parts, axis=1)

    inputs32 = jnp.concatenate(inputs).astype(f32)
    grads_own = jnp.concatenate(
        [mirrored(grad_output[s]) if late[s] else grad_output[s] for s in range(seqs)]
    )
    grads32 = grads_own.astype(f32)
    middle = inputs32 + dot(attended, proj_heads, ((0,), (0,))) + proj_add
    normed_two = layer_norm(middle, gain_two, shift_two).astype(bf16)

    normed_pair = jnp.concatenate([normed_two, swapped(normed_two, 0)])
    grads_pair = jnp.concatenate([grads_own, swapped(grads_own, 0)])
    preactivation = dot(normed_pair, fc_half, ((1,), (0,))) + fc_add
    hidden = gelu_tanh(preactivation).astype(bf16)
    out_part = dot(hidden, out_half, ((1,), (0,)))
    layer_output = middle + (out_part[:tokens] + swapped(out_part[tokens:], 0)) + out_add
    layer_output = layer_output.astype(bf16)
    grad_hidden = dot(grads_pair, out_half, ((1,), (1,)))
    grad_pre = jax.vjp(gelu_tanh, preactivation)[1](grad_hidden)[0].astype(bf16)
    normed_part = dot(grad_pre, fc_half, ((1,), (1,)))
    grad_normed_two = normed_part[:tokens] + swapped(normed_part[tokens:], 0)
    grad_mid_part, gain_two_grad, shift_two_grad = jax.vjp(
        layer_norm, middle, gain_two, shift_two
    )[1](grad_normed_two)
    grad_middle = grads32 + grad_mid_part
    grad_branch = grad_middle.astype(bf16)

    grad_attended = dot(proj_heads, grad_branch, ((1,), (1,))).astype(bf16)
    query_low = [None] * seqs
    kv_parts = [None] * seqs
    for s in reversed(range(seqs)):
        go = grad_attended[:, s * piece : (s + 1) * piece]
        go = [go[e * group : (e + 1) * group] for e in range(shards)]
        go = [go[0]] + [shifted(go[e], e) for e in range(1, shards)]
        out, lse = saved[s]
        query_low[s], near, far = attend_back(
            shards, slots[s], infos[s], queries[s], out, lse, go, blocks[s]
        )
        kv_parts[s] = near.astype(f32) + swapped(far, 0).astype(f32)
    kv_low = [None] * seqs
    input_grads = [None] * seqs
    gain_one_grad = jnp.zeros((width,), f32)
    shift_one_grad = jnp.zeros((width,), f32)
    for s in reversed(range(seqs)):
        total = kv_parts[s][0]
        for i in range(1, cycle // 2):
            total = total + sent_up(kv_parts[s][i].astype(bf16), 2 * i, late[s]).astype(f32)
        kv_low[s] = total.astype(bf16)
        part = dot(query_low[s], q_weight, ((1,), (1,))) + dot(kv_low[s], kv_weight, ((1,), (1,)))
        gain_one_grad = gain_one_grad + jnp.sum(part * group_norms[s], axis=0)
        shift_one_grad = shift_one_grad + jnp.sum(part, axis=0)
        low = part.astype(bf16)
        grad_normed = part[:piece]
        for d in range(1, shards):
            grad_normed = grad_normed + shifted(low[d * piece : (d + 1) * piece], -d).astype(f32)
        own = slice(s * piece, (s + 1) * piece)
        pull = jax.vjp(lambda v: normalized(v) * gain_one, inputs32[own])[1]
        result = (grad_middle[own] + pull(grad_normed)[0]).astype(bf16)
        input_grads[s] = mirrored(result) if late[s] else result
    layer_output = [
        mirrored(layer_output[s * piece : (s + 1) * piece])
        if late[s]
        else layer_output[s * piece : (s + 1) * piece]
        for s in range(seqs)
    ]

    def pair_split(grad):
        parts = grad.astype(bf16).reshape(shards, 2, half_width, -1)
        mine = lax.dynamic_index_in_dim(parts, odd, 1, False)
        sent = lax.dynamic_index_in_dim(parts, 1 - odd, 1, False)
        return (mine.astype(f32) + swapped(sent, 0).astype(f32)).astype(bf16)

    flat = ((0,), (0,))
    out_grad = lax.psum_scatter(
        dot(hidden, grads_pair, flat).astype(bf16).reshape(shards, half_hidden, width),
        "shard",
        scatter_dimension=0,
        tiled=False,
    )
    out_grad = jnp.concatenate(pair_joined(summed_over_chips(out_grad, chip_bits[::-1]), odd))
    fc_grad = lax.psum_scatter(
        dot(normed_pair, grad_pre, flat).astype(bf16).reshape(shards, local_width, -1),
        "shard",
        scatter_dimension=0,
        tiled=False,
    )
    fc_halves = pair_joined(summed_over_chips(fc_grad, chip_bits), odd)
    fc_grad = jnp.concatenate(
        [
            fc_halves[h][:, z * half_hidden : (z + 1) * half_hidden]
            for z in range(shards)
            for h in range(2)
        ],
        axis=1,
    )
    in_order = rolled(attended.reshape(shards, group, tokens), (shards - shard_at) % shards)
    proj_grad = lax.psum_scatter(
        pair_split(dot(in_order.reshape(padded, tokens)[:width], grad_branch, ((1,), (0,)))),
        "shard",
        scatter_dimension=0,
        tiled=False,
    )
    proj_grad = jnp.concatenate(pair_joined(summed_over_chips(proj_grad, chip_bits), odd))

    def head_columns(low):
        grad = dot(normed_one[0], low[0], flat)
        for s in range(1, seqs):
            grad = grad + dot(normed_one[s], low[s], flat)
        grad = lax.all_to_all(pair_split(grad), "shard", 0, 0, tiled=True)
        halves = pair_joined(summed_over_chips(grad, chip_bits), odd)
        full = jnp.concatenate(halves, axis=1)
        return [
            jnp.concatenate(
                [full[z, :, at * group : (at + 1) * group] for z in range(shards)], axis=1
            )[:, :width]
            for at in range(full.shape[2] // group)
        ]

    qkv_grad = jnp.concatenate(head_columns(query_low) + head_columns(kv_low), axis=1)

    fc_add_part = jnp.sum(grad_pre.astype(f32), axis=0).reshape(shards, 1, half_hidden)
    fc_add_part = jnp.where(jnp.arange(2)[None, :, None] == odd, fc_add_part, 0.0)

    def all_heads(vector):
        return lax.dynamic_update_slice_in_dim(
            jnp.zeros((padded,), f32), vector, shard_at * group, 0
        )[:width]

    query_sum = sum(jnp.sum(low.astype(f32), axis=0) for low in query_low)
    value_sum = sum(jnp.sum(low[:, group:].astype(f32), axis=0) for low in kv_low)
    sums = reduce_small(
        jnp.concatenate(
            [
                v.reshape(shards, -1)
                for v in (
                    gain_one_grad,
                    shift_one_grad,
                    all_heads(query_sum),
                    all_heads(value_sum),
                    jnp.sum(grad_branch.astype(f32), axis=0),
                    gain_two_grad,
                    shift_two_grad,
                    jnp.sum(grads32, axis=0),
                    fc_add_part,
                )
            ],
            axis=1,
        )
    )
    parts = [sums[i * local_width : (i + 1) * local_width] for i in range(8)]
    return (
        jnp.stack(layer_output),
        jnp.stack(input_grads),
        parts[0],
        parts[1],
        qkv_grad,
        parts[2],
        parts[3],
        proj_grad,
        parts[4],
        parts[5],
        parts[6],
        fc_grad,
        sums[8 * local_width :],
        out_grad,
        parts[7],
    )


def solution(mesh):
    tokens = P(None, ("ctx", "shard"), None)
    vector = P("shard")
    matrix = P("shard", None)
    return jax.shard_map(
        body,
        mesh=mesh,
        in_specs=(
            tokens,
            vector,
            vector,
            matrix,
            vector,
            vector,
            matrix,
            vector,
            vector,
            vector,
            matrix,
            vector,
            matrix,
            vector,
            tokens,
        ),
        out_specs=(
            tokens,
            tokens,
            vector,
            vector,
            matrix,
            vector,
            vector,
            matrix,
            vector,
            vector,
            vector,
            matrix,
            vector,
            matrix,
            vector,
        ),
        check_vma=False,
    )
```

```python
import functools

import jax
import jax.numpy as jnp
from jax import lax
from jax.experimental import pallas as pl
from jax.experimental.pallas import tpu as pltpu
from jax.sharding import PartitionSpec as P

HEADS = 12
HEAD = 64
TILE = 512
EXP2_SCALE = 0.125 * 1.4426950408889634
f32 = jnp.float32
bf16 = jnp.bfloat16
FC_BIT = 1
OUT_BIT = 2
VMEM_LIMIT = 56 * 1024 * 1024


def normalized(values):
    centered = values - jnp.mean(values, axis=-1, keepdims=True)
    variance = jnp.mean(centered * centered, axis=-1, keepdims=True)
    return centered * lax.rsqrt(variance + 1e-05)


def layer_norm(values, gain, shift):
    return normalized(values) * gain + shift


def gelu_tanh(values):
    return jax.nn.gelu(values, approximate=True)


def swapped(block, bit):
    n = lax.axis_size("ctx")
    return lax.ppermute(block, "ctx", [(i, i ^ (1 << bit)) for i in range(n)])


def tree_pairs(order, held, bit, late, back):
    n = lax.axis_size("ctx")
    later = order[order.index(bit) + 1 :]
    reach = [0]
    for other in later:
        reach += [r ^ (1 << other) for r in reach]
    place = (lambda i: n - 1 - i) if late else (lambda i: i)
    pairs = []
    for i in range(n):
        target = i ^ (1 << bit)
        if any(place(i ^ held) <= place(target ^ r) for r in reach):
            pairs.append((target, i) if back else (i, target))
    return pairs


def spread(own, order, late):
    held = [(0, own)]
    for bit in order:
        held += [
            (apart ^ (1 << bit), lax.ppermute(block, "ctx", tree_pairs(order, apart, bit, late, False)))
            for apart, block in held
        ]
    return [block for _, block in held], [apart for apart, _ in held]


def returned(parts, aparts, order, late):
    for bit in order[::-1]:
        half = len(parts) // 2
        sums = []
        for i in range(half):
            pairs = tree_pairs(order, aparts[i], bit, late, True)
            received = lax.ppermute(parts[half + i], "ctx", pairs)
            sums.append((parts[i].astype(f32) + received.astype(f32)).astype(bf16))
        parts = sums
    return parts[0]


def mirrored(block):
    n = lax.axis_size("ctx")
    return lax.ppermute(block, "ctx", [(i, n - 1 - i) for i in range(n)])


def shifted(block, distance):
    n = lax.axis_size("shard")
    return lax.ppermute(block, "shard", [(i, (i + distance) % n) for i in range(n)])


def dot(a, b, contract):
    return lax.dot_general(a, b, ((contract[0], contract[1]), ((), ())), preferred_element_type=f32)


def rolled(block, start):
    return lax.dynamic_slice_in_dim(jnp.concatenate([block, block]), start, block.shape[0], 0)


def reduce_small(parts):
    n = lax.axis_size("shard")
    me = lax.axis_index("shard")
    total = lax.dynamic_index_in_dim(parts, me, 0, False)
    for d in range(1, n):
        total = total + shifted(lax.dynamic_index_in_dim(parts, (me + d) % n, 0, False), d)
    for bit in range(lax.axis_size("ctx").bit_length() - 1):
        total = total + swapped(total, bit)
    return total


def summed_over_chips(part, bits):
    for bit in bits:
        low = part.astype(bf16)
        part = low.astype(f32) + swapped(low, bit).astype(f32)
    return part


def joined(half, bit, side):
    other = swapped(half, bit)
    return jnp.where(side, other, half), jnp.where(side, half, other)


def pair_joined(half, odd):
    return joined(half, 0, odd)


def load_blocks(refs, held, sems):
    copies = [pltpu.make_async_copy(ref, held.at[i], sems.at[i]) for i, ref in enumerate(refs)]
    for copy in copies:
        copy.start()
    return copies


def forward_kernel(heads, shards, count, slots, info, q_ref, *refs):
    kv_refs = refs[:count]
    att_ref, out_ref, lse_ref, held, sems, m_ref, l_ref, acc_ref = refs[count:]
    rows, width = q_ref.shape
    piece = rows // shards
    tile = min(TILE, rows)
    per = rows // tile
    copies = load_blocks(kv_refs, held, sems)
    key_places = lax.broadcasted_iota(jnp.int32, (rows, 1), 0)
    query_places = lax.broadcasted_iota(jnp.int32, (1, rows), 1)
    for copy in copies:
        copy.wait()
    for part in range(per):
        span = slice(part * tile, (part + 1) * tile)

        def step(slot, key_part, masked, start):
            keys_at = slice(key_part * tile, (key_part + 1) * tile)
            allowed = key_places[keys_at] <= query_places[:, span] if masked else None
            for h in range(heads):
                lanes = slice(h * HEAD, (h + 1) * HEAD)
                lanes_v = slice(width + h * HEAD, width + (h + 1) * HEAD)
                q = q_ref[span, lanes]
                k = held[slot, keys_at, lanes]
                v = held[slot, keys_at, lanes_v]
                s = dot(k, q, ((1,), (1,))) * EXP2_SCALE
                if masked:
                    s = jnp.where(allowed, s, -1e30)
                m = jnp.max(s, axis=0, keepdims=True)
                if start:
                    p = jnp.exp2(s - m)
                    l_ref[h] = jnp.sum(p, axis=0, keepdims=True)
                    acc_ref[h] = dot(v, p.astype(bf16), ((0,), (0,)))
                else:
                    old = m_ref[h]
                    m = jnp.maximum(old, m)
                    p = jnp.exp2(s - m)
                    factor = jnp.exp2(old - m)
                    l_ref[h] = l_ref[h] * factor + jnp.sum(p, axis=0, keepdims=True)
                    acc_ref[h] = acc_ref[h] * factor + dot(v, p.astype(bf16), ((0,), (0,)))
                m_ref[h] = m

        for key_part in range(per):
            step(slots[info[0]], key_part, True, key_part == 0)

        @pl.loop(0, info[0])
        def _(j):
            for key_part in range(per):
                step(slots[j], key_part, False, False)

        for h in range(heads):
            total = l_ref[h]
            done = acc_ref[h] / total
            out_ref[h * HEAD : (h + 1) * HEAD, span] = done
            lse_ref[h, :, span] = m_ref[h] + jnp.log2(total)
            low = done.astype(bf16)
            for z in range(tile // piece):
                apart = lax.rem(info[1] + shards - part * (tile // piece) - z, shards)
                att_ref[apart, h * HEAD : (h + 1) * HEAD, :] = low[:, z * piece : (z + 1) * piece]


def backward_kernel(heads, shards, count, slots, info, q_ref, out_ref, lse_ref, *refs):
    go_refs = refs[:shards]
    kv_refs = refs[shards : shards + count]
    dq_ref = refs[shards + count]
    dkv_refs = refs[shards + count + 1 : shards + 2 * count + 1]
    go_held, held, sums, sems, end_sems, acc_ref = refs[shards + 2 * count + 1 :]
    rows, width = q_ref.shape
    piece = rows // shards
    tile = min(TILE, rows)
    per = rows // tile
    copies = load_blocks(kv_refs, held, sems)
    key_places = lax.broadcasted_iota(jnp.int32, (rows, 1), 0)
    query_places = lax.broadcasted_iota(jnp.int32, (1, rows), 1)

    for e, ref in enumerate(go_refs):
        go_held[lax.rem(info[1] + shards - e, shards)] = ref[...]

    @pl.loop(info[0] + 1, count)
    def _(j):
        sums[slots[j]] = jnp.zeros((rows, 2 * width), bf16)

    for copy in copies:
        copy.wait()
    for part in range(per):
        span = slice(part * tile, (part + 1) * tile)
        pieces = range(part * (tile // piece), (part + 1) * (tile // piece))
        go_all = jnp.concatenate([go_held[z] for z in pieces], axis=1)
        deltas = []
        for h in range(heads):
            lanes = slice(h * HEAD, (h + 1) * HEAD)
            deltas.append(
                jnp.sum(go_all[lanes].astype(f32) * out_ref[lanes, span], axis=0, keepdims=True)
            )

        def step(slot, key_part, masked, start):
            keys_at = slice(key_part * tile, (key_part + 1) * tile)
            allowed = key_places[keys_at] <= query_places[:, span] if masked else None
            for h in range(heads):
                lanes = slice(h * HEAD, (h + 1) * HEAD)
                lanes_v = slice(width + h * HEAD, width + (h + 1) * HEAD)
                q = q_ref[span, lanes]
                go = go_all[lanes]
                k = held[slot, keys_at, lanes]
                v = held[slot, keys_at, lanes_v]
                p = jnp.exp2(dot(k, q, ((1,), (1,))) * EXP2_SCALE - lse_ref[h, :, span])
                if masked:
                    p = jnp.where(allowed, p, 0.0)
                pulled = dot(v, go, ((1,), (0,)))
                slopes = (p * (pulled - deltas[h])).astype(bf16)
                dv = dot(p.astype(bf16), go, ((1,), (1,)))
                dk = dot(slopes, q, ((1,), (0,))) * 0.125
                if part:
                    dk = dk + sums[slot, keys_at, lanes].astype(f32)
                    dv = dv + sums[slot, keys_at, lanes_v].astype(f32)
                sums[slot, keys_at, lanes] = dk.astype(bf16)
                sums[slot, keys_at, lanes_v] = dv.astype(bf16)
                dq = dot(k, slopes, ((0,), (0,)))
                if start:
                    acc_ref[h] = dq
                else:
                    acc_ref[h] += dq

        for key_part in range(per):
            step(slots[info[0]], key_part, True, key_part == 0)

        @pl.loop(0, info[0])
        def _(j):
            for key_part in range(per):
                step(slots[j], key_part, False, False)

        for h in range(heads):
            dq_ref[span, h * HEAD : (h + 1) * HEAD] = (acc_ref[h] * 0.125).T.astype(bf16)
    copies = [
        pltpu.make_async_copy(sums.at[i], ref, end_sems.at[i]) for i, ref in enumerate(dkv_refs)
    ]
    for copy in copies:
        copy.start()
    for copy in copies:
        copy.wait()


SMEM = pl.BlockSpec(memory_space=pltpu.SMEM)
VMEM = pl.BlockSpec(memory_space=pltpu.VMEM)
ANY = pl.BlockSpec(memory_space=pl.ANY)


def attend(shards, slots, info, queries, blocks):
    rows, width = queries.shape
    heads = width // HEAD
    count = len(blocks)
    tile = min(TILE, rows)
    scores = heads * rows * rows * (count + 1) // 2
    return pl.pallas_call(
        functools.partial(forward_kernel, heads, shards, count),
        out_shape=(
            jax.ShapeDtypeStruct((shards, width, rows // shards), bf16),
            jax.ShapeDtypeStruct((width, rows), f32),
            jax.ShapeDtypeStruct((heads, 1, rows), f32),
        ),
        in_specs=[SMEM, SMEM, VMEM] + [ANY] * count,
        out_specs=(VMEM, VMEM, VMEM),
        scratch_shapes=[
            pltpu.VMEM((count, rows, 2 * width), bf16),
            pltpu.SemaphoreType.DMA((count,)),
            pltpu.VMEM((heads, 1, tile), f32),
            pltpu.VMEM((heads, 1, tile), f32),
            pltpu.VMEM((heads, HEAD, tile), f32),
        ],
        compiler_params=pltpu.CompilerParams(vmem_limit_bytes=VMEM_LIMIT),
        cost_estimate=pl.CostEstimate(
            flops=scores * 16 * HEAD,
            bytes_accessed=4 * rows * width * (count + 2),
            transcendentals=scores,
        ),
        name="attention_forward",
    )(slots, info, queries, *blocks)


def attend_back(shards, slots, info, queries, out, lse, grads, blocks):
    rows, width = queries.shape
    heads = width // HEAD
    count = len(blocks)
    tile = min(TILE, rows)
    scores = heads * rows * rows * (count + 1) // 2
    return pl.pallas_call(
        functools.partial(backward_kernel, heads, shards, count),
        out_shape=[jax.ShapeDtypeStruct((rows, width), bf16)]
        + [jax.ShapeDtypeStruct((rows, 2 * width), bf16)] * count,
        in_specs=[SMEM, SMEM, VMEM, VMEM, VMEM] + [VMEM] * shards + [ANY] * count,
        out_specs=[VMEM] + [ANY] * count,
        scratch_shapes=[
            pltpu.VMEM((shards, width, rows // shards), bf16),
            pltpu.VMEM((count, rows, 2 * width), bf16),
            pltpu.VMEM((count, rows, 2 * width), bf16),
            pltpu.SemaphoreType.DMA((count,)),
            pltpu.SemaphoreType.DMA((count,)),
            pltpu.VMEM((heads, HEAD, tile), f32),
        ],
        compiler_params=pltpu.CompilerParams(vmem_limit_bytes=VMEM_LIMIT),
        cost_estimate=pl.CostEstimate(
            flops=scores * 40 * HEAD,
            bytes_accessed=8 * rows * width * (count + 2),
            transcendentals=scores,
        ),
        name="attention_backward",
    )(slots, info, queries, out, lse, *grads, *blocks)


def body(
    layer_input,
    attn_gain,
    attn_shift,
    qkv_weight,
    query_bias,
    value_bias,
    proj_weight,
    proj_bias,
    mlp_gain,
    mlp_shift,
    fc_weight,
    fc_bias,
    out_weight,
    out_bias,
    grad_output,
):
    seqs, piece, width = layer_input.shape
    cycle = lax.axis_size("ctx")
    shards = lax.axis_size("shard")
    here = lax.axis_index("ctx")
    shard_at = lax.axis_index("shard")
    odd = here % 2
    chip_bits = list(range(1, cycle.bit_length() - 1))
    rows = shards * piece
    local_width = qkv_weight.shape[0]
    local_hidden = out_weight.shape[0]
    half_width = local_width // 2
    half_hidden = local_hidden // 2
    quarter = half_hidden // 2
    group = -(-HEADS // shards) * HEAD
    padded = group * shards
    late = [seq >= (seqs + 1) // 2 for seq in range(seqs)]
    tokens = seqs * piece

    def by_heads(weight):
        parts = []
        for third in range(3):
            part = weight[:, third * width : (third + 1) * width]
            parts.append(jnp.pad(part, ((0, 0), (0, padded - width))))
        return jnp.stack(
            [
                jnp.concatenate([part[:, z * group : (z + 1) * group] for part in parts], axis=1)
                for z in range(shards)
            ]
        )

    weight_half = lax.dynamic_slice_in_dim(qkv_weight, odd * half_width, half_width, 0)
    moved = lax.all_to_all(by_heads(weight_half), "shard", 0, 0, tiled=True)
    qkv_own = jnp.stack(pair_joined(moved, odd), axis=1).reshape(width, 3 * group)
    q_weight = qkv_own[:, :group]
    kv_weight = qkv_own[:, group:]

    packed = jnp.concatenate(
        [
            attn_gain,
            attn_shift,
            query_bias,
            value_bias,
            proj_bias,
            mlp_gain,
            mlp_shift,
            out_bias,
            fc_bias,
        ]
    )
    packed = jnp.pad(packed, (0, 16 * width - packed.size)).reshape(16, width)
    inputs = [mirrored(layer_input[s]) if late[s] else layer_input[s] for s in range(seqs)]
    gathered = [
        lax.all_gather(
            inputs[s] if s else jnp.concatenate([inputs[s], packed]), "shard", axis=0
        )
        for s in range(seqs)
    ]
    small = gathered[0][:, piece:].reshape(shards, -1).astype(f32)
    gathered[0] = gathered[0][:, :piece]
    vectors = [small[:, i * local_width : (i + 1) * local_width].reshape(-1) for i in range(8)]
    gain_one, shift_one, query_add, value_add, proj_add, gain_two, shift_two, out_add = vectors
    fc_bias_all = small[:, 8 * local_width : 8 * local_width + local_hidden]
    fc_add = lax.dynamic_index_in_dim(
        fc_bias_all.reshape(shards, 2, half_hidden), odd, 1, False
    ).reshape(-1)

    def own_heads(vector):
        return lax.dynamic_slice_in_dim(
            jnp.pad(vector, (0, padded - width)), shard_at * group, group, 0
        )

    kv_add = jnp.concatenate([jnp.zeros((group,), f32), own_heads(value_add)])
    query_add = own_heads(query_add)

    proj_half = lax.all_gather(
        lax.dynamic_slice_in_dim(proj_weight, odd * half_width, half_width, 0), "shard", axis=0
    )
    proj_full = jnp.concatenate(
        [half.reshape(shards, 1, half_width, width) for half in pair_joined(proj_half, odd)], axis=1
    ).reshape(width, width)
    fc_side = (here >> FC_BIT) % 2
    out_side = (here >> OUT_BIT) % 2
    fc_quarter = lax.all_gather(
        jnp.concatenate(
            [
                lax.dynamic_slice_in_dim(
                    fc_weight,
                    (fc_side * (shards // 2) + z) * local_hidden + odd * half_hidden,
                    half_hidden,
                    1,
                )
                for z in range(shards // 2)
            ],
            axis=1,
        ),
        "shard",
        axis=0,
        tiled=True,
    )
    fc_half = jnp.concatenate(joined(fc_quarter, FC_BIT, fc_side), axis=1)
    out_quarter = lax.all_gather(
        lax.dynamic_slice_in_dim(
            out_weight, odd * half_hidden + out_side * quarter, quarter, 0
        ),
        "shard",
        axis=0,
    )
    out_half = jnp.stack(joined(out_quarter, OUT_BIT, out_side), axis=1).reshape(-1, width)
    proj_heads = rolled(
        jnp.pad(proj_full, ((0, padded - width), (0, 0))).reshape(shards, group, width), shard_at
    ).reshape(padded, width)

    block_index = [cycle - 1 - here if late[s] else here for s in range(seqs)]
    orders = [chip_bits + [0], chip_bits[::-1] + [0]]
    group_norms, normed_one, queries, blocks, aparts, slots, infos = [], [], [], [], [], [], []
    for s in range(seqs):
        norm = normalized(gathered[s].reshape(rows, width).astype(f32))
        normed = (norm * gain_one + shift_one).astype(bf16)
        group_norms.append(norm)
        normed_one.append(normed)
        own = (dot(normed, kv_weight, ((1,), (0,))) + kv_add).astype(bf16)
        held, apart = spread(own, orders[s % 2], late[s])
        blocks.append(held)
        aparts.append(apart)
        queries.append((dot(normed, q_weight, ((1,), (0,))) + query_add).astype(bf16))
        owners = jnp.arange(cycle)
        distance = (cycle - 1 - owners if late[s] else owners) ^ here
        places = jnp.array([apart.index(i) for i in range(cycle)], jnp.int32)
        slots.append(places[distance])
        infos.append(jnp.stack([block_index[s], shard_at]).astype(jnp.int32))
    saved = []
    attended_parts = []
    for s in range(seqs):
        att, out, lse = attend(shards, slots[s], infos[s], queries[s], blocks[s])
        saved.append((out, lse))
        attended_parts.append(
            jnp.concatenate([att[0]] + [shifted(att[d], -d) for d in range(1, shards)])
        )
    attended = jnp.concatenate(attended_parts, axis=1)

    inputs32 = jnp.concatenate(inputs).astype(f32)
    grads_own = jnp.concatenate(
        [mirrored(grad_output[s]) if late[s] else grad_output[s] for s in range(seqs)]
    )
    grads32 = grads_own.astype(f32)
    middle = inputs32 + dot(attended, proj_heads, ((0,), (0,))) + proj_add
    normed_two = layer_norm(middle, gain_two, shift_two).astype(bf16)

    normed_pair = jnp.concatenate([normed_two, swapped(normed_two, 0)])
    grads_pair = jnp.concatenate([grads_own, swapped(grads_own, 0)])
    preactivation = dot(normed_pair, fc_half, ((1,), (0,))) + fc_add
    hidden = gelu_tanh(preactivation).astype(bf16)
    out_part = dot(hidden, out_half, ((1,), (0,)))
    layer_output = middle + (out_part[:tokens] + swapped(out_part[tokens:], 0)) + out_add
    layer_output = layer_output.astype(bf16)
    grad_hidden = dot(grads_pair, out_half, ((1,), (1,)))
    grad_pre = jax.vjp(gelu_tanh, preactivation)[1](grad_hidden)[0].astype(bf16)
    normed_part = dot(grad_pre, fc_half, ((1,), (1,)))
    grad_normed_two = normed_part[:tokens] + swapped(normed_part[tokens:], 0)
    grad_mid_part, gain_two_grad, shift_two_grad = jax.vjp(
        layer_norm, middle, gain_two, shift_two
    )[1](grad_normed_two)
    grad_middle = grads32 + grad_mid_part
    grad_branch = grad_middle.astype(bf16)

    grad_attended = dot(proj_heads, grad_branch, ((1,), (1,))).astype(bf16)
    query_low = [None] * seqs
    kv_parts = [None] * seqs
    for s in reversed(range(seqs)):
        go = grad_attended[:, s * piece : (s + 1) * piece]
        go = [go[e * group : (e + 1) * group] for e in range(shards)]
        go = [go[0]] + [shifted(go[e], e) for e in range(1, shards)]
        out, lse = saved[s]
        query_low[s], *kv_parts[s] = attend_back(
            shards, slots[s], infos[s], queries[s], out, lse, go, blocks[s]
        )
    kv_low = [None] * seqs
    input_grads = [None] * seqs
    gain_one_grad = jnp.zeros((width,), f32)
    shift_one_grad = jnp.zeros((width,), f32)
    for s in reversed(range(seqs)):
        kv_low[s] = returned(kv_parts[s], aparts[s], orders[s % 2], late[s])
        part = dot(query_low[s], q_weight, ((1,), (1,))) + dot(kv_low[s], kv_weight, ((1,), (1,)))
        gain_one_grad = gain_one_grad + jnp.sum(part * group_norms[s], axis=0)
        shift_one_grad = shift_one_grad + jnp.sum(part, axis=0)
        grad_normed = lax.psum_scatter(
            part.astype(bf16).reshape(shards, piece, width), "shard", scatter_dimension=0, tiled=False
        ).astype(f32)
        own = slice(s * piece, (s + 1) * piece)
        pull = jax.vjp(lambda v: normalized(v) * gain_one, inputs32[own])[1]
        result = (grad_middle[own] + pull(grad_normed)[0]).astype(bf16)
        input_grads[s] = mirrored(result) if late[s] else result
    layer_output = [
        mirrored(layer_output[s * piece : (s + 1) * piece])
        if late[s]
        else layer_output[s * piece : (s + 1) * piece]
        for s in range(seqs)
    ]

    def pair_split(grad):
        parts = grad.astype(bf16).reshape(shards, 2, half_width, -1)
        mine = lax.dynamic_index_in_dim(parts, odd, 1, False)
        sent = lax.dynamic_index_in_dim(parts, 1 - odd, 1, False)
        return (mine.astype(f32) + swapped(sent, 0).astype(f32)).astype(bf16)

    flat = ((0,), (0,))
    def split_sum(first, second, bit, side):
        sent = jnp.where(side, first, second)
        mine = jnp.where(side, second, first)
        return (mine.astype(f32) + swapped(sent, bit).astype(f32)).astype(bf16)

    out_grad = dot(hidden, grads_pair, flat).astype(bf16).reshape(shards, 2, quarter, width)
    out_grad = lax.psum_scatter(
        split_sum(out_grad[:, 0], out_grad[:, 1], OUT_BIT, out_side),
        "shard",
        scatter_dimension=0,
        tiled=False,
    )
    out_grad = summed_over_chips(out_grad, [bit for bit in chip_bits if bit != OUT_BIT])
    out_grad = jnp.concatenate(joined(out_grad, OUT_BIT, out_side))
    out_grad = jnp.concatenate(pair_joined(out_grad, odd))
    fc_grad = dot(normed_pair, grad_pre, flat).astype(bf16).reshape(shards, local_width, -1)
    middle_column = fc_grad.shape[2] // 2
    fc_grad = lax.psum_scatter(
        split_sum(fc_grad[..., :middle_column], fc_grad[..., middle_column:], FC_BIT, fc_side),
        "shard",
        scatter_dimension=0,
        tiled=False,
    )
    fc_grad = summed_over_chips(fc_grad, [bit for bit in chip_bits if bit != FC_BIT])
    fc_grad = jnp.concatenate(joined(fc_grad, FC_BIT, fc_side), axis=1)
    fc_halves = pair_joined(fc_grad, odd)
    fc_grad = jnp.concatenate(
        [
            fc_halves[h][:, z * half_hidden : (z + 1) * half_hidden]
            for z in range(shards)
            for h in range(2)
        ],
        axis=1,
    )
    in_order = rolled(attended.reshape(shards, group, tokens), (shards - shard_at) % shards)
    proj_grad = lax.psum_scatter(
        pair_split(dot(in_order.reshape(padded, tokens)[:width], grad_branch, ((1,), (0,)))),
        "shard",
        scatter_dimension=0,
        tiled=False,
    )
    proj_grad = jnp.concatenate(pair_joined(summed_over_chips(proj_grad, chip_bits), odd))

    def head_columns(low):
        grad = dot(normed_one[0], low[0], flat)
        for s in range(1, seqs):
            grad = grad + dot(normed_one[s], low[s], flat)
        grad = lax.all_to_all(pair_split(grad), "shard", 0, 0, tiled=True)
        halves = pair_joined(summed_over_chips(grad, chip_bits), odd)
        full = jnp.concatenate(halves, axis=1)
        return [
            jnp.concatenate(
                [full[z, :, at * group : (at + 1) * group] for z in range(shards)], axis=1
            )[:, :width]
            for at in range(full.shape[2] // group)
        ]

    qkv_grad = jnp.concatenate(head_columns(query_low) + head_columns(kv_low), axis=1)

    fc_add_part = jnp.sum(grad_pre.astype(f32), axis=0).reshape(shards, 1, half_hidden)
    fc_add_part = jnp.where(jnp.arange(2)[None, :, None] == odd, fc_add_part, 0.0)

    def all_heads(vector):
        return lax.dynamic_update_slice_in_dim(
            jnp.zeros((padded,), f32), vector, shard_at * group, 0
        )[:width]

    query_sum = sum(jnp.sum(low.astype(f32), axis=0) for low in query_low)
    value_sum = sum(jnp.sum(low[:, group:].astype(f32), axis=0) for low in kv_low)
    sums = reduce_small(
        jnp.concatenate(
            [
                v.reshape(shards, -1)
                for v in (
                    gain_one_grad,
                    shift_one_grad,
                    all_heads(query_sum),
                    all_heads(value_sum),
                    jnp.sum(grad_branch.astype(f32), axis=0),
                    gain_two_grad,
                    shift_two_grad,
                    jnp.sum(grads32, axis=0),
                    fc_add_part,
                )
            ],
            axis=1,
        )
    )
    parts = [sums[i * local_width : (i + 1) * local_width] for i in range(8)]
    return (
        jnp.stack(layer_output),
        jnp.stack(input_grads),
        parts[0],
        parts[1],
        qkv_grad,
        parts[2],
        parts[3],
        proj_grad,
        parts[4],
        parts[5],
        parts[6],
        fc_grad,
        sums[8 * local_width :],
        out_grad,
        parts[7],
    )


def solution(mesh):
    tokens = P(None, ("ctx", "shard"), None)
    vector = P("shard")
    matrix = P("shard", None)
    return jax.shard_map(
        body,
        mesh=mesh,
        in_specs=(
            tokens,
            vector,
            vector,
            matrix,
            vector,
            vector,
            matrix,
            vector,
            vector,
            vector,
            matrix,
            vector,
            matrix,
            vector,
            tokens,
        ),
        out_specs=(
            tokens,
            tokens,
            vector,
            vector,
            matrix,
            vector,
            vector,
            matrix,
            vector,
            vector,
            vector,
            matrix,
            vector,
            matrix,
            vector,
        ),
        check_vma=False,
    )
```

```python
import functools

import jax
import jax.numpy as jnp
from jax import lax
from jax.experimental import pallas as pl
from jax.experimental.pallas import tpu as pltpu
from jax.sharding import PartitionSpec as P

HEADS = 12
HEAD = 64
TILE = 512
EXP2_SCALE = 0.125 * 1.4426950408889634
f32 = jnp.float32
bf16 = jnp.bfloat16
FC_BIT = 1
OUT_BIT = 2
VMEM_LIMIT = 56 * 1024 * 1024


def normalized(values):
    centered = values - jnp.mean(values, axis=-1, keepdims=True)
    variance = jnp.mean(centered * centered, axis=-1, keepdims=True)
    return centered * lax.rsqrt(variance + 1e-05)


def layer_norm(values, gain, shift):
    return normalized(values) * gain + shift


def gelu_tanh(values):
    return jax.nn.gelu(values, approximate=True)


def swapped(block, bit):
    n = lax.axis_size("ctx")
    return lax.ppermute(block, "ctx", [(i, i ^ (1 << bit)) for i in range(n)])


def tree_pairs(aparts, bit, later, late, back):
    n = lax.axis_size("ctx")
    reach = [0]
    for other in later:
        reach += [r ^ (1 << other) for r in reach]
    place = (lambda i: n - 1 - i) if late else (lambda i: i)
    pairs = []
    for i in range(n):
        target = i ^ (1 << bit)
        if any(place(i ^ apart) <= place(target ^ r) for r in reach for apart in aparts):
            pairs.append((target, i) if back else (i, target))
    return pairs


def spread(own, order, late):
    held, aparts = own[None], [0]
    for bit in order[:-2]:
        pairs = tree_pairs(aparts, bit, order[order.index(bit) + 1 :], late, False)
        held = jnp.concatenate([held, lax.ppermute(held, "ctx", pairs)])
        aparts = aparts + [apart ^ (1 << bit) for apart in aparts]
    bit = order[-2]
    received = lax.ppermute(held, "ctx", tree_pairs(aparts, bit, order[-1:], late, False))
    aparts = aparts + [apart ^ (1 << bit) for apart in aparts]
    blocks = [held, received, swapped(held, 0), swapped(received, 0)]
    return blocks, aparts + [apart ^ 1 for apart in aparts]


def added(first, second):
    return (first.astype(f32) + second.astype(f32)).astype(bf16)


def returned(near, middle, far, aparts, order, late):
    received = swapped(far, 0)
    count = near.shape[0]
    middle = added(middle, received[count:])
    pairs = tree_pairs(aparts[:count], order[-2], order[-1:], late, True)
    near = added(added(near, received[:count]), lax.ppermute(middle, "ctx", pairs))
    for bit in order[:-2][::-1]:
        count = near.shape[0] // 2
        pairs = tree_pairs(aparts[:count], bit, order[order.index(bit) + 1 :], late, True)
        near = added(near[:count], lax.ppermute(near[count:], "ctx", pairs))
    return near[0]


def after(value, *others):
    return lax.optimization_barrier((value,) + others)[0]


def mirrored(block):
    n = lax.axis_size("ctx")
    return lax.ppermute(block, "ctx", [(i, n - 1 - i) for i in range(n)])


def shifted(block, distance):
    n = lax.axis_size("shard")
    return lax.ppermute(block, "shard", [(i, (i + distance) % n) for i in range(n)])


def dot(a, b, contract):
    return lax.dot_general(a, b, ((contract[0], contract[1]), ((), ())), preferred_element_type=f32)


def reduce_small(parts):
    n = lax.axis_size("shard")
    me = lax.axis_index("shard")
    total = lax.dynamic_index_in_dim(parts, me, 0, False)
    for d in range(1, n):
        total = total + shifted(lax.dynamic_index_in_dim(parts, (me + d) & (n - 1), 0, False), d)
    for bit in range(lax.axis_size("ctx").bit_length() - 1):
        total = total + swapped(total, bit)
    return total


def summed_over_chips(part, bits):
    for bit in bits:
        low = part.astype(bf16)
        part = low.astype(f32) + swapped(low, bit).astype(f32)
    return part


def joined(half, bit, side):
    other = swapped(half, bit)
    return jnp.where(side, other, half), jnp.where(side, half, other)


def pair_joined(half, odd):
    return joined(half, 0, odd)


def load_blocks(refs, held, sems):
    each = refs[0].shape[0]
    copies = [
        pltpu.make_async_copy(ref, held.at[pl.ds(i * each, each)], sems.at[i])
        for i, ref in enumerate(refs)
    ]
    for copy in copies:
        copy.start()
    return copies


def forward_kernel(heads, shards, slots, info, q_ref, *refs):
    kv_refs = refs[:4]
    att_ref, out_ref, lse_ref, held, sems, m_ref, l_ref, acc_ref = refs[4:]
    rows, width = q_ref.shape
    piece = rows // shards
    tile = min(TILE, rows)
    per = rows // tile
    copies = load_blocks(kv_refs, held, sems)
    key_places = lax.broadcasted_iota(jnp.int32, (rows, 1), 0)
    query_places = lax.broadcasted_iota(jnp.int32, (1, rows), 1)
    for copy in copies:
        copy.wait()
    for part in range(per):
        span = slice(part * tile, (part + 1) * tile)

        def step(slot, key_part, masked, start):
            keys_at = slice(key_part * tile, (key_part + 1) * tile)
            allowed = key_places[keys_at] <= query_places[:, span] if masked else None
            for h in range(heads):
                lanes = slice(h * HEAD, (h + 1) * HEAD)
                lanes_v = slice(width + h * HEAD, width + (h + 1) * HEAD)
                q = q_ref[span, lanes]
                k = held[slot, keys_at, lanes]
                v = held[slot, keys_at, lanes_v]
                s = dot(k, q, ((1,), (1,))) * EXP2_SCALE
                if masked:
                    s = jnp.where(allowed, s, -1e30)
                m = jnp.max(s, axis=0, keepdims=True)
                if start:
                    p = jnp.exp2(s - m)
                    l_ref[h] = jnp.sum(p, axis=0, keepdims=True)
                    acc_ref[h] = dot(v, p.astype(bf16), ((0,), (0,)))
                else:
                    old = m_ref[h]
                    m = jnp.maximum(old, m)
                    p = jnp.exp2(s - m)
                    factor = jnp.exp2(old - m)
                    l_ref[h] = l_ref[h] * factor + jnp.sum(p, axis=0, keepdims=True)
                    acc_ref[h] = acc_ref[h] * factor + dot(v, p.astype(bf16), ((0,), (0,)))
                m_ref[h] = m

        for key_part in range(per):
            step(slots[info[0]], key_part, True, key_part == 0)

        @pl.loop(0, info[0])
        def _(j):
            for key_part in range(per):
                step(slots[j], key_part, False, False)

        for h in range(heads):
            total = l_ref[h]
            done = acc_ref[h] / total
            out_ref[h * HEAD : (h + 1) * HEAD, span] = done
            lse_ref[h, :, span] = m_ref[h] + jnp.log2(total)
            low = done.astype(bf16)
            for z in range(tile // piece):
                att_ref[part * (tile // piece) + z, h * HEAD : (h + 1) * HEAD, :] = low[
                    :, z * piece : (z + 1) * piece
                ]


def backward_kernel(heads, shards, seq, slots, info, q_ref, out_ref, lse_ref, go_ref, *refs):
    kv_refs = refs[:4]
    dq_ref, near_ref, middle_ref, far_ref, held, sums, sems, end_sems, acc_ref = refs[4:]
    count = held.shape[0]
    rows, width = q_ref.shape
    piece = rows // shards
    tile = min(TILE, rows)
    per = rows // tile
    copies = load_blocks(kv_refs, held, sems)
    key_places = lax.broadcasted_iota(jnp.int32, (rows, 1), 0)
    query_places = lax.broadcasted_iota(jnp.int32, (1, rows), 1)

    @pl.loop(info[0] + 1, count)
    def _(j):
        sums[slots[j]] = jnp.zeros((rows, 2 * width), bf16)

    for copy in copies:
        copy.wait()
    for part in range(per):
        span = slice(part * tile, (part + 1) * tile)
        pieces = range(part * (tile // piece), (part + 1) * (tile // piece))
        go_all = jnp.concatenate(
            [go_ref[z, :, seq * piece : (seq + 1) * piece] for z in pieces], axis=1
        )
        deltas = []
        for h in range(heads):
            lanes = slice(h * HEAD, (h + 1) * HEAD)
            deltas.append(
                jnp.sum(go_all[lanes].astype(f32) * out_ref[lanes, span], axis=0, keepdims=True)
            )

        def step(slot, key_part, masked, start):
            keys_at = slice(key_part * tile, (key_part + 1) * tile)
            allowed = key_places[keys_at] <= query_places[:, span] if masked else None
            for h in range(heads):
                lanes = slice(h * HEAD, (h + 1) * HEAD)
                lanes_v = slice(width + h * HEAD, width + (h + 1) * HEAD)
                q = q_ref[span, lanes]
                go = go_all[lanes]
                k = held[slot, keys_at, lanes]
                v = held[slot, keys_at, lanes_v]
                p = jnp.exp2(dot(k, q, ((1,), (1,))) * EXP2_SCALE - lse_ref[h, :, span])
                if masked:
                    p = jnp.where(allowed, p, 0.0)
                pulled = dot(v, go, ((1,), (0,)))
                slopes = (p * (pulled - deltas[h])).astype(bf16)
                dv = dot(p.astype(bf16), go, ((1,), (1,)))
                dk = dot(slopes, q, ((1,), (0,))) * 0.125
                if part:
                    dk = dk + sums[slot, keys_at, lanes].astype(f32)
                    dv = dv + sums[slot, keys_at, lanes_v].astype(f32)
                sums[slot, keys_at, lanes] = dk.astype(bf16)
                sums[slot, keys_at, lanes_v] = dv.astype(bf16)
                dq = dot(k, slopes, ((0,), (0,)))
                if start:
                    acc_ref[h] = dq
                else:
                    acc_ref[h] += dq

        for key_part in range(per):
            step(slots[info[0]], key_part, True, key_part == 0)

        @pl.loop(0, info[0])
        def _(j):
            for key_part in range(per):
                step(slots[j], key_part, False, False)

        for h in range(heads):
            dq_ref[span, h * HEAD : (h + 1) * HEAD] = (acc_ref[h] * 0.125).T.astype(bf16)
    copies = []
    base = 0
    for i, ref in enumerate((near_ref, middle_ref, far_ref)):
        copies.append(
            pltpu.make_async_copy(sums.at[pl.ds(base, ref.shape[0])], ref, end_sems.at[i])
        )
        base += ref.shape[0]
    for copy in copies:
        copy.start()
    for copy in copies:
        copy.wait()


SMEM = pl.BlockSpec(memory_space=pltpu.SMEM)
VMEM = pl.BlockSpec(memory_space=pltpu.VMEM)
ANY = pl.BlockSpec(memory_space=pl.ANY)


def attend(shards, slots, info, queries, blocks):
    rows, width = queries.shape
    heads = width // HEAD
    count = 4 * blocks[0].shape[0]
    tile = min(TILE, rows)
    scores = heads * rows * rows * (count + 1) // 2
    return pl.pallas_call(
        functools.partial(forward_kernel, heads, shards),
        out_shape=(
            jax.ShapeDtypeStruct((shards, width, rows // shards), bf16),
            jax.ShapeDtypeStruct((width, rows), f32),
            jax.ShapeDtypeStruct((heads, 1, rows), f32),
        ),
        in_specs=[SMEM, SMEM, VMEM] + [ANY] * 4,
        out_specs=(VMEM, VMEM, VMEM),
        scratch_shapes=[
            pltpu.VMEM((count, rows, 2 * width), bf16),
            pltpu.SemaphoreType.DMA((4,)),
            pltpu.VMEM((heads, 1, tile), f32),
            pltpu.VMEM((heads, 1, tile), f32),
            pltpu.VMEM((heads, HEAD, tile), f32),
        ],
        compiler_params=pltpu.CompilerParams(vmem_limit_bytes=VMEM_LIMIT),
        cost_estimate=pl.CostEstimate(
            flops=scores * 16 * HEAD,
            bytes_accessed=4 * rows * width * (count + 2),
            transcendentals=scores,
        ),
        name="attention_forward",
    )(slots, info, queries, *blocks)


def attend_back(shards, seq, slots, info, queries, out, lse, grads, blocks):
    rows, width = queries.shape
    heads = width // HEAD
    count = 4 * blocks[0].shape[0]
    tile = min(TILE, rows)
    scores = heads * rows * rows * (count + 1) // 2
    return pl.pallas_call(
        functools.partial(backward_kernel, heads, shards, seq),
        out_shape=[jax.ShapeDtypeStruct((rows, width), bf16)]
        + [
            jax.ShapeDtypeStruct((share, rows, 2 * width), bf16)
            for share in (count // 4, count // 4, count // 2)
        ],
        in_specs=[SMEM, SMEM] + [VMEM] * 4 + [ANY] * 4,
        out_specs=[VMEM] + [ANY] * 3,
        scratch_shapes=[
            pltpu.VMEM((count, rows, 2 * width), bf16),
            pltpu.VMEM((count, rows, 2 * width), bf16),
            pltpu.SemaphoreType.DMA((4,)),
            pltpu.SemaphoreType.DMA((3,)),
            pltpu.VMEM((heads, HEAD, tile), f32),
        ],
        compiler_params=pltpu.CompilerParams(vmem_limit_bytes=VMEM_LIMIT),
        cost_estimate=pl.CostEstimate(
            flops=scores * 40 * HEAD,
            bytes_accessed=8 * rows * width * (count + 2),
            transcendentals=scores,
        ),
        name="attention_backward",
    )(slots, info, queries, out, lse, grads, *blocks)


def body(
    layer_input,
    attn_gain,
    attn_shift,
    qkv_weight,
    query_bias,
    value_bias,
    proj_weight,
    proj_bias,
    mlp_gain,
    mlp_shift,
    fc_weight,
    fc_bias,
    out_weight,
    out_bias,
    grad_output,
):
    seqs, piece, width = layer_input.shape
    cycle = lax.axis_size("ctx")
    shards = lax.axis_size("shard")
    here = lax.axis_index("ctx")
    shard_at = lax.axis_index("shard")
    odd = here & 1
    chip_bits = list(range(1, cycle.bit_length() - 1))
    rows = shards * piece
    local_width = qkv_weight.shape[0]
    local_hidden = out_weight.shape[0]
    half_width = local_width // 2
    half_hidden = local_hidden // 2
    quarter = half_hidden // 2
    group = -(-HEADS // shards) * HEAD
    padded = group * shards
    late = [seq >= (seqs + 1) // 2 for seq in range(seqs)]
    tokens = seqs * piece

    def by_heads(weight):
        parts = []
        for third in range(3):
            part = weight[:, third * width : (third + 1) * width]
            parts.append(jnp.pad(part, ((0, 0), (0, padded - width))))
        return jnp.stack(
            [
                jnp.concatenate([part[:, z * group : (z + 1) * group] for part in parts], axis=1)
                for z in range(shards)
            ]
        )

    weight_half = lax.dynamic_slice_in_dim(qkv_weight, odd * half_width, half_width, 0)
    moved = lax.all_to_all(by_heads(weight_half), "shard", 0, 0, tiled=True)
    qkv_own = jnp.stack(pair_joined(moved, odd), axis=1).reshape(width, 3 * group)
    q_weight = qkv_own[:, :group]
    kv_weight = qkv_own[:, group:]

    packed = jnp.concatenate(
        [
            attn_gain,
            attn_shift,
            query_bias,
            value_bias,
            proj_bias,
            mlp_gain,
            mlp_shift,
            out_bias,
            fc_bias,
        ]
    )
    packed = jnp.pad(packed, (0, 16 * width - packed.size)).reshape(16, width)
    inputs = [mirrored(layer_input[s]) if late[s] else layer_input[s] for s in range(seqs)]
    gathered = lax.all_gather(jnp.concatenate(inputs + [packed]), "shard", axis=0)
    small = gathered[:, tokens:].reshape(shards, -1).astype(f32)
    vectors = [small[:, i * local_width : (i + 1) * local_width].reshape(-1) for i in range(8)]
    gain_one, shift_one, query_add, value_add, proj_add, gain_two, shift_two, out_add = vectors
    fc_bias_all = small[:, 8 * local_width : 8 * local_width + local_hidden]
    fc_add = lax.dynamic_index_in_dim(
        fc_bias_all.reshape(shards, 2, half_hidden), odd, 1, False
    ).reshape(-1)

    def own_heads(vector):
        return lax.dynamic_slice_in_dim(
            jnp.pad(vector, (0, padded - width)), shard_at * group, group, 0
        )

    kv_add = jnp.concatenate([jnp.zeros((group,), f32), own_heads(value_add)])
    query_add = own_heads(query_add)

    proj_full = lax.all_gather(proj_weight, "shard", axis=0, tiled=True)
    fc_side = (here >> FC_BIT) & 1
    out_side = (here >> OUT_BIT) & 1
    fc_quarter = lax.all_gather(
        jnp.concatenate(
            [
                lax.dynamic_slice_in_dim(
                    fc_weight,
                    (fc_side * (shards // 2) + z) * local_hidden + odd * half_hidden,
                    half_hidden,
                    1,
                )
                for z in range(shards // 2)
            ],
            axis=1,
        ),
        "shard",
        axis=0,
        tiled=True,
    )
    fc_half = jnp.concatenate(joined(fc_quarter, FC_BIT, fc_side), axis=1)
    out_quarter = lax.all_gather(
        lax.dynamic_slice_in_dim(
            out_weight, odd * half_hidden + out_side * quarter, quarter, 0
        ),
        "shard",
        axis=0,
    )
    out_half = jnp.stack(joined(out_quarter, OUT_BIT, out_side), axis=1).reshape(-1, width)
    block_index = [cycle - 1 - here if late[s] else here for s in range(seqs)]
    orders = [chip_bits + [0], chip_bits[::-1] + [0]]
    group_norms, normed_one, queries, blocks, aparts, slots, infos = [], [], [], [], [], [], []
    for s in range(seqs):
        norm = normalized(
            gathered[:, s * piece : (s + 1) * piece].reshape(rows, width).astype(f32)
        )
        normed = (norm * gain_one + shift_one).astype(bf16)
        group_norms.append(norm)
        normed_one.append(normed)
        own = (dot(normed, kv_weight, ((1,), (0,))) + kv_add).astype(bf16)
        held, apart = spread(own, orders[s % 2], late[s])
        blocks.append(held)
        aparts.append(apart)
        queries.append((dot(normed, q_weight, ((1,), (0,))) + query_add).astype(bf16))
        owners = jnp.arange(cycle)
        distance = (cycle - 1 - owners if late[s] else owners) ^ here
        places = jnp.array([apart.index(i) for i in range(cycle)], jnp.int32)
        slots.append(places[distance])
        infos.append(jnp.stack([block_index[s], shard_at]).astype(jnp.int32))
    saved = []
    attended_parts = []
    for s in range(seqs):
        att, out, lse = attend(shards, slots[s], infos[s], queries[s], blocks[s])
        saved.append((out, lse))
        attended_parts.append(att)
    attended = lax.all_to_all(
        jnp.concatenate(attended_parts, axis=2), "shard", 0, 0, tiled=True
    ).reshape(padded, tokens)[:width]

    inputs32 = jnp.concatenate(inputs).astype(f32)
    grads_own = jnp.concatenate(
        [mirrored(grad_output[s]) if late[s] else grad_output[s] for s in range(seqs)]
    )
    grads32 = grads_own.astype(f32)
    middle = inputs32 + dot(attended, proj_full, ((0,), (0,))) + proj_add
    normed_two = layer_norm(middle, gain_two, shift_two).astype(bf16)

    normed_pair = jnp.concatenate([normed_two, swapped(normed_two, 0)])
    grads_pair = jnp.concatenate([grads_own, swapped(grads_own, 0)])
    preactivation = dot(normed_pair, fc_half, ((1,), (0,))) + fc_add
    hidden = gelu_tanh(preactivation).astype(bf16)
    out_part = dot(hidden, out_half, ((1,), (0,)))
    layer_output = middle + (out_part[:tokens] + swapped(out_part[tokens:], 0)) + out_add
    layer_output = layer_output.astype(bf16)
    grad_hidden = dot(grads_pair, out_half, ((1,), (1,)))
    grad_pre = jax.vjp(gelu_tanh, preactivation)[1](grad_hidden)[0].astype(bf16)
    normed_part = dot(grad_pre, fc_half, ((1,), (1,)))
    grad_normed_two = normed_part[:tokens] + swapped(normed_part[tokens:], 0)
    grad_mid_part, gain_two_grad, shift_two_grad = jax.vjp(
        layer_norm, middle, gain_two, shift_two
    )[1](grad_normed_two)
    grad_middle = grads32 + grad_mid_part
    grad_branch = grad_middle.astype(bf16)

    grad_attended = jnp.pad(
        dot(proj_full, grad_branch, ((1,), (1,))).astype(bf16), ((0, padded - width), (0, 0))
    ).reshape(shards, group, tokens)
    grad_heads = lax.all_to_all(grad_attended, "shard", 0, 0, tiled=True)
    flat = ((0,), (0,))
    def split_sum(first, second, bit, side):
        sent = jnp.where(side, first, second)
        mine = jnp.where(side, second, first)
        return (mine.astype(f32) + swapped(sent, bit).astype(f32)).astype(bf16)

    hidden_then = after(hidden, grad_attended)
    normed_then = after(normed_pair, grad_attended)
    out_grad = dot(hidden_then, grads_pair, flat).astype(bf16).reshape(shards, 2, quarter, width)
    out_whole = out_grad
    out_grad = split_sum(out_grad[:, 0], out_grad[:, 1], OUT_BIT, out_side)
    fc_grad = dot(normed_then, grad_pre, flat).astype(bf16).reshape(shards, local_width, -1)
    fc_whole = fc_grad
    middle_column = fc_grad.shape[2] // 2
    fc_grad = split_sum(
        fc_grad[..., :middle_column], fc_grad[..., middle_column:], FC_BIT, fc_side
    )
    rest = fc_grad.reshape(shards, -1, width)
    cut = rest.shape[1]
    scattered = jnp.concatenate([rest, out_grad], axis=1)
    waits = [(out_whole, fc_whole), (scattered,)] + [()] * seqs
    query_low = [None] * seqs
    kv_parts = [None] * seqs
    for turn, s in enumerate(reversed(range(seqs))):
        out, lse = saved[s]
        heads_grad = after(grad_heads, *waits[turn])
        query_low[s], *kv_parts[s] = attend_back(
            shards, s, slots[s], infos[s], queries[s], out, lse, heads_grad, blocks[s]
        )
    kv_low = [None] * seqs
    normed_parts = []
    gain_one_grad = jnp.zeros((width,), f32)
    shift_one_grad = jnp.zeros((width,), f32)
    for s in range(seqs):
        kv_low[s] = returned(*kv_parts[s], aparts[s], orders[s % 2], late[s])
        part = dot(query_low[s], q_weight, ((1,), (1,))) + dot(kv_low[s], kv_weight, ((1,), (1,)))
        gain_one_grad = gain_one_grad + jnp.sum(part * group_norms[s], axis=0)
        shift_one_grad = shift_one_grad + jnp.sum(part, axis=0)
        normed_parts.append(part.astype(bf16).reshape(shards, piece, width))
    normed_parts = jnp.concatenate(normed_parts, axis=1)
    grad_normed_one = lax.psum_scatter(
        normed_parts, "shard", scatter_dimension=0, tiled=False
    ).astype(f32)
    pull = jax.vjp(lambda v: normalized(v) * gain_one, inputs32)[1]
    input_grad = (grad_middle + pull(grad_normed_one)[0]).astype(bf16)
    def mirrored_back(rows_held):
        parts = [rows_held[s * piece : (s + 1) * piece] for s in range(seqs)]
        return jnp.stack([mirrored(part) if late[s] else part for s, part in enumerate(parts)])

    both = lax.psum_scatter(
        scattered, "shard", scatter_dimension=0, tiled=False
    )
    out_grad = summed_over_chips(both[cut:], [bit for bit in chip_bits if bit != OUT_BIT])
    out_grad = jnp.concatenate(joined(out_grad, OUT_BIT, out_side))
    out_grad = jnp.concatenate(pair_joined(out_grad, odd))
    fc_grad = summed_over_chips(both[:cut], [bit for bit in chip_bits if bit != FC_BIT])
    fc_grad = fc_grad.reshape(local_width, middle_column)
    fc_grad = jnp.concatenate(joined(fc_grad, FC_BIT, fc_side), axis=1)
    fc_halves = pair_joined(fc_grad, odd)
    fc_grad = jnp.concatenate(
        [
            fc_halves[h][:, z * half_hidden : (z + 1) * half_hidden]
            for z in range(shards)
            for h in range(2)
        ],
        axis=1,
    )
    grad = []
    for s in range(seqs):
        normed = after(normed_one[s], normed_parts)
        low = jnp.concatenate([query_low[s], kv_low[s]], axis=1)
        grad.append(dot(normed, low, flat))
    grad = jnp.concatenate(
        [sum(grad), dot(after(attended, normed_parts), grad_branch, ((1,), (0,)))], axis=1
    )
    grad = grad.astype(bf16).reshape(shards, 2, half_width, -1)
    grad = split_sum(grad[:, 0], grad[:, 1], 0, odd)
    grad = after(lax.all_to_all(grad, "shard", 0, 0, tiled=True), grad_normed_one)
    proj_part = jnp.sum(grad[..., 3 * group :].astype(f32), axis=0).astype(bf16)
    grad = jnp.concatenate([grad[z, :, : 3 * group] for z in range(shards)] + [proj_part], axis=1)
    grad = jnp.concatenate(pair_joined(summed_over_chips(grad, chip_bits), odd))
    proj_grad = grad[:, 3 * padded :]
    thirds = [
        jnp.concatenate(
            [
                grad[:, (3 * z + third) * group : (3 * z + third + 1) * group]
                for z in range(shards)
            ],
            axis=1,
        )[:, :width]
        for third in range(3)
    ]
    qkv_grad = jnp.concatenate(thirds, axis=1)

    fc_add_part = jnp.sum(grad_pre.astype(f32), axis=0).reshape(shards, 1, half_hidden)
    fc_add_part = jnp.where(jnp.arange(2)[None, :, None] == odd, fc_add_part, 0.0)

    def all_heads(vector):
        return lax.dynamic_update_slice_in_dim(
            jnp.zeros((padded,), f32), vector, shard_at * group, 0
        )[:width]

    query_sum = sum(jnp.sum(low.astype(f32), axis=0) for low in query_low)
    value_sum = sum(jnp.sum(low[:, group:].astype(f32), axis=0) for low in kv_low)
    sums = reduce_small(
        jnp.concatenate(
            [
                v.reshape(shards, -1)
                for v in (
                    gain_one_grad,
                    shift_one_grad,
                    all_heads(query_sum),
                    all_heads(value_sum),
                    jnp.sum(grad_branch.astype(f32), axis=0),
                    gain_two_grad,
                    shift_two_grad,
                    jnp.sum(grads32, axis=0),
                    fc_add_part,
                )
            ],
            axis=1,
        )
    )
    parts = [sums[i * local_width : (i + 1) * local_width] for i in range(8)]
    return (
        mirrored_back(layer_output),
        mirrored_back(input_grad),
        parts[0],
        parts[1],
        qkv_grad,
        parts[2],
        parts[3],
        proj_grad,
        parts[4],
        parts[5],
        parts[6],
        fc_grad,
        sums[8 * local_width :],
        out_grad,
        parts[7],
    )


def solution(mesh):
    tokens = P(None, ("ctx", "shard"), None)
    vector = P("shard")
    matrix = P("shard", None)
    return jax.shard_map(
        body,
        mesh=mesh,
        in_specs=(
            tokens,
            vector,
            vector,
            matrix,
            vector,
            vector,
            matrix,
            vector,
            vector,
            vector,
            matrix,
            vector,
            matrix,
            vector,
            tokens,
        ),
        out_specs=(
            tokens,
            tokens,
            vector,
            vector,
            matrix,
            vector,
            vector,
            matrix,
            vector,
            vector,
            vector,
            matrix,
            vector,
            matrix,
            vector,
        ),
        check_vma=False,
    )
```

```python
import functools

import jax
import jax.numpy as jnp
from jax import lax
from jax.experimental import pallas as pl
from jax.experimental.pallas import tpu as pltpu
from jax.sharding import PartitionSpec as P

HEADS = 12
HEAD = 64
TILE = 512
EXP2_SCALE = 0.125 * 1.4426950408889634
f32 = jnp.float32
bf16 = jnp.bfloat16
FC_BIT = 1
OUT_BIT = 2
VMEM_LIMIT = 56 * 1024 * 1024


def normalized(values):
    centered = values - jnp.mean(values, axis=-1, keepdims=True)
    variance = jnp.mean(centered * centered, axis=-1, keepdims=True)
    return centered * lax.rsqrt(variance + 1e-05)


def layer_norm(values, gain, shift):
    return normalized(values) * gain + shift


def gelu_tanh(values):
    return jax.nn.gelu(values, approximate=True)


def swapped(block, bit):
    n = lax.axis_size("ctx")
    return lax.ppermute(block, "ctx", [(i, i ^ (1 << bit)) for i in range(n)])


def tree_pairs(aparts, bit, later, late, back):
    n = lax.axis_size("ctx")
    reach = [0]
    for other in later:
        reach += [r ^ (1 << other) for r in reach]
    pairs = []
    for i in range(n):
        target = i ^ (1 << bit)
        queries = [n - 1 - (target ^ r) if late else target ^ r for r in reach]
        if any(i ^ apart <= max(queries) for apart in aparts):
            pairs.append((target, i) if back else (i, target))
    return pairs


def spread(own, order, late, before):
    held, aparts = own[None], [0]
    for bit in order[:-2]:
        pairs = tree_pairs(aparts, bit, order[order.index(bit) + 1 :], late, False)
        held = jnp.concatenate([held, lax.ppermute(held, "ctx", pairs)])
        aparts = aparts + [apart ^ (1 << bit) for apart in aparts]
    bit = order[-2]
    held = after(held, *before)
    received = lax.ppermute(held, "ctx", tree_pairs(aparts, bit, order[-1:], late, False))
    aparts = aparts + [apart ^ (1 << bit) for apart in aparts]
    blocks = [held, received, swapped(held, 0), swapped(received, 0)]
    return blocks, aparts + [apart ^ 1 for apart in aparts]


def added(first, second):
    return (first.astype(f32) + second.astype(f32)).astype(bf16)


def returned(near, middle, far, aparts, order, late):
    received = swapped(far, 0)
    count = near.shape[0]
    middle = added(middle, received[count:])
    pairs = tree_pairs(aparts[:count], order[-2], order[-1:], late, True)
    near = added(added(near, received[:count]), lax.ppermute(middle, "ctx", pairs))
    for bit in order[:-2][::-1]:
        count = near.shape[0] // 2
        pairs = tree_pairs(aparts[:count], bit, order[order.index(bit) + 1 :], late, True)
        near = added(near[:count], lax.ppermute(near[count:], "ctx", pairs))
    return near[0]


def after(value, *others):
    return lax.optimization_barrier((value,) + others)[0]


def mirrored(block):
    n = lax.axis_size("ctx")
    return lax.ppermute(block, "ctx", [(i, n - 1 - i) for i in range(n)])


def shifted(block, distance):
    n = lax.axis_size("shard")
    return lax.ppermute(block, "shard", [(i, (i + distance) % n) for i in range(n)])


def dot(a, b, contract):
    return lax.dot_general(a, b, ((contract[0], contract[1]), ((), ())), preferred_element_type=f32)


def summed_over_chips(part, bits):
    for bit in bits:
        low = part.astype(bf16)
        part = low.astype(f32) + swapped(low, bit).astype(f32)
    return part


def joined(half, bit, side):
    other = swapped(half, bit)
    return jnp.where(side, other, half), jnp.where(side, half, other)


def pair_joined(half, odd):
    return joined(half, 0, odd)


def load_blocks(refs, held, sems):
    each = refs[0].shape[0]
    copies = [
        pltpu.make_async_copy(ref, held.at[pl.ds(i * each, each)], sems.at[i])
        for i, ref in enumerate(refs)
    ]
    for copy in copies:
        copy.start()
    return copies


def slot_of(place, here, order):
    apart = place ^ here
    return sum(((apart >> bit) & 1) << k for k, bit in enumerate(order))


def forward_kernel(heads, shards, order, info, q_ref, *refs):
    kv_refs = refs[:4]
    att_ref, out_ref, lse_ref, held, sems, m_ref, l_ref, acc_ref = refs[4:]
    rows, width = q_ref.shape
    piece = rows // shards
    tile = min(TILE, rows)
    per = rows // tile
    copies = load_blocks(kv_refs, held, sems)
    key_places = lax.broadcasted_iota(jnp.int32, (rows, 1), 0)
    query_places = lax.broadcasted_iota(jnp.int32, (1, rows), 1)
    for copy in copies:
        copy.wait()
    for part in range(per):
        span = slice(part * tile, (part + 1) * tile)

        def step(slot, key_part, masked, start):
            keys_at = slice(key_part * tile, (key_part + 1) * tile)
            allowed = key_places[keys_at] <= query_places[:, span] if masked else None
            for h in range(heads):
                lanes = slice(h * HEAD, (h + 1) * HEAD)
                lanes_v = slice(width + h * HEAD, width + (h + 1) * HEAD)
                q = q_ref[span, lanes]
                k = held[slot, keys_at, lanes]
                v = held[slot, keys_at, lanes_v]
                s = dot(k, q, ((1,), (1,))) * EXP2_SCALE
                if masked:
                    s = jnp.where(allowed, s, -1e30)
                m = jnp.max(s, axis=0, keepdims=True)
                if start:
                    p = jnp.exp2(s - m)
                    l_ref[h] = jnp.sum(p, axis=0, keepdims=True)
                    acc_ref[h] = dot(v, p.astype(bf16), ((0,), (0,)))
                else:
                    old = m_ref[h]
                    m = jnp.maximum(old, m)
                    p = jnp.exp2(s - m)
                    factor = jnp.exp2(old - m)
                    l_ref[h] = l_ref[h] * factor + jnp.sum(p, axis=0, keepdims=True)
                    acc_ref[h] = acc_ref[h] * factor + dot(v, p.astype(bf16), ((0,), (0,)))
                m_ref[h] = m

        for key_part in range(per):
            step(slot_of(info[0], info[1], order), key_part, True, key_part == 0)

        @pl.loop(0, info[0])
        def _(j):
            for key_part in range(per):
                step(slot_of(j, info[1], order), key_part, False, False)

        for h in range(heads):
            total = l_ref[h]
            done = acc_ref[h] / total
            out_ref[h * HEAD : (h + 1) * HEAD, span] = done
            lse_ref[h, :, span] = m_ref[h] + jnp.log2(total)
            low = done.astype(bf16)
            for z in range(tile // piece):
                att_ref[part * (tile // piece) + z, h * HEAD : (h + 1) * HEAD, :] = low[
                    :, z * piece : (z + 1) * piece
                ]


def backward_kernel(heads, shards, order, first, info, q_ref, out_ref, lse_ref, go_ref, *refs):
    kv_refs = refs[:4]
    dq_ref, near_ref, middle_ref, far_ref, held, sums, sems, end_sems, acc_ref = refs[4:]
    count = held.shape[0]
    rows, width = q_ref.shape
    piece = rows // shards
    tile = min(TILE, rows)
    per = rows // tile
    copies = load_blocks(kv_refs, held, sems)
    key_places = lax.broadcasted_iota(jnp.int32, (rows, 1), 0)
    query_places = lax.broadcasted_iota(jnp.int32, (1, rows), 1)

    @pl.loop(info[0] + 1, count)
    def _(j):
        sums[slot_of(j, info[1], order)] = jnp.zeros((rows, 2 * width), bf16)

    for copy in copies:
        copy.wait()
    for part in range(per):
        span = slice(part * tile, (part + 1) * tile)
        pieces = range(part * (tile // piece), (part + 1) * (tile // piece))
        go_all = jnp.concatenate(
            [go_ref[z, :, first : first + piece] for z in pieces], axis=1
        )
        deltas = []
        for h in range(heads):
            lanes = slice(h * HEAD, (h + 1) * HEAD)
            deltas.append(
                jnp.sum(go_all[lanes].astype(f32) * out_ref[lanes, span], axis=0, keepdims=True)
            )

        def step(slot, key_part, masked, start):
            keys_at = slice(key_part * tile, (key_part + 1) * tile)
            allowed = key_places[keys_at] <= query_places[:, span] if masked else None
            for h in range(heads):
                lanes = slice(h * HEAD, (h + 1) * HEAD)
                lanes_v = slice(width + h * HEAD, width + (h + 1) * HEAD)
                q = q_ref[span, lanes]
                go = go_all[lanes]
                k = held[slot, keys_at, lanes]
                v = held[slot, keys_at, lanes_v]
                p = jnp.exp2(dot(k, q, ((1,), (1,))) * EXP2_SCALE - lse_ref[h, :, span])
                if masked:
                    p = jnp.where(allowed, p, 0.0)
                pulled = dot(v, go, ((1,), (0,)))
                slopes = (p * (pulled - deltas[h])).astype(bf16)
                dv = dot(p.astype(bf16), go, ((1,), (1,)))
                dk = dot(slopes, q, ((1,), (0,))) * 0.125
                if part:
                    dk = dk + sums[slot, keys_at, lanes].astype(f32)
                    dv = dv + sums[slot, keys_at, lanes_v].astype(f32)
                sums[slot, keys_at, lanes] = dk.astype(bf16)
                sums[slot, keys_at, lanes_v] = dv.astype(bf16)
                dq = dot(k, slopes, ((0,), (0,)))
                if start:
                    acc_ref[h] = dq
                else:
                    acc_ref[h] += dq

        for key_part in range(per):
            step(slot_of(info[0], info[1], order), key_part, True, key_part == 0)

        @pl.loop(0, info[0])
        def _(j):
            for key_part in range(per):
                step(slot_of(j, info[1], order), key_part, False, False)

        for h in range(heads):
            dq_ref[span, h * HEAD : (h + 1) * HEAD] = (acc_ref[h] * 0.125).T.astype(bf16)
    copies = []
    base = 0
    for i, ref in enumerate((near_ref, middle_ref, far_ref)):
        copies.append(
            pltpu.make_async_copy(sums.at[pl.ds(base, ref.shape[0])], ref, end_sems.at[i])
        )
        base += ref.shape[0]
    for copy in copies:
        copy.start()
    for copy in copies:
        copy.wait()


SMEM = pl.BlockSpec(memory_space=pltpu.SMEM)
VMEM = pl.BlockSpec(memory_space=pltpu.VMEM)
ANY = pl.BlockSpec(memory_space=pl.ANY)


def attend(shards, order, info, queries, blocks):
    rows, width = queries.shape
    heads = width // HEAD
    count = 4 * blocks[0].shape[0]
    tile = min(TILE, rows)
    scores = heads * rows * rows * (count + 1) // 2
    return pl.pallas_call(
        functools.partial(forward_kernel, heads, shards, order),
        out_shape=(
            jax.ShapeDtypeStruct((shards, width, rows // shards), bf16),
            jax.ShapeDtypeStruct((width, rows), f32),
            jax.ShapeDtypeStruct((heads, 1, rows), f32),
        ),
        in_specs=[SMEM, VMEM] + [ANY] * 4,
        out_specs=(VMEM, VMEM, VMEM),
        scratch_shapes=[
            pltpu.VMEM((count, rows, 2 * width), bf16),
            pltpu.SemaphoreType.DMA((4,)),
            pltpu.VMEM((heads, 1, tile), f32),
            pltpu.VMEM((heads, 1, tile), f32),
            pltpu.VMEM((heads, HEAD, tile), f32),
        ],
        compiler_params=pltpu.CompilerParams(vmem_limit_bytes=VMEM_LIMIT),
        cost_estimate=pl.CostEstimate(
            flops=scores * 16 * HEAD,
            bytes_accessed=4 * rows * width * (count + 2),
            transcendentals=scores,
        ),
        name="attention_forward",
    )(info, queries, *blocks)


def attend_back(shards, order, first, info, queries, out, lse, grads, blocks):
    rows, width = queries.shape
    heads = width // HEAD
    count = 4 * blocks[0].shape[0]
    tile = min(TILE, rows)
    scores = heads * rows * rows * (count + 1) // 2
    return pl.pallas_call(
        functools.partial(backward_kernel, heads, shards, order, first),
        out_shape=[jax.ShapeDtypeStruct((rows, width), bf16)]
        + [
            jax.ShapeDtypeStruct((share, rows, 2 * width), bf16)
            for share in (count // 4, count // 4, count // 2)
        ],
        in_specs=[SMEM] + [VMEM] * 4 + [ANY] * 4,
        out_specs=[VMEM] + [ANY] * 3,
        scratch_shapes=[
            pltpu.VMEM((count, rows, 2 * width), bf16),
            pltpu.VMEM((count, rows, 2 * width), bf16),
            pltpu.SemaphoreType.DMA((4,)),
            pltpu.SemaphoreType.DMA((3,)),
            pltpu.VMEM((heads, HEAD, tile), f32),
        ],
        compiler_params=pltpu.CompilerParams(vmem_limit_bytes=VMEM_LIMIT),
        cost_estimate=pl.CostEstimate(
            flops=scores * 40 * HEAD,
            bytes_accessed=8 * rows * width * (count + 2),
            transcendentals=scores,
        ),
        name="attention_backward",
    )(info, queries, out, lse, grads, *blocks)


def body(
    layer_input,
    attn_gain,
    attn_shift,
    qkv_weight,
    query_bias,
    value_bias,
    proj_weight,
    proj_bias,
    mlp_gain,
    mlp_shift,
    fc_weight,
    fc_bias,
    out_weight,
    out_bias,
    grad_output,
):
    seqs, piece, width = layer_input.shape
    cycle = lax.axis_size("ctx")
    shards = lax.axis_size("shard")
    here = lax.axis_index("ctx")
    shard_at = lax.axis_index("shard")
    odd = here & 1
    chip_bits = list(range(1, cycle.bit_length() - 1))
    rows = shards * piece
    local_width = qkv_weight.shape[0]
    local_hidden = out_weight.shape[0]
    half_width = local_width // 2
    half_hidden = local_hidden // 2
    quarter = half_hidden // 2
    group = -(-HEADS // shards) * HEAD
    padded = group * shards
    late = [seq >= (seqs + 1) // 2 for seq in range(seqs)]
    tokens = seqs * piece

    gathered = lax.all_gather(layer_input, "shard", axis=0)

    def by_heads(weight):
        parts = []
        for third in range(3):
            part = weight[:, third * width : (third + 1) * width]
            parts.append(jnp.pad(part, ((0, 0), (0, padded - width))))
        return jnp.stack(
            [
                jnp.concatenate([part[:, z * group : (z + 1) * group] for part in parts], axis=1)
                for z in range(shards)
            ]
        )

    weight_half = lax.dynamic_slice_in_dim(qkv_weight, odd * half_width, half_width, 0)
    packed = jnp.concatenate(
        [
            jnp.stack(
                [attn_gain, attn_shift, query_bias, value_bias, proj_bias, mlp_gain, mlp_shift, out_bias]
            ),
            fc_bias.reshape(-1, local_width),
        ]
    )
    vector_rows = packed.shape[0]
    packed = jnp.pad(packed, ((0, 16 - vector_rows), (0, 3 * group - local_width)))
    moved = lax.all_to_all(
        jnp.concatenate(
            [by_heads(weight_half), jnp.broadcast_to(packed, (shards,) + packed.shape)], axis=1
        ),
        "shard",
        0,
        0,
        tiled=True,
    )
    small = moved[:, half_width : half_width + vector_rows, :local_width].astype(f32)
    qkv_own = jnp.stack(pair_joined(moved[:, :half_width], odd), axis=1).reshape(width, 3 * group)
    q_weight = qkv_own[:, :group]
    kv_weight = qkv_own[:, group:]

    vectors = [small[:, i].reshape(-1) for i in range(8)]
    gain_one, shift_one, query_add, value_add, proj_add, gain_two, shift_two, out_add = vectors
    fc_add = lax.dynamic_index_in_dim(
        small[:, 8:].reshape(shards, 2, half_hidden), odd, 1, False
    ).reshape(-1)

    def own_heads(vector):
        return lax.dynamic_slice_in_dim(
            jnp.pad(vector, (0, padded - width)), shard_at * group, group, 0
        )

    kv_add = jnp.concatenate([jnp.zeros((group,), f32), own_heads(value_add)])
    query_add = own_heads(query_add)

    fc_side = (here >> FC_BIT) & 1
    out_side = (here >> OUT_BIT) & 1
    proj_half = lax.dynamic_slice_in_dim(proj_weight, odd * half_width, half_width, 0)
    fc_quarter = jnp.concatenate(
        [
            lax.dynamic_slice_in_dim(
                fc_weight,
                (fc_side * (shards // 2) + z) * local_hidden + odd * half_hidden,
                half_hidden,
                1,
            )
            for z in range(shards // 2)
        ],
        axis=1,
    )
    moved = lax.all_gather(jnp.concatenate([proj_half, fc_quarter]), "shard", axis=0)
    proj_half = pair_joined(moved[:, :half_width], odd)
    proj_full = jnp.stack(proj_half, axis=1).reshape(width, width)
    fc_quarter = moved[:, half_width:].reshape(width, -1)
    fc_half = jnp.concatenate(joined(fc_quarter, FC_BIT, fc_side), axis=1)
    out_quarter = lax.all_gather(
        lax.dynamic_slice_in_dim(
            out_weight, odd * half_hidden + out_side * quarter, quarter, 0
        ),
        "shard",
        axis=0,
    )
    out_half = jnp.stack(joined(out_quarter, OUT_BIT, out_side), axis=1).reshape(-1, width)
    orders = [chip_bits + [0], chip_bits[::-1] + [0]]
    orders = [orders[s % 2] for s in range(seqs)]
    group_norms, normed_one, own_blocks, queries, infos = [], [], [], [], []
    for s in range(seqs):
        norm = normalized(gathered[:, s].reshape(rows, width).astype(f32))
        normed = (norm * gain_one + shift_one).astype(bf16)
        group_norms.append(norm)
        normed_one.append(normed)
        own_blocks.append((dot(normed, kv_weight, ((1,), (0,))) + kv_add).astype(bf16))
        queries.append((dot(normed, q_weight, ((1,), (0,))) + query_add).astype(bf16))
        infos.append(jnp.stack([cycle - 1 - here if late[s] else here, here]).astype(jnp.int32))
    spreads = [spread(own_blocks[s], orders[s], late[s], queries) for s in range(seqs)]
    queries = [mirrored(queries[s]) if late[s] else queries[s] for s in range(seqs)]
    blocks = [blocks for blocks, _ in spreads]
    aparts = [apart for _, apart in spreads]
    saved = [None] * seqs
    attended_parts = [None] * seqs
    for s in reversed(range(seqs)):
        att, *saved[s] = attend(shards, orders[s], infos[s], queries[s], blocks[s])
        attended_parts[s] = mirrored(att) if late[s] else att
    attended = lax.all_to_all(
        jnp.concatenate(attended_parts, axis=2), "shard", 0, 0, tiled=True
    ).reshape(padded, tokens)[:width]

    inputs32 = layer_input.reshape(tokens, width).astype(f32)
    grads_own = grad_output.reshape(tokens, width)
    grads32 = grads_own.astype(f32)
    middle = inputs32 + dot(attended, proj_full, ((0,), (0,))) + proj_add
    normed_two = layer_norm(middle, gain_two, shift_two).astype(bf16)

    normed_pair = jnp.concatenate([normed_two, swapped(normed_two, 0)])
    grads_pair = jnp.concatenate([grads_own, swapped(grads_own, 0)])
    preactivation = dot(normed_pair, fc_half, ((1,), (0,))) + fc_add
    hidden = gelu_tanh(preactivation).astype(bf16)
    out_part = dot(hidden, out_half, ((1,), (0,)))
    layer_output = middle + (out_part[:tokens] + swapped(out_part[tokens:], 0)) + out_add
    layer_output = layer_output.astype(bf16)
    grad_hidden = dot(grads_pair, out_half, ((1,), (1,)))
    grad_pre = jax.vjp(gelu_tanh, preactivation)[1](grad_hidden)[0].astype(bf16)
    normed_part = dot(grad_pre, fc_half, ((1,), (1,)))
    grad_normed_two = normed_part[:tokens] + swapped(normed_part[tokens:], 0)
    grad_mid_part, gain_two_grad, shift_two_grad = jax.vjp(
        layer_norm, middle, gain_two, shift_two
    )[1](grad_normed_two)
    grad_middle = grads32 + grad_mid_part
    grad_branch = grad_middle.astype(bf16)

    grad_attended = jnp.pad(
        dot(proj_full, grad_branch, ((1,), (1,))).astype(bf16), ((0, padded - width), (0, 0))
    ).reshape(shards, group, tokens)
    grad_heads = lax.all_to_all(grad_attended, "shard", 0, 0, tiled=True)
    flat = ((0,), (0,))

    def parted(first, second, side):
        return jnp.where(side, second, first), jnp.where(side, first, second)

    proj_grad = dot(attended, grad_branch, ((1,), (0,))).astype(bf16)
    proj_grad = proj_grad.reshape(shards, 2, half_width, width)
    mine, sent = parted(proj_grad[:, 0], proj_grad[:, 1], odd)
    proj_grad = added(mine, swapped(sent, 0))
    fc_grad = dot(normed_pair, grad_pre, flat).astype(bf16).reshape(shards, local_width, -1)
    column = fc_grad.shape[2] // 2
    fc_mine, fc_sent = parted(
        jnp.concatenate([fc_grad[..., :column], proj_grad[:, : half_width // 2]], axis=1),
        jnp.concatenate([fc_grad[..., column:], proj_grad[:, half_width // 2 :]], axis=1),
        fc_side,
    )
    out_grad = dot(hidden, grads_pair, flat).astype(bf16).reshape(shards, 2, quarter, width)
    out_mine, out_sent = parted(out_grad[:, 0], out_grad[:, 1], out_side)
    fc_received = swapped(fc_sent, FC_BIT)
    out_received = swapped(out_sent, OUT_BIT)

    query_low = [None] * seqs
    kv_parts = [None] * seqs
    grad_heads = after(grad_heads, fc_sent, out_sent)
    for s in range(seqs):
        heads_grad, first = grad_heads, s * piece
        if late[s]:
            heads_grad, first = mirrored(grad_heads[:, :, s * piece : (s + 1) * piece]), 0
        low, *kv_parts[s] = attend_back(
            shards, orders[s], first, infos[s], queries[s], *saved[s], heads_grad, blocks[s]
        )
        query_low[s] = mirrored(low) if late[s] else low

    ended = [part for parts in kv_parts for part in parts[:1]]
    scattered = jnp.concatenate(
        [
            added(fc_mine, after(fc_received, *ended)),
            added(out_mine, after(out_received, *ended)),
        ],
        axis=1,
    )
    both = lax.psum_scatter(scattered, "shard", scatter_dimension=0, tiled=False)

    kv_low = [None] * seqs
    normed_parts = []
    gain_one_grad = jnp.zeros((width,), f32)
    shift_one_grad = jnp.zeros((width,), f32)
    for s in range(seqs):
        kv_low[s] = returned(*kv_parts[s], aparts[s], orders[s], late[s])
        part = dot(query_low[s], q_weight, ((1,), (1,))) + dot(kv_low[s], kv_weight, ((1,), (1,)))
        gain_one_grad = gain_one_grad + jnp.sum(part * group_norms[s], axis=0)
        shift_one_grad = shift_one_grad + jnp.sum(part, axis=0)
        normed_parts.append(part.astype(bf16).reshape(shards, piece, width))
    fc_add_part = jnp.sum(grad_pre.astype(f32), axis=0).reshape(shards, 1, half_hidden)
    fc_add_part = jnp.where(jnp.arange(2)[None, :, None] == odd, fc_add_part, 0.0)

    def all_heads(vector):
        return lax.dynamic_update_slice_in_dim(
            jnp.zeros((padded,), f32), vector, shard_at * group, 0
        )[:width]

    query_sum = sum(jnp.sum(low.astype(f32), axis=0) for low in query_low)
    value_sum = sum(jnp.sum(low[:, group:].astype(f32), axis=0) for low in kv_low)
    vectors = jnp.stack(
        [
            gain_one_grad,
            shift_one_grad,
            all_heads(query_sum),
            all_heads(value_sum),
            jnp.sum(grad_branch.astype(f32), axis=0),
            gain_two_grad,
            shift_two_grad,
            jnp.sum(grads32, axis=0),
        ]
    )
    vectors = jnp.concatenate(
        [
            vectors.reshape(8, shards, local_width).transpose(1, 0, 2),
            fc_add_part.reshape(shards, -1, local_width),
        ],
        axis=1,
    ).astype(bf16)
    normed_parts = jnp.concatenate(
        normed_parts
        + [jnp.pad(vectors, ((0, 0), (0, 16 - vector_rows), (0, width - local_width)))],
        axis=1,
    )
    summed = lax.psum_scatter(normed_parts, "shard", scatter_dimension=0, tiled=False).astype(f32)
    pull = jax.vjp(lambda v: normalized(v) * gain_one, inputs32)[1]
    input_grad = (grad_middle + pull(summed[:tokens])[0]).astype(bf16)
    sums = summed[tokens : tokens + vector_rows, :local_width]
    for bit in range(cycle.bit_length() - 1):
        sums = sums + swapped(sums, bit)

    cut = both.shape[0] - quarter
    out_grad = summed_over_chips(both[cut:], [bit for bit in chip_bits if bit != OUT_BIT])
    out_grad = jnp.concatenate(joined(out_grad, OUT_BIT, out_side))
    out_grad = jnp.concatenate(pair_joined(out_grad, odd))
    rest = summed_over_chips(both[:cut], [bit for bit in chip_bits if bit != FC_BIT])
    first, second = joined(rest, FC_BIT, fc_side)
    proj_grad = jnp.concatenate([first[local_width:], second[local_width:]])
    proj_grad = jnp.concatenate(pair_joined(proj_grad, odd))
    fc_grad = jnp.concatenate([first[:local_width], second[:local_width]], axis=1)
    fc_halves = pair_joined(fc_grad, odd)
    fc_grad = jnp.concatenate(
        [
            fc_halves[h][:, z * half_hidden : (z + 1) * half_hidden]
            for z in range(shards)
            for h in range(2)
        ],
        axis=1,
    )

    grad = []
    for s in range(seqs):
        normed = after(normed_one[s], normed_parts)
        low = jnp.concatenate([query_low[s], kv_low[s]], axis=1)
        grad.append(dot(normed, low, flat))
    grad = sum(grad).astype(bf16).reshape(shards, 2, half_width, -1)
    mine, sent = parted(grad[:, 0], grad[:, 1], odd)
    grad = lax.all_to_all(added(mine, swapped(sent, 0)), "shard", 0, 0, tiled=True)
    grad = jnp.concatenate([grad[z] for z in range(shards)], axis=1)
    grad = jnp.concatenate(pair_joined(summed_over_chips(grad, chip_bits), odd))
    thirds = [
        jnp.concatenate(
            [
                grad[:, (3 * z + third) * group : (3 * z + third + 1) * group]
                for z in range(shards)
            ],
            axis=1,
        )[:, :width]
        for third in range(3)
    ]
    qkv_grad = jnp.concatenate(thirds, axis=1)

    return (
        layer_output.reshape(seqs, piece, width),
        input_grad.reshape(seqs, piece, width),
        sums[0],
        sums[1],
        qkv_grad,
        sums[2],
        sums[3],
        proj_grad,
        sums[4],
        sums[5],
        sums[6],
        fc_grad,
        sums[8:].reshape(-1),
        out_grad,
        sums[7],
    )


def solution(mesh):
    tokens = P(None, ("ctx", "shard"), None)
    vector = P("shard")
    matrix = P("shard", None)
    return jax.shard_map(
        body,
        mesh=mesh,
        in_specs=(
            tokens,
            vector,
            vector,
            matrix,
            vector,
            vector,
            matrix,
            vector,
            vector,
            vector,
            matrix,
            vector,
            matrix,
            vector,
            tokens,
        ),
        out_specs=(
            tokens,
            tokens,
            vector,
            vector,
            matrix,
            vector,
            vector,
            matrix,
            vector,
            vector,
            vector,
            matrix,
            vector,
            matrix,
            vector,
        ),
        check_vma=False,
    )
```

```python
import functools

import jax
import jax.numpy as jnp
from jax import lax
from jax.experimental import pallas as pl
from jax.experimental.pallas import tpu as pltpu
from jax.sharding import PartitionSpec as P

HEADS = 12
HEAD = 64
TILE = 512
EXP2_SCALE = 0.125 * 1.4426950408889634
f32 = jnp.float32
bf16 = jnp.bfloat16
FC_BIT = 1
OUT_BIT = 2
VMEM_LIMIT = 56 * 1024 * 1024


def normalized(values):
    centered = values - jnp.mean(values, axis=-1, keepdims=True)
    variance = jnp.mean(centered * centered, axis=-1, keepdims=True)
    return centered * lax.rsqrt(variance + 1e-05)


def layer_norm(values, gain, shift):
    return normalized(values) * gain + shift


def gelu_tanh(values):
    return jax.nn.gelu(values, approximate=True)


def swapped(block, bit):
    n = lax.axis_size("ctx")
    return lax.ppermute(block, "ctx", [(i, i ^ (1 << bit)) for i in range(n)])


def tree_pairs(aparts, bit, later, late, back):
    n = lax.axis_size("ctx")
    reach = [0]
    for other in later:
        reach += [r ^ (1 << other) for r in reach]
    pairs = []
    for i in range(n):
        target = i ^ (1 << bit)
        queries = [n - 1 - (target ^ r) if late else target ^ r for r in reach]
        if any(i ^ apart <= max(queries) for apart in aparts):
            pairs.append((target, i) if back else (i, target))
    return pairs


def spread(own, order, late, before):
    held, aparts = own[None], [0]
    for bit in order[:-2]:
        pairs = tree_pairs(aparts, bit, order[order.index(bit) + 1 :], late, False)
        held = jnp.concatenate([held, lax.ppermute(held, "ctx", pairs)])
        aparts = aparts + [apart ^ (1 << bit) for apart in aparts]
    bit = order[-2]
    held = after(held, *before)
    received = lax.ppermute(held, "ctx", tree_pairs(aparts, bit, order[-1:], late, False))
    aparts = aparts + [apart ^ (1 << bit) for apart in aparts]
    blocks = [held, received, swapped(held, 0), swapped(received, 0)]
    return blocks, aparts + [apart ^ 1 for apart in aparts]


def added(first, second):
    return (first.astype(f32) + second.astype(f32)).astype(bf16)


def returned(near, middle, far, aparts, order, late):
    received = swapped(far, 0)
    count = near.shape[0]
    middle = added(middle, received[count:])
    pairs = tree_pairs(aparts[:count], order[-2], order[-1:], late, True)
    near = added(added(near, received[:count]), lax.ppermute(middle, "ctx", pairs))
    for bit in order[:-2][::-1]:
        count = near.shape[0] // 2
        pairs = tree_pairs(aparts[:count], bit, order[order.index(bit) + 1 :], late, True)
        near = added(near[:count], lax.ppermute(near[count:], "ctx", pairs))
    return near[0]


def after(value, *others):
    return lax.optimization_barrier((value,) + others)[0]


def mirrored(block):
    n = lax.axis_size("ctx")
    return lax.ppermute(block, "ctx", [(i, n - 1 - i) for i in range(n)])


def shifted(block, distance):
    n = lax.axis_size("shard")
    return lax.ppermute(block, "shard", [(i, (i + distance) % n) for i in range(n)])


def dot(a, b, contract):
    return lax.dot_general(a, b, ((contract[0], contract[1]), ((), ())), preferred_element_type=f32)


def summed_over_chips(part, bits):
    for bit in bits:
        low = part.astype(bf16)
        part = low.astype(f32) + swapped(low, bit).astype(f32)
    return part


def joined(half, bit, side):
    other = swapped(half, bit)
    return jnp.where(side, other, half), jnp.where(side, half, other)


def pair_joined(half, odd):
    return joined(half, 0, odd)


def load_blocks(refs, held, sems):
    each = refs[0].shape[0]
    copies = [
        pltpu.make_async_copy(ref, held.at[pl.ds(i * each, each)], sems.at[i])
        for i, ref in enumerate(refs)
    ]
    for copy in copies:
        copy.start()
    return copies


def slot_of(place, here, order):
    apart = place ^ here
    return sum(((apart >> bit) & 1) << k for k, bit in enumerate(order))


def forward_kernel(heads, shards, order, info, q_ref, *refs):
    kv_refs = refs[:4]
    att_ref, out_ref, lse_ref, held, sems, m_ref, l_ref, acc_ref = refs[4:]
    rows, width = q_ref.shape
    piece = rows // shards
    tile = min(TILE, rows)
    per = rows // tile
    copies = load_blocks(kv_refs, held, sems)
    key_places = lax.broadcasted_iota(jnp.int32, (rows, 1), 0)
    query_places = lax.broadcasted_iota(jnp.int32, (1, rows), 1)
    for copy in copies:
        copy.wait()
    for part in range(per):
        span = slice(part * tile, (part + 1) * tile)

        def step(slot, key_part, masked, start):
            keys_at = slice(key_part * tile, (key_part + 1) * tile)
            allowed = key_places[keys_at] <= query_places[:, span] if masked else None
            for h in range(heads):
                lanes = slice(h * HEAD, (h + 1) * HEAD)
                lanes_v = slice(width + h * HEAD, width + (h + 1) * HEAD)
                q = q_ref[span, lanes]
                k = held[slot, keys_at, lanes]
                v = held[slot, keys_at, lanes_v]
                s = dot(k, q, ((1,), (1,))) * EXP2_SCALE
                if masked:
                    s = jnp.where(allowed, s, -1e30)
                m = jnp.max(s, axis=0, keepdims=True)
                if start:
                    p = jnp.exp2(s - m)
                    l_ref[h] = jnp.sum(p, axis=0, keepdims=True)
                    acc_ref[h] = dot(v, p.astype(bf16), ((0,), (0,)))
                else:
                    old = m_ref[h]
                    m = jnp.maximum(old, m)
                    p = jnp.exp2(s - m)
                    factor = jnp.exp2(old - m)
                    l_ref[h] = l_ref[h] * factor + jnp.sum(p, axis=0, keepdims=True)
                    acc_ref[h] = acc_ref[h] * factor + dot(v, p.astype(bf16), ((0,), (0,)))
                m_ref[h] = m

        for key_part in range(per):
            step(slot_of(info[0], info[1], order), key_part, True, key_part == 0)

        @pl.loop(0, info[0])
        def _(j):
            for key_part in range(per):
                step(slot_of(j, info[1], order), key_part, False, False)

        for h in range(heads):
            total = l_ref[h]
            done = acc_ref[h] / total
            out_ref[h * HEAD : (h + 1) * HEAD, span] = done
            lse_ref[h, :, span] = m_ref[h] + jnp.log2(total)
            low = done.astype(bf16)
            for z in range(tile // piece):
                att_ref[part * (tile // piece) + z, h * HEAD : (h + 1) * HEAD, :] = low[
                    :, z * piece : (z + 1) * piece
                ]


def backward_kernel(heads, shards, order, first, info, q_ref, out_ref, lse_ref, go_ref, *refs):
    kv_refs = refs[:4]
    dq_ref, near_ref, middle_ref, far_ref, held, sums, sems, end_sems, acc_ref = refs[4:]
    count = held.shape[0]
    rows, width = q_ref.shape
    piece = rows // shards
    tile = min(TILE, rows)
    per = rows // tile
    copies = load_blocks(kv_refs, held, sems)
    key_places = lax.broadcasted_iota(jnp.int32, (rows, 1), 0)
    query_places = lax.broadcasted_iota(jnp.int32, (1, rows), 1)

    @pl.loop(info[0] + 1, count)
    def _(j):
        sums[slot_of(j, info[1], order)] = jnp.zeros((rows, 2 * width), bf16)

    for copy in copies:
        copy.wait()
    for part in range(per):
        span = slice(part * tile, (part + 1) * tile)
        pieces = range(part * (tile // piece), (part + 1) * (tile // piece))
        go_all = jnp.concatenate(
            [go_ref[z, :, first : first + piece] for z in pieces], axis=1
        )
        deltas = []
        for h in range(heads):
            lanes = slice(h * HEAD, (h + 1) * HEAD)
            deltas.append(
                jnp.sum(go_all[lanes].astype(f32) * out_ref[lanes, span], axis=0, keepdims=True)
            )

        def step(slot, key_part, masked, start):
            keys_at = slice(key_part * tile, (key_part + 1) * tile)
            allowed = key_places[keys_at] <= query_places[:, span] if masked else None
            for h in range(heads):
                lanes = slice(h * HEAD, (h + 1) * HEAD)
                lanes_v = slice(width + h * HEAD, width + (h + 1) * HEAD)
                q = q_ref[span, lanes]
                go = go_all[lanes]
                k = held[slot, keys_at, lanes]
                v = held[slot, keys_at, lanes_v]
                p = jnp.exp2(dot(k, q, ((1,), (1,))) * EXP2_SCALE - lse_ref[h, :, span])
                if masked:
                    p = jnp.where(allowed, p, 0.0)
                pulled = dot(v, go, ((1,), (0,)))
                slopes = (p * (pulled - deltas[h])).astype(bf16)
                dv = dot(p.astype(bf16), go, ((1,), (1,)))
                dk = dot(slopes, q, ((1,), (0,))) * 0.125
                if part:
                    dk = dk + sums[slot, keys_at, lanes].astype(f32)
                    dv = dv + sums[slot, keys_at, lanes_v].astype(f32)
                sums[slot, keys_at, lanes] = dk.astype(bf16)
                sums[slot, keys_at, lanes_v] = dv.astype(bf16)
                dq = dot(k, slopes, ((0,), (0,)))
                if start:
                    acc_ref[h] = dq
                else:
                    acc_ref[h] += dq

        for key_part in range(per):
            step(slot_of(info[0], info[1], order), key_part, True, key_part == 0)

        @pl.loop(0, info[0])
        def _(j):
            for key_part in range(per):
                step(slot_of(j, info[1], order), key_part, False, False)

        for h in range(heads):
            dq_ref[span, h * HEAD : (h + 1) * HEAD] = (acc_ref[h] * 0.125).T.astype(bf16)
    copies = []
    base = 0
    for i, ref in enumerate((near_ref, middle_ref, far_ref)):
        copies.append(
            pltpu.make_async_copy(sums.at[pl.ds(base, ref.shape[0])], ref, end_sems.at[i])
        )
        base += ref.shape[0]
    for copy in copies:
        copy.start()
    for copy in copies:
        copy.wait()


SMEM = pl.BlockSpec(memory_space=pltpu.SMEM)
VMEM = pl.BlockSpec(memory_space=pltpu.VMEM)
ANY = pl.BlockSpec(memory_space=pl.ANY)


def attend(shards, order, info, queries, blocks):
    rows, width = queries.shape
    heads = width // HEAD
    count = 4 * blocks[0].shape[0]
    tile = min(TILE, rows)
    scores = heads * rows * rows * (count + 1) // 2
    return pl.pallas_call(
        functools.partial(forward_kernel, heads, shards, order),
        out_shape=(
            jax.ShapeDtypeStruct((shards, width, rows // shards), bf16),
            jax.ShapeDtypeStruct((width, rows), f32),
            jax.ShapeDtypeStruct((heads, 1, rows), f32),
        ),
        in_specs=[SMEM, VMEM] + [ANY] * 4,
        out_specs=(VMEM, VMEM, VMEM),
        scratch_shapes=[
            pltpu.VMEM((count, rows, 2 * width), bf16),
            pltpu.SemaphoreType.DMA((4,)),
            pltpu.VMEM((heads, 1, tile), f32),
            pltpu.VMEM((heads, 1, tile), f32),
            pltpu.VMEM((heads, HEAD, tile), f32),
        ],
        compiler_params=pltpu.CompilerParams(vmem_limit_bytes=VMEM_LIMIT),
        cost_estimate=pl.CostEstimate(
            flops=scores * 16 * HEAD,
            bytes_accessed=4 * rows * width * (count + 2),
            transcendentals=scores,
        ),
        name="attention_forward",
    )(info, queries, *blocks)


def attend_back(shards, order, first, info, queries, out, lse, grads, blocks):
    rows, width = queries.shape
    heads = width // HEAD
    count = 4 * blocks[0].shape[0]
    tile = min(TILE, rows)
    scores = heads * rows * rows * (count + 1) // 2
    return pl.pallas_call(
        functools.partial(backward_kernel, heads, shards, order, first),
        out_shape=[jax.ShapeDtypeStruct((rows, width), bf16)]
        + [
            jax.ShapeDtypeStruct((share, rows, 2 * width), bf16)
            for share in (count // 4, count // 4, count // 2)
        ],
        in_specs=[SMEM] + [VMEM] * 4 + [ANY] * 4,
        out_specs=[VMEM] + [ANY] * 3,
        scratch_shapes=[
            pltpu.VMEM((count, rows, 2 * width), bf16),
            pltpu.VMEM((count, rows, 2 * width), bf16),
            pltpu.SemaphoreType.DMA((4,)),
            pltpu.SemaphoreType.DMA((3,)),
            pltpu.VMEM((heads, HEAD, tile), f32),
        ],
        compiler_params=pltpu.CompilerParams(vmem_limit_bytes=VMEM_LIMIT),
        cost_estimate=pl.CostEstimate(
            flops=scores * 40 * HEAD,
            bytes_accessed=8 * rows * width * (count + 2),
            transcendentals=scores,
        ),
        name="attention_backward",
    )(info, queries, out, lse, grads, *blocks)


def body(
    layer_input,
    attn_gain,
    attn_shift,
    qkv_weight,
    query_bias,
    value_bias,
    proj_weight,
    proj_bias,
    mlp_gain,
    mlp_shift,
    fc_weight,
    fc_bias,
    out_weight,
    out_bias,
    grad_output,
):
    seqs, piece, width = layer_input.shape
    cycle = lax.axis_size("ctx")
    shards = lax.axis_size("shard")
    here = lax.axis_index("ctx")
    shard_at = lax.axis_index("shard")
    odd = here & 1
    chip_bits = list(range(1, cycle.bit_length() - 1))
    rows = shards * piece
    local_width = qkv_weight.shape[0]
    local_hidden = out_weight.shape[0]
    half_width = local_width // 2
    half_hidden = local_hidden // 2
    quarter = half_hidden // 2
    group = -(-HEADS // shards) * HEAD
    padded = group * shards
    late = [seq >= (seqs + 1) // 2 for seq in range(seqs)]
    tokens = seqs * piece

    gathered = lax.all_gather(layer_input, "shard", axis=0)

    def by_heads(weight):
        parts = []
        for third in range(3):
            part = weight[:, third * width : (third + 1) * width]
            parts.append(jnp.pad(part, ((0, 0), (0, padded - width))))
        return jnp.stack(
            [
                jnp.concatenate([part[:, z * group : (z + 1) * group] for part in parts], axis=1)
                for z in range(shards)
            ]
        )

    joins = chip_bits[::-1] + [0]
    share = local_width // cycle
    weight_share = lax.dynamic_slice_in_dim(
        qkv_weight, sum(((here >> bit) & 1) << k for k, bit in enumerate(joins)) * share, share, 0
    )
    packed = jnp.concatenate(
        [
            jnp.stack(
                [attn_gain, attn_shift, query_bias, value_bias, proj_bias, mlp_gain, mlp_shift, out_bias]
            ),
            fc_bias.reshape(-1, local_width),
        ]
    )
    vector_rows = packed.shape[0]
    packed = jnp.pad(packed, ((0, 16 - vector_rows), (0, 3 * group - local_width)))
    moved = lax.all_to_all(
        jnp.concatenate(
            [by_heads(weight_share), jnp.broadcast_to(packed, (shards,) + packed.shape)], axis=1
        ),
        "shard",
        0,
        0,
        tiled=True,
    )
    small = moved[:, share : share + vector_rows, :local_width].astype(f32)
    qkv_own = moved[:, :share]
    for bit in joins:
        qkv_own = jnp.concatenate(joined(qkv_own, bit, (here >> bit) & 1), axis=1)
    qkv_own = qkv_own.reshape(width, 3 * group)
    q_weight = qkv_own[:, :group]
    kv_weight = qkv_own[:, group:]

    vectors = [small[:, i].reshape(-1) for i in range(8)]
    gain_one, shift_one, query_add, value_add, proj_add, gain_two, shift_two, out_add = vectors
    fc_add = lax.dynamic_index_in_dim(
        small[:, 8:].reshape(shards, 2, half_hidden), odd, 1, False
    ).reshape(-1)

    def own_heads(vector):
        return lax.dynamic_slice_in_dim(
            jnp.pad(vector, (0, padded - width)), shard_at * group, group, 0
        )

    kv_add = jnp.concatenate([jnp.zeros((group,), f32), own_heads(value_add)])
    query_add = own_heads(query_add)

    fc_side = (here >> FC_BIT) & 1
    out_side = (here >> OUT_BIT) & 1
    proj_half = lax.dynamic_slice_in_dim(proj_weight, odd * half_width, half_width, 0)
    fc_quarter = jnp.concatenate(
        [
            lax.dynamic_slice_in_dim(
                fc_weight,
                (fc_side * (shards // 2) + z) * local_hidden + odd * half_hidden,
                half_hidden,
                1,
            )
            for z in range(shards // 2)
        ],
        axis=1,
    )
    moved = lax.all_gather(jnp.concatenate([proj_half, fc_quarter]), "shard", axis=0)
    proj_half = pair_joined(moved[:, :half_width], odd)
    proj_full = jnp.stack(proj_half, axis=1).reshape(width, width)
    fc_quarter = moved[:, half_width:].reshape(width, -1)
    fc_half = jnp.concatenate(joined(fc_quarter, FC_BIT, fc_side), axis=1)
    out_quarter = lax.dynamic_slice_in_dim(
        out_weight, odd * half_hidden + out_side * quarter, quarter, 0
    )
    out_quarter = lax.all_gather(after(out_quarter, gathered), "shard", axis=0)

    orders = [chip_bits + [0], chip_bits[::-1] + [0]]
    orders = [orders[s % 2] for s in range(seqs)]
    group_norms, normed_one, own_blocks, queries, infos = [], [], [], [], []
    for s in range(seqs):
        norm = normalized(gathered[:, s].reshape(rows, width).astype(f32))
        normed = (norm * gain_one + shift_one).astype(bf16)
        group_norms.append(norm)
        normed_one.append(normed)
        own_blocks.append((dot(normed, kv_weight, ((1,), (0,))) + kv_add).astype(bf16))
        queries.append((dot(normed, q_weight, ((1,), (0,))) + query_add).astype(bf16))
        infos.append(jnp.stack([cycle - 1 - here if late[s] else here, here]).astype(jnp.int32))
    spreads = [spread(own_blocks[s], orders[s], late[s], queries) for s in range(seqs)]
    queries = [mirrored(queries[s]) if late[s] else queries[s] for s in range(seqs)]
    blocks = [blocks for blocks, _ in spreads]
    aparts = [apart for _, apart in spreads]
    saved = [None] * seqs
    attended_parts = [None] * seqs
    for s in reversed(range(seqs)):
        att, *saved[s] = attend(shards, orders[s], infos[s], queries[s], blocks[s])
        attended_parts[s] = mirrored(att) if late[s] else att
    attended = after(jnp.concatenate(attended_parts, axis=2), fc_half)
    attended = lax.all_to_all(attended, "shard", 0, 0, tiled=True).reshape(padded, tokens)[:width]
    out_quarter = after(out_quarter, *attended_parts)
    out_half = jnp.stack(joined(out_quarter, OUT_BIT, out_side), axis=1).reshape(-1, width)

    inputs32 = layer_input.reshape(tokens, width).astype(f32)
    grads_own = grad_output.reshape(tokens, width)
    grads32 = grads_own.astype(f32)
    middle = inputs32 + dot(attended, proj_full, ((0,), (0,))) + proj_add
    normed_two = layer_norm(middle, gain_two, shift_two).astype(bf16)

    normed_pair = jnp.concatenate([normed_two, swapped(normed_two, 0)])
    grads_pair = jnp.concatenate([grads_own, swapped(grads_own, 0)])
    preactivation = dot(normed_pair, fc_half, ((1,), (0,))) + fc_add
    hidden = gelu_tanh(preactivation).astype(bf16)
    out_part = dot(hidden, out_half, ((1,), (0,)))
    layer_output = middle + (out_part[:tokens] + swapped(out_part[tokens:], 0)) + out_add
    layer_output = layer_output.astype(bf16)
    grad_hidden = dot(grads_pair, out_half, ((1,), (1,)))
    grad_pre = jax.vjp(gelu_tanh, preactivation)[1](grad_hidden)[0].astype(bf16)
    normed_part = dot(grad_pre, fc_half, ((1,), (1,)))
    grad_normed_two = normed_part[:tokens] + swapped(normed_part[tokens:], 0)
    grad_mid_part, gain_two_grad, shift_two_grad = jax.vjp(
        layer_norm, middle, gain_two, shift_two
    )[1](grad_normed_two)
    grad_middle = grads32 + grad_mid_part
    grad_branch = grad_middle.astype(bf16)

    grad_attended = jnp.pad(
        dot(proj_full, grad_branch, ((1,), (1,))).astype(bf16), ((0, padded - width), (0, 0))
    ).reshape(shards, group, tokens)
    grad_heads = lax.all_to_all(grad_attended, "shard", 0, 0, tiled=True)
    flat = ((0,), (0,))

    def parted(first, second, side):
        return jnp.where(side, second, first), jnp.where(side, first, second)

    proj_grad = dot(attended, grad_branch, ((1,), (0,))).astype(bf16)
    proj_grad = proj_grad.reshape(shards, 2, half_width, width)
    mine, sent = parted(proj_grad[:, 0], proj_grad[:, 1], odd)
    proj_grad = added(mine, swapped(sent, 0))
    fc_grad = dot(normed_pair, grad_pre, flat).astype(bf16).reshape(shards, local_width, -1)
    column = fc_grad.shape[2] // 2
    fc_mine, fc_sent = parted(
        jnp.concatenate([fc_grad[..., :column], proj_grad[:, : half_width // 2]], axis=1),
        jnp.concatenate([fc_grad[..., column:], proj_grad[:, half_width // 2 :]], axis=1),
        fc_side,
    )
    out_grad = dot(hidden, grads_pair, flat).astype(bf16).reshape(shards, 2, quarter, width)
    out_mine, out_sent = parted(out_grad[:, 0], out_grad[:, 1], out_side)
    fc_received = swapped(fc_sent, FC_BIT)
    out_received = swapped(out_sent, OUT_BIT)

    query_low = [None] * seqs
    kv_parts = [None] * seqs
    scattered = jnp.concatenate([added(fc_mine, fc_received), added(out_mine, out_received)], axis=1)
    grad_heads = after(grad_heads, scattered)
    for s in range(seqs):
        heads_grad, first = grad_heads, s * piece
        if late[s]:
            heads_grad, first = mirrored(grad_heads[:, :, s * piece : (s + 1) * piece]), 0
        low, *kv_parts[s] = attend_back(
            shards, orders[s], first, infos[s], queries[s], *saved[s], heads_grad, blocks[s]
        )
        query_low[s] = mirrored(low) if late[s] else low

    both = lax.psum_scatter(scattered, "shard", scatter_dimension=0, tiled=False)

    kv_low = [None] * seqs
    normed_parts = []
    gain_one_grad = jnp.zeros((width,), f32)
    shift_one_grad = jnp.zeros((width,), f32)
    for s in range(seqs):
        kv_low[s] = returned(*kv_parts[s], aparts[s], orders[s], late[s])
        part = dot(query_low[s], q_weight, ((1,), (1,))) + dot(kv_low[s], kv_weight, ((1,), (1,)))
        gain_one_grad = gain_one_grad + jnp.sum(part * group_norms[s], axis=0)
        shift_one_grad = shift_one_grad + jnp.sum(part, axis=0)
        normed_parts.append(part.astype(bf16).reshape(shards, piece, width))
    fc_add_part = jnp.sum(grad_pre.astype(f32), axis=0).reshape(shards, 1, half_hidden)
    fc_add_part = jnp.where(jnp.arange(2)[None, :, None] == odd, fc_add_part, 0.0)

    def all_heads(vector):
        return lax.dynamic_update_slice_in_dim(
            jnp.zeros((padded,), f32), vector, shard_at * group, 0
        )[:width]

    query_sum = sum(jnp.sum(low.astype(f32), axis=0) for low in query_low)
    value_sum = sum(jnp.sum(low[:, group:].astype(f32), axis=0) for low in kv_low)
    vectors = jnp.stack(
        [
            gain_one_grad,
            shift_one_grad,
            all_heads(query_sum),
            all_heads(value_sum),
            jnp.sum(grad_branch.astype(f32), axis=0),
            gain_two_grad,
            shift_two_grad,
            jnp.sum(grads32, axis=0),
        ]
    )
    vectors = jnp.concatenate(
        [
            vectors.reshape(8, shards, local_width).transpose(1, 0, 2),
            fc_add_part.reshape(shards, -1, local_width),
        ],
        axis=1,
    ).astype(bf16)
    normed_parts = jnp.concatenate(
        normed_parts
        + [jnp.pad(vectors, ((0, 0), (0, 16 - vector_rows), (0, width - local_width)))],
        axis=1,
    )
    summed = lax.psum_scatter(normed_parts, "shard", scatter_dimension=0, tiled=False).astype(f32)
    pull = jax.vjp(lambda v: normalized(v) * gain_one, inputs32)[1]
    input_grad = (grad_middle + pull(summed[:tokens])[0]).astype(bf16)
    sums = summed[tokens : tokens + vector_rows, :local_width]
    for bit in range(cycle.bit_length() - 1):
        sums = sums + swapped(sums, bit)

    cut = both.shape[0] - quarter
    out_grad = summed_over_chips(both[cut:], [bit for bit in chip_bits if bit != OUT_BIT])
    out_grad = jnp.concatenate(joined(out_grad.astype(bf16), OUT_BIT, out_side))
    out_grad = jnp.concatenate(pair_joined(out_grad, odd)).astype(f32)
    rest = summed_over_chips(both[:cut], [bit for bit in chip_bits if bit != FC_BIT])
    first, second = joined(rest.astype(bf16), FC_BIT, fc_side)
    proj_grad = jnp.concatenate([first[local_width:], second[local_width:]])
    proj_grad = jnp.concatenate(pair_joined(proj_grad, odd)).astype(f32)
    fc_grad = jnp.concatenate([first[:local_width], second[:local_width]], axis=1)
    fc_halves = pair_joined(fc_grad, odd)
    fc_grad = jnp.concatenate(
        [
            fc_halves[h][:, z * half_hidden : (z + 1) * half_hidden]
            for z in range(shards)
            for h in range(2)
        ],
        axis=1,
    ).astype(f32)

    grad = []
    for s in range(seqs):
        normed = after(normed_one[s], normed_parts)
        low = jnp.concatenate([query_low[s], kv_low[s]], axis=1)
        grad.append(dot(normed, low, flat))
    grad = sum(grad).astype(bf16).reshape(shards, 2, half_width, -1)
    mine, sent = parted(grad[:, 0], grad[:, 1], odd)
    grad = lax.all_to_all(added(mine, swapped(sent, 0)), "shard", 0, 0, tiled=True)
    grad = jnp.concatenate([grad[z] for z in range(shards)], axis=1)
    grad = jnp.concatenate(pair_joined(summed_over_chips(grad, chip_bits), odd))
    thirds = [
        jnp.concatenate(
            [
                grad[:, (3 * z + third) * group : (3 * z + third + 1) * group]
                for z in range(shards)
            ],
            axis=1,
        )[:, :width]
        for third in range(3)
    ]
    qkv_grad = jnp.concatenate(thirds, axis=1)

    return (
        layer_output.reshape(seqs, piece, width),
        input_grad.reshape(seqs, piece, width),
        sums[0],
        sums[1],
        qkv_grad,
        sums[2],
        sums[3],
        proj_grad,
        sums[4],
        sums[5],
        sums[6],
        fc_grad,
        sums[8:].reshape(-1),
        out_grad,
        sums[7],
    )


def solution(mesh):
    tokens = P(None, ("ctx", "shard"), None)
    vector = P("shard")
    matrix = P("shard", None)
    return jax.shard_map(
        body,
        mesh=mesh,
        in_specs=(
            tokens,
            vector,
            vector,
            matrix,
            vector,
            vector,
            matrix,
            vector,
            vector,
            vector,
            matrix,
            vector,
            matrix,
            vector,
            tokens,
        ),
        out_specs=(
            tokens,
            tokens,
            vector,
            vector,
            matrix,
            vector,
            vector,
            matrix,
            vector,
            vector,
            vector,
            matrix,
            vector,
            matrix,
            vector,
        ),
        check_vma=False,
    )
```

```python
import functools

import jax
import jax.numpy as jnp
from jax import lax
from jax.experimental import pallas as pl
from jax.experimental.pallas import tpu as pltpu
from jax.sharding import PartitionSpec as P

HEADS = 12
HEAD = 64
TILE = 512
EXP2_SCALE = 0.125 * 1.4426950408889634
f32 = jnp.float32
bf16 = jnp.bfloat16
FC_BIT = 1
OUT_BIT = 2
VMEM_LIMIT = 56 * 1024 * 1024


def normalized(values):
    centered = values - jnp.mean(values, axis=-1, keepdims=True)
    variance = jnp.mean(centered * centered, axis=-1, keepdims=True)
    return centered * lax.rsqrt(variance + 1e-05)


def layer_norm(values, gain, shift):
    return normalized(values) * gain + shift


def gelu_tanh(values):
    return jax.nn.gelu(values, approximate=True)


def swapped(block, bit):
    n = lax.axis_size("ctx")
    return lax.ppermute(block, "ctx", [(i, i ^ (1 << bit)) for i in range(n)])


def tree_pairs(aparts, bit, later, late, back):
    n = lax.axis_size("ctx")
    reach = [0]
    for other in later:
        reach += [r ^ (1 << other) for r in reach]
    pairs = []
    for i in range(n):
        target = i ^ (1 << bit)
        queries = [n - 1 - (target ^ r) if late else target ^ r for r in reach]
        if any(i ^ apart <= max(queries) for apart in aparts):
            pairs.append((target, i) if back else (i, target))
    return pairs


def spread(own, order, late, before, beside):
    held, aparts = own[None], [0]
    for bit in order[:-2]:
        pairs = tree_pairs(aparts, bit, order[order.index(bit) + 1 :], late, False)
        held = jnp.concatenate([held, lax.ppermute(held, "ctx", pairs)])
        aparts = aparts + [apart ^ (1 << bit) for apart in aparts]
    bit = order[-2]
    held = after(held, *before)
    received = lax.ppermute(held, "ctx", tree_pairs(aparts, bit, order[-1:], late, False))
    aparts = aparts + [apart ^ (1 << bit) for apart in aparts]
    received = after(received, *beside)
    blocks = [held, received, swapped(held, 0), swapped(received, 0)]
    return blocks, aparts + [apart ^ 1 for apart in aparts]


def added(first, second):
    return (first.astype(f32) + second.astype(f32)).astype(bf16)


def returned(near, middle, far, aparts, order, late, before):
    received = swapped(far, 0)
    count = near.shape[0]
    middle = after(added(middle, received[count:]), *before)
    pairs = tree_pairs(aparts[:count], order[-2], order[-1:], late, True)
    near = added(added(near, received[:count]), lax.ppermute(middle, "ctx", pairs))
    for bit in order[:-2][::-1]:
        count = near.shape[0] // 2
        pairs = tree_pairs(aparts[:count], bit, order[order.index(bit) + 1 :], late, True)
        near = added(near[:count], lax.ppermute(near[count:], "ctx", pairs))
    return near[0]


def after(value, *others):
    return lax.optimization_barrier((value,) + others)[0]


def mirrored(block):
    n = lax.axis_size("ctx")
    return lax.ppermute(block, "ctx", [(i, n - 1 - i) for i in range(n)])


def shifted(block, distance):
    n = lax.axis_size("shard")
    return lax.ppermute(block, "shard", [(i, (i + distance) % n) for i in range(n)])


def dot(a, b, contract):
    return lax.dot_general(a, b, ((contract[0], contract[1]), ((), ())), preferred_element_type=f32)


def summed_over_chips(part, bits):
    for bit in bits:
        low = part.astype(bf16)
        part = low.astype(f32) + swapped(low, bit).astype(f32)
    return part


def joined(half, bit, side):
    other = swapped(half, bit)
    return jnp.where(side, other, half), jnp.where(side, half, other)


def pair_joined(half, odd):
    return joined(half, 0, odd)


def load_blocks(refs, held, sems):
    each = refs[0].shape[0]
    copies = [
        pltpu.make_async_copy(ref, held.at[pl.ds(i * each, each)], sems.at[i])
        for i, ref in enumerate(refs)
    ]
    for copy in copies:
        copy.start()
    return copies


def slot_of(place, here, order):
    apart = place ^ here
    return sum(((apart >> bit) & 1) << k for k, bit in enumerate(order))


def forward_kernel(heads, shards, order, info, q_ref, *refs):
    kv_refs = refs[:4]
    att_ref, out_ref, lse_ref, held, sems, m_ref, l_ref, acc_ref = refs[4:]
    rows, width = q_ref.shape
    piece = rows // shards
    tile = min(TILE, rows)
    per = rows // tile
    copies = load_blocks(kv_refs, held, sems)
    key_places = lax.broadcasted_iota(jnp.int32, (rows, 1), 0)
    query_places = lax.broadcasted_iota(jnp.int32, (1, rows), 1)
    for copy in copies:
        copy.wait()
    for part in range(per):
        span = slice(part * tile, (part + 1) * tile)

        def step(slot, key_part, masked, start):
            keys_at = slice(key_part * tile, (key_part + 1) * tile)
            allowed = key_places[keys_at] <= query_places[:, span] if masked else None
            for h in range(heads):
                lanes = slice(h * HEAD, (h + 1) * HEAD)
                lanes_v = slice(width + h * HEAD, width + (h + 1) * HEAD)
                q = q_ref[span, lanes]
                k = held[slot, keys_at, lanes]
                v = held[slot, keys_at, lanes_v]
                s = dot(k, q, ((1,), (1,))) * EXP2_SCALE
                if masked:
                    s = jnp.where(allowed, s, -1e30)
                m = jnp.max(s, axis=0, keepdims=True)
                if start:
                    p = jnp.exp2(s - m)
                    l_ref[h] = jnp.sum(p, axis=0, keepdims=True)
                    acc_ref[h] = dot(v, p.astype(bf16), ((0,), (0,)))
                else:
                    old = m_ref[h]
                    m = jnp.maximum(old, m)
                    p = jnp.exp2(s - m)
                    factor = jnp.exp2(old - m)
                    l_ref[h] = l_ref[h] * factor + jnp.sum(p, axis=0, keepdims=True)
                    acc_ref[h] = acc_ref[h] * factor + dot(v, p.astype(bf16), ((0,), (0,)))
                m_ref[h] = m

        for key_part in range(per):
            step(slot_of(info[0], info[1], order), key_part, True, key_part == 0)

        @pl.loop(0, info[0])
        def _(j):
            for key_part in range(per):
                step(slot_of(j, info[1], order), key_part, False, False)

        for h in range(heads):
            total = l_ref[h]
            done = acc_ref[h] / total
            out_ref[h * HEAD : (h + 1) * HEAD, span] = done
            lse_ref[h, :, span] = m_ref[h] + jnp.log2(total)
            low = done.astype(bf16)
            for z in range(tile // piece):
                att_ref[part * (tile // piece) + z, h * HEAD : (h + 1) * HEAD, :] = low[
                    :, z * piece : (z + 1) * piece
                ]


def backward_kernel(heads, shards, order, first, info, q_ref, out_ref, lse_ref, go_ref, *refs):
    kv_refs = refs[:4]
    dq_ref, near_ref, middle_ref, far_ref, held, sums, sems, end_sems, acc_ref = refs[4:]
    count = held.shape[0]
    rows, width = q_ref.shape
    piece = rows // shards
    tile = min(TILE, rows)
    per = rows // tile
    copies = load_blocks(kv_refs, held, sems)
    key_places = lax.broadcasted_iota(jnp.int32, (rows, 1), 0)
    query_places = lax.broadcasted_iota(jnp.int32, (1, rows), 1)

    @pl.loop(info[0] + 1, count)
    def _(j):
        sums[slot_of(j, info[1], order)] = jnp.zeros((rows, 2 * width), bf16)

    for copy in copies:
        copy.wait()
    for part in range(per):
        span = slice(part * tile, (part + 1) * tile)
        pieces = range(part * (tile // piece), (part + 1) * (tile // piece))
        go_all = jnp.concatenate(
            [go_ref[z, :, first : first + piece] for z in pieces], axis=1
        )
        deltas = []
        for h in range(heads):
            lanes = slice(h * HEAD, (h + 1) * HEAD)
            deltas.append(
                jnp.sum(go_all[lanes].astype(f32) * out_ref[lanes, span], axis=0, keepdims=True)
            )

        def step(slot, key_part, masked, start):
            keys_at = slice(key_part * tile, (key_part + 1) * tile)
            allowed = key_places[keys_at] <= query_places[:, span] if masked else None
            for h in range(heads):
                lanes = slice(h * HEAD, (h + 1) * HEAD)
                lanes_v = slice(width + h * HEAD, width + (h + 1) * HEAD)
                q = q_ref[span, lanes]
                go = go_all[lanes]
                k = held[slot, keys_at, lanes]
                v = held[slot, keys_at, lanes_v]
                p = jnp.exp2(dot(k, q, ((1,), (1,))) * EXP2_SCALE - lse_ref[h, :, span])
                if masked:
                    p = jnp.where(allowed, p, 0.0)
                pulled = dot(v, go, ((1,), (0,)))
                slopes = (p * (pulled - deltas[h])).astype(bf16)
                dv = dot(p.astype(bf16), go, ((1,), (1,)))
                dk = dot(slopes, q, ((1,), (0,))) * 0.125
                if part:
                    dk = dk + sums[slot, keys_at, lanes].astype(f32)
                    dv = dv + sums[slot, keys_at, lanes_v].astype(f32)
                sums[slot, keys_at, lanes] = dk.astype(bf16)
                sums[slot, keys_at, lanes_v] = dv.astype(bf16)
                dq = dot(k, slopes, ((0,), (0,)))
                if start:
                    acc_ref[h] = dq
                else:
                    acc_ref[h] += dq

        for key_part in range(per):
            step(slot_of(info[0], info[1], order), key_part, True, key_part == 0)

        @pl.loop(0, info[0])
        def _(j):
            for key_part in range(per):
                step(slot_of(j, info[1], order), key_part, False, False)

        for h in range(heads):
            dq_ref[span, h * HEAD : (h + 1) * HEAD] = (acc_ref[h] * 0.125).T.astype(bf16)
    copies = []
    base = 0
    for i, ref in enumerate((near_ref, middle_ref, far_ref)):
        copies.append(
            pltpu.make_async_copy(sums.at[pl.ds(base, ref.shape[0])], ref, end_sems.at[i])
        )
        base += ref.shape[0]
    for copy in copies:
        copy.start()
    for copy in copies:
        copy.wait()


SMEM = pl.BlockSpec(memory_space=pltpu.SMEM)
VMEM = pl.BlockSpec(memory_space=pltpu.VMEM)
ANY = pl.BlockSpec(memory_space=pl.ANY)


def attend(shards, order, info, queries, blocks):
    rows, width = queries.shape
    heads = width // HEAD
    count = 4 * blocks[0].shape[0]
    tile = min(TILE, rows)
    scores = heads * rows * rows * (count + 1) // 2
    return pl.pallas_call(
        functools.partial(forward_kernel, heads, shards, order),
        out_shape=(
            jax.ShapeDtypeStruct((shards, width, rows // shards), bf16),
            jax.ShapeDtypeStruct((width, rows), f32),
            jax.ShapeDtypeStruct((heads, 1, rows), f32),
        ),
        in_specs=[SMEM, VMEM] + [ANY] * 4,
        out_specs=(VMEM, VMEM, VMEM),
        scratch_shapes=[
            pltpu.VMEM((count, rows, 2 * width), bf16),
            pltpu.SemaphoreType.DMA((4,)),
            pltpu.VMEM((heads, 1, tile), f32),
            pltpu.VMEM((heads, 1, tile), f32),
            pltpu.VMEM((heads, HEAD, tile), f32),
        ],
        compiler_params=pltpu.CompilerParams(vmem_limit_bytes=VMEM_LIMIT),
        cost_estimate=pl.CostEstimate(
            flops=scores * 16 * HEAD,
            bytes_accessed=4 * rows * width * (count + 2),
            transcendentals=scores,
        ),
        name="attention_forward",
    )(info, queries, *blocks)


def attend_back(shards, order, first, info, queries, out, lse, grads, blocks):
    rows, width = queries.shape
    heads = width // HEAD
    count = 4 * blocks[0].shape[0]
    tile = min(TILE, rows)
    scores = heads * rows * rows * (count + 1) // 2
    return pl.pallas_call(
        functools.partial(backward_kernel, heads, shards, order, first),
        out_shape=[jax.ShapeDtypeStruct((rows, width), bf16)]
        + [
            jax.ShapeDtypeStruct((share, rows, 2 * width), bf16)
            for share in (count // 4, count // 4, count // 2)
        ],
        in_specs=[SMEM] + [VMEM] * 4 + [ANY] * 4,
        out_specs=[VMEM] + [ANY] * 3,
        scratch_shapes=[
            pltpu.VMEM((count, rows, 2 * width), bf16),
            pltpu.VMEM((count, rows, 2 * width), bf16),
            pltpu.SemaphoreType.DMA((4,)),
            pltpu.SemaphoreType.DMA((3,)),
            pltpu.VMEM((heads, HEAD, tile), f32),
        ],
        compiler_params=pltpu.CompilerParams(vmem_limit_bytes=VMEM_LIMIT),
        cost_estimate=pl.CostEstimate(
            flops=scores * 10 * HEAD,
            bytes_accessed=8 * rows * width * (count + 2),
            transcendentals=scores,
        ),
        name="attention_backward",
    )(info, queries, out, lse, grads, *blocks)


def body(
    layer_input,
    attn_gain,
    attn_shift,
    qkv_weight,
    query_bias,
    value_bias,
    proj_weight,
    proj_bias,
    mlp_gain,
    mlp_shift,
    fc_weight,
    fc_bias,
    out_weight,
    out_bias,
    grad_output,
):
    seqs, piece, width = layer_input.shape
    cycle = lax.axis_size("ctx")
    shards = lax.axis_size("shard")
    here = lax.axis_index("ctx")
    shard_at = lax.axis_index("shard")
    odd = here & 1
    chip_bits = list(range(1, cycle.bit_length() - 1))
    rows = shards * piece
    local_width = qkv_weight.shape[0]
    local_hidden = out_weight.shape[0]
    half_width = local_width // 2
    half_hidden = local_hidden // 2
    quarter = half_hidden // 2
    group = -(-HEADS // shards) * HEAD
    padded = group * shards
    late = [seq >= (seqs + 1) // 2 for seq in range(seqs)]
    tokens = seqs * piece

    gathered = lax.all_gather(layer_input, "shard", axis=0)

    def by_heads(weight):
        parts = []
        for third in range(3):
            part = weight[:, third * width : (third + 1) * width]
            parts.append(jnp.pad(part, ((0, 0), (0, padded - width))))
        return jnp.stack(
            [
                jnp.concatenate([part[:, z * group : (z + 1) * group] for part in parts], axis=1)
                for z in range(shards)
            ]
        )

    joins = chip_bits[::-1] + [0]
    share = local_width // cycle
    weight_share = lax.dynamic_slice_in_dim(
        qkv_weight, sum(((here >> bit) & 1) << k for k, bit in enumerate(joins)) * share, share, 0
    )
    packed = jnp.concatenate(
        [
            jnp.stack(
                [attn_gain, attn_shift, query_bias, value_bias, proj_bias, mlp_gain, mlp_shift, out_bias]
            ),
            fc_bias.reshape(-1, local_width),
        ]
    )
    vector_rows = packed.shape[0]
    packed = jnp.pad(packed, ((0, 16 - vector_rows), (0, 3 * group - local_width)))
    moved = lax.all_to_all(
        jnp.concatenate(
            [by_heads(weight_share), jnp.broadcast_to(packed, (shards,) + packed.shape)], axis=1
        ),
        "shard",
        0,
        0,
        tiled=True,
    )
    small = moved[:, share : share + vector_rows, :local_width].astype(f32)
    qkv_own = moved[:, :share]
    for bit in joins:
        if bit == 0:
            qkv_own = after(qkv_own, gathered)
        qkv_own = jnp.concatenate(joined(qkv_own, bit, (here >> bit) & 1), axis=1)
    qkv_own = qkv_own.reshape(width, 3 * group)
    q_weight = qkv_own[:, :group]
    kv_weight = qkv_own[:, group:]

    vectors = [small[:, i].reshape(-1) for i in range(8)]
    gain_one, shift_one, query_add, value_add, proj_add, gain_two, shift_two, out_add = vectors
    bias_rows = half_hidden // local_width
    fc_add = lax.dynamic_slice_in_dim(small, 8 + odd * bias_rows, bias_rows, 1).reshape(-1)

    def own_heads(vector):
        return lax.dynamic_slice_in_dim(
            jnp.pad(vector, (0, padded - width)), shard_at * group, group, 0
        )

    kv_add = jnp.concatenate([jnp.zeros((group,), f32), own_heads(value_add)])
    query_add = own_heads(query_add)

    fc_side = (here >> FC_BIT) & 1
    out_side = (here >> OUT_BIT) & 1
    proj_half = lax.dynamic_slice_in_dim(proj_weight, odd * half_width, half_width, 0)
    fc_quarter = jnp.concatenate(
        [
            lax.dynamic_slice_in_dim(
                fc_weight,
                (fc_side * (shards // 2) + z) * local_hidden + odd * half_hidden,
                half_hidden,
                1,
            )
            for z in range(shards // 2)
        ],
        axis=1,
    )
    out_quarter = lax.dynamic_slice_in_dim(
        out_weight, odd * half_hidden + out_side * quarter, quarter, 0
    )
    weights = lax.all_gather(
        jnp.concatenate([proj_half, fc_quarter, out_quarter]), "shard", axis=0
    )

    orders = [chip_bits + [0], chip_bits[::-1] + [0]]
    orders = [orders[s % 2] for s in range(seqs)]
    group_norms, normed_one, own_blocks, queries, infos = [], [], [], [], []
    for s in range(seqs):
        norm = normalized(gathered[:, s].reshape(rows, width).astype(f32))
        normed = (norm * gain_one + shift_one).astype(bf16)
        group_norms.append(norm)
        normed_one.append(normed)
        own_blocks.append((dot(normed, kv_weight, ((1,), (0,))) + kv_add).astype(bf16))
        queries.append((dot(normed, q_weight, ((1,), (0,))) + query_add).astype(bf16))
        infos.append(jnp.stack([cycle - 1 - here if late[s] else here, here]).astype(jnp.int32))
    moved = [mirrored(queries[s]) if late[s] else queries[s] for s in range(seqs)]
    spreads = [spread(own_blocks[s], orders[s], late[s], queries, moved) for s in range(seqs)]
    queries = moved
    blocks = [blocks for blocks, _ in spreads]
    aparts = [apart for _, apart in spreads]
    saved = [None] * seqs
    attended_parts = [None] * seqs
    for s in reversed(range(seqs)):
        attended_parts[s], *saved[s] = attend(shards, orders[s], infos[s], queries[s], blocks[s])
    attended_parts = lax.optimization_barrier(tuple(attended_parts))
    attended_parts = [
        mirrored(part) if late[s] else part for s, part in enumerate(attended_parts)
    ]
    attended, weights = lax.optimization_barrier(
        (jnp.concatenate(attended_parts, axis=2), weights)
    )
    proj_half = pair_joined(weights[:, :half_width], odd)
    proj_full = jnp.stack(proj_half, axis=1).reshape(width, width)
    fc_quarter = weights[:, half_width : half_width + local_width].reshape(width, -1)
    fc_half = jnp.concatenate(joined(fc_quarter, FC_BIT, fc_side), axis=1)
    out_half = jnp.stack(
        joined(weights[:, half_width + local_width :], OUT_BIT, out_side), axis=1
    ).reshape(-1, width)
    attended = lax.all_to_all(attended, "shard", 0, 0, tiled=True).reshape(padded, tokens)[:width]

    inputs32 = layer_input.reshape(tokens, width).astype(f32)
    grads_own = grad_output.reshape(tokens, width)
    grads32 = grads_own.astype(f32)
    middle = inputs32 + dot(attended, proj_full, ((0,), (0,))) + proj_add
    normed_two = layer_norm(middle, gain_two, shift_two).astype(bf16)

    normed_pair = jnp.concatenate([normed_two, swapped(normed_two, 0)])
    grads_pair = jnp.concatenate([grads_own, swapped(grads_own, 0)])
    preactivation = dot(normed_pair, fc_half, ((1,), (0,))) + fc_add
    hidden = gelu_tanh(preactivation).astype(bf16)
    out_part = dot(hidden, out_half, ((1,), (0,)))
    layer_output = middle + (out_part[:tokens] + swapped(out_part[tokens:], 0)) + out_add
    layer_output = layer_output.astype(bf16)
    grad_hidden = dot(grads_pair, out_half, ((1,), (1,)))
    grad_pre = jax.vjp(gelu_tanh, preactivation)[1](grad_hidden)[0].astype(bf16)
    normed_part = dot(grad_pre, fc_half, ((1,), (1,)))
    grad_normed_two = normed_part[:tokens] + swapped(normed_part[tokens:], 0)
    grad_mid_part, gain_two_grad, shift_two_grad = jax.vjp(
        layer_norm, middle, gain_two, shift_two
    )[1](grad_normed_two)
    grad_middle = grads32 + grad_mid_part
    grad_branch = grad_middle.astype(bf16)

    grad_attended = jnp.pad(
        dot(proj_full, grad_branch, ((1,), (1,))).astype(bf16), ((0, padded - width), (0, 0))
    ).reshape(shards, group, tokens)
    grad_heads = lax.all_to_all(grad_attended, "shard", 0, 0, tiled=True)
    flat = ((0,), (0,))

    def parted(first, second, side):
        return jnp.where(side, second, first), jnp.where(side, first, second)

    proj_grad = dot(attended, grad_branch, ((1,), (0,))).astype(bf16)
    proj_grad = proj_grad.reshape(shards, 2, half_width, width)
    mine, sent = parted(proj_grad[:, 0], proj_grad[:, 1], odd)
    proj_grad = added(mine, swapped(sent, 0))
    fc_grad = dot(normed_pair, grad_pre, flat).astype(bf16).reshape(shards, local_width, -1)
    column = fc_grad.shape[2] // 2
    fc_mine, fc_sent = parted(
        jnp.concatenate([fc_grad[..., :column], proj_grad[:, : half_width // 2]], axis=1),
        jnp.concatenate([fc_grad[..., column:], proj_grad[:, half_width // 2 :]], axis=1),
        fc_side,
    )
    out_grad = dot(hidden, grads_pair, flat).astype(bf16).reshape(shards, 2, quarter, width)
    out_mine, out_sent = parted(out_grad[:, 0], out_grad[:, 1], out_side)
    fc_received = swapped(fc_sent, FC_BIT)
    out_received = swapped(out_sent, OUT_BIT)

    query_low = [None] * seqs
    kv_parts = [None] * seqs
    grad_heads = after(grad_heads, fc_sent, out_sent)
    for s in range(seqs):
        heads_grad, first = grad_heads, s * piece
        if late[s]:
            heads_grad, first = mirrored(grad_heads[:, :, s * piece : (s + 1) * piece]), 0
        low, *kv_parts[s] = attend_back(
            shards, orders[s], first, infos[s], queries[s], *saved[s], heads_grad, blocks[s]
        )
        query_low[s] = low

    ended = [parts[0] for parts in kv_parts]
    query_low = [
        mirrored(after(low, *ended)) if late[s] else low for s, low in enumerate(query_low)
    ]
    scattered = jnp.concatenate(
        [added(fc_mine, after(fc_received, *ended)), added(out_mine, after(out_received, *ended))],
        axis=1,
    )
    both = lax.psum_scatter(scattered, "shard", scatter_dimension=0, tiled=False)

    kv_low = [None] * seqs
    normed_parts = []
    gain_one_grad = jnp.zeros((width,), f32)
    shift_one_grad = jnp.zeros((width,), f32)
    for s in range(seqs):
        kv_low[s] = returned(*kv_parts[s], aparts[s], orders[s], late[s], query_low + [scattered])
        part = dot(query_low[s], q_weight, ((1,), (1,))) + dot(kv_low[s], kv_weight, ((1,), (1,)))
        gain_one_grad = gain_one_grad + jnp.sum(part * group_norms[s], axis=0)
        shift_one_grad = shift_one_grad + jnp.sum(part, axis=0)
        normed_parts.append(part.astype(bf16).reshape(shards, piece, width))
    fc_add_part = jnp.sum(grad_pre.astype(f32), axis=0).reshape(shards, 1, half_hidden)
    fc_add_part = jnp.where(jnp.arange(2)[None, :, None] == odd, fc_add_part, 0.0)

    def all_heads(vector):
        return lax.dynamic_update_slice_in_dim(
            jnp.zeros((padded,), f32), vector, shard_at * group, 0
        )[:width]

    query_sum = sum(jnp.sum(low.astype(f32), axis=0) for low in query_low)
    value_sum = sum(jnp.sum(low[:, group:].astype(f32), axis=0) for low in kv_low)
    vectors = jnp.stack(
        [
            gain_one_grad,
            shift_one_grad,
            all_heads(query_sum),
            all_heads(value_sum),
            jnp.sum(grad_branch.astype(f32), axis=0),
            gain_two_grad,
            shift_two_grad,
            jnp.sum(grads32, axis=0),
        ]
    )
    vectors = jnp.concatenate(
        [
            vectors.reshape(8, shards, local_width).transpose(1, 0, 2),
            fc_add_part.reshape(shards, -1, local_width),
        ],
        axis=1,
    ).astype(bf16)
    normed_parts = jnp.concatenate(
        normed_parts
        + [jnp.pad(vectors, ((0, 0), (0, 16 - vector_rows), (0, width - local_width)))],
        axis=1,
    )
    normed_parts = after(normed_parts, both)
    summed = lax.psum_scatter(normed_parts, "shard", scatter_dimension=0, tiled=False).astype(f32)
    pull = jax.vjp(lambda v: normalized(v) * gain_one, inputs32)[1]
    input_grad = (grad_middle + pull(summed[:tokens])[0]).astype(bf16)
    sums = summed[tokens : tokens + vector_rows, :local_width]
    for bit in range(cycle.bit_length() - 1):
        sums = sums + swapped(sums, bit)

    cut = both.shape[0] - quarter
    out_grad = summed_over_chips(both[cut:], [bit for bit in chip_bits if bit != OUT_BIT])
    out_grad = jnp.concatenate(joined(out_grad.astype(bf16), OUT_BIT, out_side))
    out_grad = jnp.concatenate(pair_joined(out_grad, odd)).astype(f32)
    rest = summed_over_chips(both[:cut], [bit for bit in chip_bits if bit != FC_BIT])
    first, second = joined(rest.astype(bf16), FC_BIT, fc_side)
    proj_grad = jnp.concatenate([first[local_width:], second[local_width:]])
    proj_grad = jnp.concatenate(pair_joined(proj_grad, odd)).astype(f32)
    fc_grad = jnp.concatenate([first[:local_width], second[:local_width]], axis=1)
    fc_halves = pair_joined(fc_grad, odd)
    fc_grad = jnp.concatenate(
        [
            fc_halves[h][:, z * half_hidden : (z + 1) * half_hidden]
            for z in range(shards)
            for h in range(2)
        ],
        axis=1,
    ).astype(f32)

    grad = []
    for s in range(seqs):
        normed = after(normed_one[s], normed_parts)
        low = jnp.concatenate([query_low[s], kv_low[s]], axis=1)
        grad.append(dot(normed, low, flat))
    grad = sum(grad).astype(bf16).reshape(shards, local_width, -1)
    for bit in joins[::-1]:
        cut = grad.shape[1] // 2
        mine, sent = parted(grad[:, :cut], grad[:, cut:], (here >> bit) & 1)
        grad = added(mine, swapped(sent, bit))
    grad = lax.all_to_all(grad, "shard", 0, 0, tiled=True)
    grad = jnp.concatenate([grad[z] for z in range(shards)], axis=1)
    for turn, bit in enumerate(joins):
        if turn == 1:
            grad = after(grad, summed)
        grad = jnp.concatenate(joined(grad, bit, (here >> bit) & 1))
    thirds = [
        jnp.concatenate(
            [
                grad[:, (3 * z + third) * group : (3 * z + third + 1) * group]
                for z in range(shards)
            ],
            axis=1,
        )[:, :width]
        for third in range(3)
    ]
    qkv_grad = jnp.concatenate(thirds, axis=1).astype(f32)

    return (
        layer_output.reshape(seqs, piece, width),
        input_grad.reshape(seqs, piece, width),
        sums[0],
        sums[1],
        qkv_grad,
        sums[2],
        sums[3],
        proj_grad,
        sums[4],
        sums[5],
        sums[6],
        fc_grad,
        sums[8:].reshape(-1),
        out_grad,
        sums[7],
    )


def solution(mesh):
    tokens = P(None, ("ctx", "shard"), None)
    vector = P("shard")
    matrix = P("shard", None)
    return jax.shard_map(
        body,
        mesh=mesh,
        in_specs=(
            tokens,
            vector,
            vector,
            matrix,
            vector,
            vector,
            matrix,
            vector,
            vector,
            vector,
            matrix,
            vector,
            matrix,
            vector,
            tokens,
        ),
        out_specs=(
            tokens,
            tokens,
            vector,
            vector,
            matrix,
            vector,
            vector,
            matrix,
            vector,
            vector,
            vector,
            matrix,
            vector,
            matrix,
            vector,
        ),
        check_vma=False,
    )
```

```python
import functools

import jax
import jax.numpy as jnp
from jax import lax
from jax.experimental import pallas as pl
from jax.experimental.pallas import tpu as pltpu
from jax.sharding import PartitionSpec as P

HEADS = 12
HEAD = 64
TILE = 512
EXP2_SCALE = 0.125 * 1.4426950408889634
f32 = jnp.float32
bf16 = jnp.bfloat16
FC_BIT = 1
OUT_BIT = 2
VMEM_LIMIT = 56 * 1024 * 1024


def normalized(values):
    centered = values - jnp.mean(values, axis=-1, keepdims=True)
    variance = jnp.mean(centered * centered, axis=-1, keepdims=True)
    return centered * lax.rsqrt(variance + 1e-05)


def layer_norm(values, gain, shift):
    return normalized(values) * gain + shift


def gelu_tanh(values):
    return jax.nn.gelu(values, approximate=True)


def swapped(block, bit):
    n = lax.axis_size("ctx")
    return lax.ppermute(block, "ctx", [(i, i ^ (1 << bit)) for i in range(n)])


def tree_pairs(aparts, bit, later, late, back):
    n = lax.axis_size("ctx")
    reach = [0]
    for other in later:
        reach += [r ^ (1 << other) for r in reach]
    place = (lambda i: n - 1 - i) if late else (lambda i: i)
    pairs = []
    for i in range(n):
        target = i ^ (1 << bit)
        if any(place(i ^ apart) <= place(target ^ r) for r in reach for apart in aparts):
            pairs.append((target, i) if back else (i, target))
    return pairs


def spread(own, order, late, before):
    held, aparts = own[None], [0]
    for bit in order[:-2]:
        pairs = tree_pairs(aparts, bit, order[order.index(bit) + 1 :], late, False)
        held = jnp.concatenate([held, lax.ppermute(held, "ctx", pairs)])
        aparts = aparts + [apart ^ (1 << bit) for apart in aparts]
    bit = order[-2]
    held = after(held, *before)
    received = lax.ppermute(held, "ctx", tree_pairs(aparts, bit, order[-1:], late, False))
    aparts = aparts + [apart ^ (1 << bit) for apart in aparts]
    blocks = [held, received, swapped(held, 0), swapped(received, 0)]
    return blocks, aparts + [apart ^ 1 for apart in aparts]


def added(first, second):
    return (first.astype(f32) + second.astype(f32)).astype(bf16)


def returned(near, middle, far, aparts, order, late, before):
    received = swapped(far, 0)
    count = near.shape[0]
    middle = after(added(middle, received[count:]), *before)
    pairs = tree_pairs(aparts[:count], order[-2], order[-1:], late, True)
    near = added(added(near, received[:count]), lax.ppermute(middle, "ctx", pairs))
    for bit in order[:-2][::-1]:
        count = near.shape[0] // 2
        pairs = tree_pairs(aparts[:count], bit, order[order.index(bit) + 1 :], late, True)
        near = added(near[:count], lax.ppermute(near[count:], "ctx", pairs))
    return near[0]


def after(value, *others):
    return lax.optimization_barrier((value,) + others)[0]


def mirrored(block):
    n = lax.axis_size("ctx")
    return lax.ppermute(block, "ctx", [(i, n - 1 - i) for i in range(n)])


def shifted(block, distance):
    n = lax.axis_size("shard")
    return lax.ppermute(block, "shard", [(i, (i + distance) % n) for i in range(n)])


def dot(a, b, contract):
    return lax.dot_general(a, b, ((contract[0], contract[1]), ((), ())), preferred_element_type=f32)


def summed_over_chips(part, bits):
    for bit in bits:
        low = part.astype(bf16)
        part = low.astype(f32) + swapped(low, bit).astype(f32)
    return part


def joined(half, bit, side):
    other = swapped(half, bit)
    return jnp.where(side, other, half), jnp.where(side, half, other)


def pair_joined(half, odd):
    return joined(half, 0, odd)


def load_blocks(refs, held, sems):
    each = refs[0].shape[0]
    copies = [
        pltpu.make_async_copy(ref, held.at[pl.ds(i * each, each)], sems.at[i])
        for i, ref in enumerate(refs)
    ]
    for copy in copies:
        copy.start()
    return copies


def slot_of(place, here, order):
    apart = place ^ here
    return sum(((apart >> bit) & 1) << k for k, bit in enumerate(order))


def forward_kernel(heads, shards, order, info, q_ref, *refs):
    kv_refs = refs[:4]
    att_ref, out_ref, lse_ref, held, sems, m_ref, l_ref, acc_ref = refs[4:]
    rows, width = q_ref.shape
    piece = rows // shards
    tile = min(TILE, rows)
    per = rows // tile
    copies = load_blocks(kv_refs, held, sems)
    key_places = lax.broadcasted_iota(jnp.int32, (rows, 1), 0)
    query_places = lax.broadcasted_iota(jnp.int32, (1, rows), 1)
    for copy in copies:
        copy.wait()
    for part in range(per):
        span = slice(part * tile, (part + 1) * tile)

        def step(slot, key_part, masked, start):
            keys_at = slice(key_part * tile, (key_part + 1) * tile)
            allowed = key_places[keys_at] <= query_places[:, span] if masked else None
            for h in range(heads):
                lanes = slice(h * HEAD, (h + 1) * HEAD)
                lanes_v = slice(width + h * HEAD, width + (h + 1) * HEAD)
                q = q_ref[span, lanes]
                k = held[slot, keys_at, lanes]
                v = held[slot, keys_at, lanes_v]
                s = dot(k, q, ((1,), (1,))) * EXP2_SCALE
                if masked:
                    s = jnp.where(allowed, s, -1e30)
                m = jnp.max(s, axis=0, keepdims=True)
                if start:
                    p = jnp.exp2(s - m)
                    l_ref[h] = jnp.sum(p, axis=0, keepdims=True)
                    acc_ref[h] = dot(v, p.astype(bf16), ((0,), (0,)))
                else:
                    old = m_ref[h]
                    m = jnp.maximum(old, m)
                    p = jnp.exp2(s - m)
                    factor = jnp.exp2(old - m)
                    l_ref[h] = l_ref[h] * factor + jnp.sum(p, axis=0, keepdims=True)
                    acc_ref[h] = acc_ref[h] * factor + dot(v, p.astype(bf16), ((0,), (0,)))
                m_ref[h] = m

        for key_part in range(per):
            step(slot_of(info[0], info[0], order), key_part, True, key_part == 0)

        @pl.loop(0, info[0])
        def _(j):
            for key_part in range(per):
                step(slot_of(j, info[0], order), key_part, False, False)

        for h in range(heads):
            total = l_ref[h]
            done = acc_ref[h] / total
            out_ref[h * HEAD : (h + 1) * HEAD, span] = done
            lse_ref[h, :, span] = m_ref[h] + jnp.log2(total)
            low = done.astype(bf16)
            for z in range(tile // piece):
                att_ref[part * (tile // piece) + z, h * HEAD : (h + 1) * HEAD, :] = low[
                    :, z * piece : (z + 1) * piece
                ]


def backward_kernel(heads, shards, order, first, info, q_ref, out_ref, lse_ref, go_ref, *refs):
    kv_refs = refs[:4]
    dq_ref, near_ref, middle_ref, far_ref, held, sums, sems, end_sems, acc_ref = refs[4:]
    count = held.shape[0]
    rows, width = q_ref.shape
    piece = rows // shards
    tile = min(TILE, rows)
    per = rows // tile
    copies = load_blocks(kv_refs, held, sems)
    key_places = lax.broadcasted_iota(jnp.int32, (rows, 1), 0)
    query_places = lax.broadcasted_iota(jnp.int32, (1, rows), 1)

    @pl.loop(info[0] + 1, count)
    def _(j):
        sums[slot_of(j, info[0], order)] = jnp.zeros((rows, 2 * width), bf16)

    for copy in copies:
        copy.wait()
    for part in range(per):
        span = slice(part * tile, (part + 1) * tile)
        pieces = range(part * (tile // piece), (part + 1) * (tile // piece))
        go_all = jnp.concatenate(
            [go_ref[z, :, first : first + piece] for z in pieces], axis=1
        )
        deltas = []
        for h in range(heads):
            lanes = slice(h * HEAD, (h + 1) * HEAD)
            deltas.append(
                jnp.sum(go_all[lanes].astype(f32) * out_ref[lanes, span], axis=0, keepdims=True)
            )

        def step(slot, key_part, masked, start):
            keys_at = slice(key_part * tile, (key_part + 1) * tile)
            allowed = key_places[keys_at] <= query_places[:, span] if masked else None
            for h in range(heads):
                lanes = slice(h * HEAD, (h + 1) * HEAD)
                lanes_v = slice(width + h * HEAD, width + (h + 1) * HEAD)
                q = q_ref[span, lanes]
                go = go_all[lanes]
                k = held[slot, keys_at, lanes]
                v = held[slot, keys_at, lanes_v]
                p = jnp.exp2(dot(k, q, ((1,), (1,))) * EXP2_SCALE - lse_ref[h, :, span])
                if masked:
                    p = jnp.where(allowed, p, 0.0)
                pulled = dot(v, go, ((1,), (0,)))
                slopes = (p * (pulled - deltas[h])).astype(bf16)
                dv = dot(p.astype(bf16), go, ((1,), (1,)))
                dk = dot(slopes, q, ((1,), (0,))) * 0.125
                if part:
                    dk = dk + sums[slot, keys_at, lanes].astype(f32)
                    dv = dv + sums[slot, keys_at, lanes_v].astype(f32)
                sums[slot, keys_at, lanes] = dk.astype(bf16)
                sums[slot, keys_at, lanes_v] = dv.astype(bf16)
                dq = dot(k, slopes, ((0,), (0,)))
                if start:
                    acc_ref[h] = dq
                else:
                    acc_ref[h] += dq

        for key_part in range(per):
            step(slot_of(info[0], info[0], order), key_part, True, key_part == 0)

        @pl.loop(0, info[0])
        def _(j):
            for key_part in range(per):
                step(slot_of(j, info[0], order), key_part, False, False)

        for h in range(heads):
            dq_ref[span, h * HEAD : (h + 1) * HEAD] = (acc_ref[h] * 0.125).T.astype(bf16)
    copies = []
    base = 0
    for i, ref in enumerate((near_ref, middle_ref, far_ref)):
        copies.append(
            pltpu.make_async_copy(sums.at[pl.ds(base, ref.shape[0])], ref, end_sems.at[i])
        )
        base += ref.shape[0]
    for copy in copies:
        copy.start()
    for copy in copies:
        copy.wait()


SMEM = pl.BlockSpec(memory_space=pltpu.SMEM)
VMEM = pl.BlockSpec(memory_space=pltpu.VMEM)
ANY = pl.BlockSpec(memory_space=pl.ANY)


def attend(shards, order, info, queries, blocks):
    rows, width = queries.shape
    heads = width // HEAD
    count = 4 * blocks[0].shape[0]
    tile = min(TILE, rows)
    scores = heads * rows * rows * (count + 1) // 2
    return pl.pallas_call(
        functools.partial(forward_kernel, heads, shards, order),
        out_shape=(
            jax.ShapeDtypeStruct((shards, width, rows // shards), bf16),
            jax.ShapeDtypeStruct((width, rows), f32),
            jax.ShapeDtypeStruct((heads, 1, rows), f32),
        ),
        in_specs=[SMEM, VMEM] + [ANY] * 4,
        out_specs=(VMEM, VMEM, VMEM),
        scratch_shapes=[
            pltpu.VMEM((count, rows, 2 * width), bf16),
            pltpu.SemaphoreType.DMA((4,)),
            pltpu.VMEM((heads, 1, tile), f32),
            pltpu.VMEM((heads, 1, tile), f32),
            pltpu.VMEM((heads, HEAD, tile), f32),
        ],
        compiler_params=pltpu.CompilerParams(vmem_limit_bytes=VMEM_LIMIT),
        cost_estimate=pl.CostEstimate(
            flops=scores * 16 * HEAD,
            bytes_accessed=4 * rows * width * (count + 2),
            transcendentals=scores,
        ),
        name="attention_forward",
    )(info, queries, *blocks)


def attend_back(shards, order, first, info, queries, out, lse, grads, blocks):
    rows, width = queries.shape
    heads = width // HEAD
    count = 4 * blocks[0].shape[0]
    tile = min(TILE, rows)
    scores = heads * rows * rows * (count + 1) // 2
    return pl.pallas_call(
        functools.partial(backward_kernel, heads, shards, order, first),
        out_shape=[jax.ShapeDtypeStruct((rows, width), bf16)]
        + [
            jax.ShapeDtypeStruct((share, rows, 2 * width), bf16)
            for share in (count // 4, count // 4, count // 2)
        ],
        in_specs=[SMEM] + [VMEM] * 4 + [ANY] * 4,
        out_specs=[VMEM] + [ANY] * 3,
        scratch_shapes=[
            pltpu.VMEM((count, rows, 2 * width), bf16),
            pltpu.VMEM((count, rows, 2 * width), bf16),
            pltpu.SemaphoreType.DMA((4,)),
            pltpu.SemaphoreType.DMA((3,)),
            pltpu.VMEM((heads, HEAD, tile), f32),
        ],
        compiler_params=pltpu.CompilerParams(vmem_limit_bytes=VMEM_LIMIT),
        cost_estimate=pl.CostEstimate(
            flops=scores * 10 * HEAD,
            bytes_accessed=8 * rows * width * (count + 2),
            transcendentals=scores,
        ),
        name="attention_backward",
    )(info, queries, out, lse, grads, *blocks)


def body(
    layer_input,
    attn_gain,
    attn_shift,
    qkv_weight,
    query_bias,
    value_bias,
    proj_weight,
    proj_bias,
    mlp_gain,
    mlp_shift,
    fc_weight,
    fc_bias,
    out_weight,
    out_bias,
    grad_output,
):
    seqs, piece, width = layer_input.shape
    cycle = lax.axis_size("ctx")
    shards = lax.axis_size("shard")
    here = lax.axis_index("ctx")
    shard_at = lax.axis_index("shard")
    odd = here & 1
    chip_bits = list(range(1, cycle.bit_length() - 1))
    rows = shards * piece
    local_width = qkv_weight.shape[0]
    local_hidden = out_weight.shape[0]
    half_width = local_width // 2
    half_hidden = local_hidden // 2
    quarter = half_hidden // 2
    group = -(-HEADS // shards) * HEAD
    padded = group * shards
    late = [seq >= (seqs + 1) // 2 for seq in range(seqs)]
    tokens = seqs * piece


    def mirror_late(held):
        return jnp.stack([mirrored(held[s]) if late[s] else held[s] for s in range(seqs)])

    layer_input = mirror_late(layer_input)
    grad_output = mirror_late(grad_output)
    gathered = lax.all_gather(layer_input, "shard", axis=0)

    def by_heads(weight):
        parts = []
        for third in range(3):
            part = weight[:, third * width : (third + 1) * width]
            parts.append(jnp.pad(part, ((0, 0), (0, padded - width))))
        return jnp.stack(
            [
                jnp.concatenate([part[:, z * group : (z + 1) * group] for part in parts], axis=1)
                for z in range(shards)
            ]
        )

    joins = chip_bits[::-1] + [0]
    share = local_width // cycle
    weight_share = lax.dynamic_slice_in_dim(
        qkv_weight, sum(((here >> bit) & 1) << k for k, bit in enumerate(joins)) * share, share, 0
    )
    packed = jnp.concatenate(
        [
            jnp.stack(
                [attn_gain, attn_shift, query_bias, value_bias, proj_bias, mlp_gain, mlp_shift, out_bias]
            ),
            fc_bias.reshape(-1, local_width),
        ]
    )
    vector_rows = packed.shape[0]
    packed = jnp.pad(packed, ((0, 16 - vector_rows), (0, 3 * group - local_width)))
    moved = lax.all_to_all(
        jnp.concatenate(
            [by_heads(weight_share), jnp.broadcast_to(packed, (shards,) + packed.shape)], axis=1
        ),
        "shard",
        0,
        0,
        tiled=True,
    )
    small = moved[:, share : share + vector_rows, :local_width].astype(f32)
    qkv_own = moved[:, :share]
    for bit in joins:
        if bit == 0:
            qkv_own, grad_output, _ = lax.optimization_barrier((qkv_own, grad_output, gathered))
        qkv_own = jnp.concatenate(joined(qkv_own, bit, (here >> bit) & 1), axis=1)
    qkv_own = qkv_own.reshape(width, 3 * group)
    q_weight = qkv_own[:, :group]
    kv_weight = qkv_own[:, group:]

    vectors = [small[:, i].reshape(-1) for i in range(8)]
    gain_one, shift_one, query_add, value_add, proj_add, gain_two, shift_two, out_add = vectors
    bias_rows = half_hidden // local_width
    fc_add = lax.dynamic_slice_in_dim(small, 8 + odd * bias_rows, bias_rows, 1).reshape(-1)

    def own_heads(vector):
        return lax.dynamic_slice_in_dim(
            jnp.pad(vector, (0, padded - width)), shard_at * group, group, 0
        )

    kv_add = jnp.concatenate([jnp.zeros((group,), f32), own_heads(value_add)])
    query_add = own_heads(query_add)

    fc_side = (here >> FC_BIT) & 1
    out_side = (here >> OUT_BIT) & 1
    proj_half = lax.dynamic_slice_in_dim(proj_weight, odd * half_width, half_width, 0)
    fc_quarter = jnp.concatenate(
        [
            lax.dynamic_slice_in_dim(
                fc_weight,
                (fc_side * (shards // 2) + z) * local_hidden + odd * half_hidden,
                half_hidden,
                1,
            )
            for z in range(shards // 2)
        ],
        axis=1,
    )
    out_quarter = lax.dynamic_slice_in_dim(
        out_weight, odd * half_hidden + out_side * quarter, quarter, 0
    )
    weights = lax.all_gather(
        jnp.concatenate([proj_half, fc_quarter, out_quarter]), "shard", axis=0
    )

    orders = [chip_bits + [0], chip_bits[::-1] + [0]]
    orders = [orders[s % 2] for s in range(seqs)]
    group_norms, normed_one, own_blocks, queries, infos = [], [], [], [], []
    for s in range(seqs):
        norm = normalized(gathered[:, s].reshape(rows, width).astype(f32))
        normed = (norm * gain_one + shift_one).astype(bf16)
        group_norms.append(norm)
        normed_one.append(normed)
        own_blocks.append((dot(normed, kv_weight, ((1,), (0,))) + kv_add).astype(bf16))
        queries.append((dot(normed, q_weight, ((1,), (0,))) + query_add).astype(bf16))
        infos.append(jnp.reshape(cycle - 1 - here if late[s] else here, (1,)).astype(jnp.int32))
    spreads = [spread(own_blocks[s], orders[s], late[s], queries) for s in range(seqs)]
    blocks = [blocks for blocks, _ in spreads]
    aparts = [apart for _, apart in spreads]
    saved = [None] * seqs
    attended_parts = [None] * seqs
    for s in reversed(range(seqs)):
        attended_parts[s], *saved[s] = attend(shards, orders[s], infos[s], queries[s], blocks[s])
    attended, weights = lax.optimization_barrier(
        (jnp.concatenate(attended_parts, axis=2), weights)
    )
    cut = half_width + local_width
    proj_half, fc_quarter, out_quarter = lax.optimization_barrier(
        (weights[:, :half_width], weights[:, half_width:cut], weights[:, cut:])
    )
    proj_half = pair_joined(proj_half, odd)
    proj_full = jnp.stack(proj_half, axis=1).reshape(width, width)
    fc_quarter = fc_quarter.reshape(width, -1)
    fc_half = jnp.concatenate(joined(fc_quarter, FC_BIT, fc_side), axis=1)
    out_half = jnp.stack(joined(out_quarter, OUT_BIT, out_side), axis=1).reshape(-1, width)
    attended = lax.all_to_all(attended, "shard", 0, 0, tiled=True).reshape(padded, tokens)[:width]

    inputs32 = layer_input.reshape(tokens, width).astype(f32)
    grads_own = grad_output.reshape(tokens, width)
    grads32 = grads_own.astype(f32)
    attended, fc_half = lax.optimization_barrier((attended, fc_half))
    middle = inputs32 + dot(attended, proj_full, ((0,), (0,))) + proj_add
    normed_two = layer_norm(middle, gain_two, shift_two).astype(bf16)

    normed_pair = jnp.concatenate([normed_two, swapped(normed_two, 0)])
    grads_pair = jnp.concatenate([grads_own, swapped(grads_own, 0)])
    preactivation = dot(normed_pair, fc_half, ((1,), (0,))) + fc_add
    hidden = gelu_tanh(preactivation).astype(bf16)
    out_part = dot(hidden, out_half, ((1,), (0,)))
    layer_output = middle + (out_part[:tokens] + swapped(out_part[tokens:], 0)) + out_add
    layer_output = layer_output.astype(bf16)
    grad_hidden = dot(grads_pair, out_half, ((1,), (1,)))
    grad_pre = jax.vjp(gelu_tanh, preactivation)[1](grad_hidden)[0].astype(bf16)
    normed_part = dot(grad_pre, fc_half, ((1,), (1,)))
    grad_normed_two = normed_part[:tokens] + swapped(normed_part[tokens:], 0)
    grad_mid_part, gain_two_grad, shift_two_grad = jax.vjp(
        layer_norm, middle, gain_two, shift_two
    )[1](grad_normed_two)
    grad_middle = grads32 + grad_mid_part
    grad_branch = grad_middle.astype(bf16)

    grad_attended = jnp.pad(
        dot(proj_full, grad_branch, ((1,), (1,))).astype(bf16), ((0, padded - width), (0, 0))
    ).reshape(shards, group, tokens)
    grad_heads = lax.all_to_all(grad_attended, "shard", 0, 0, tiled=True)
    flat = ((0,), (0,))

    def parted(first, second, side):
        return jnp.where(side, second, first), jnp.where(side, first, second)

    proj_grad = dot(attended, grad_branch, ((1,), (0,))).astype(bf16)
    proj_grad = proj_grad.reshape(shards, 2, half_width, width)
    mine, sent = parted(proj_grad[:, 0], proj_grad[:, 1], odd)
    proj_grad = added(mine, swapped(sent, 0))
    fc_grad = dot(normed_pair, grad_pre, flat).astype(bf16).reshape(shards, local_width, -1)
    column = fc_grad.shape[2] // 2
    fc_mine, fc_sent = parted(
        jnp.concatenate([fc_grad[..., :column], proj_grad[:, : half_width // 2]], axis=1),
        jnp.concatenate([fc_grad[..., column:], proj_grad[:, half_width // 2 :]], axis=1),
        fc_side,
    )
    out_grad = dot(hidden, grads_pair, flat).astype(bf16).reshape(shards, 2, quarter, width)
    out_mine, out_sent = parted(out_grad[:, 0], out_grad[:, 1], out_side)
    fc_received = swapped(fc_sent, FC_BIT)
    out_received = swapped(out_sent, OUT_BIT)

    query_low = [None] * seqs
    kv_parts = [None] * seqs
    grad_heads = after(grad_heads, fc_sent, out_sent)
    for s in range(seqs):
        query_low[s], *kv_parts[s] = attend_back(
            shards, orders[s], s * piece, infos[s], queries[s], *saved[s], grad_heads, blocks[s]
        )

    ended = [parts[0] for parts in kv_parts]
    scattered = jnp.concatenate(
        [added(fc_mine, after(fc_received, *ended)), added(out_mine, after(out_received, *ended))],
        axis=1,
    )
    both = lax.psum_scatter(scattered, "shard", scatter_dimension=0, tiled=False)

    kv_low = [None] * seqs
    normed_parts = []
    gain_one_grad = jnp.zeros((width,), f32)
    shift_one_grad = jnp.zeros((width,), f32)
    for s in range(seqs):
        kv_low[s] = returned(*kv_parts[s], aparts[s], orders[s], late[s], [scattered])
        part = dot(query_low[s], q_weight, ((1,), (1,))) + dot(kv_low[s], kv_weight, ((1,), (1,)))
        gain_one_grad = gain_one_grad + jnp.sum(part * group_norms[s], axis=0)
        shift_one_grad = shift_one_grad + jnp.sum(part, axis=0)
        normed_parts.append(part.astype(bf16).reshape(shards, piece, width))
    fc_add_part = jnp.sum(grad_pre.astype(f32), axis=0).reshape(shards, 1, half_hidden)
    fc_add_part = jnp.where(jnp.arange(2)[None, :, None] == odd, fc_add_part, 0.0)

    def all_heads(vector):
        return lax.dynamic_update_slice_in_dim(
            jnp.zeros((padded,), f32), vector, shard_at * group, 0
        )[:width]

    query_sum = sum(jnp.sum(low.astype(f32), axis=0) for low in query_low)
    value_sum = sum(jnp.sum(low[:, group:].astype(f32), axis=0) for low in kv_low)
    vectors = jnp.stack(
        [
            gain_one_grad,
            shift_one_grad,
            all_heads(query_sum),
            all_heads(value_sum),
            jnp.sum(grad_branch.astype(f32), axis=0),
            gain_two_grad,
            shift_two_grad,
            jnp.sum(grads32, axis=0),
        ]
    )
    vectors = jnp.concatenate(
        [
            vectors.reshape(8, shards, local_width).transpose(1, 0, 2),
            fc_add_part.reshape(shards, -1, local_width),
        ],
        axis=1,
    ).astype(bf16)
    vectors = jnp.pad(vectors, ((0, 0), (0, 16 - vector_rows), (0, width - local_width)))
    vectors = lax.dynamic_update_slice(
        vectors, jnp.broadcast_to(both[:1, :1], (shards, 1, 1)), (0, 15, 0)
    )
    normed_parts = jnp.concatenate(normed_parts + [vectors], axis=1)
    summed = lax.psum_scatter(normed_parts, "shard", scatter_dimension=0, tiled=False).astype(f32)
    pull = jax.vjp(lambda v: normalized(v) * gain_one, inputs32)[1]
    input_grad = (grad_middle + pull(summed[:tokens])[0]).astype(bf16)
    sums = summed[tokens : tokens + vector_rows, :local_width]
    for bit in range(cycle.bit_length() - 1):
        sums = sums + swapped(sums, bit)

    cut = both.shape[0] - quarter
    out_grad = summed_over_chips(both[cut:], [bit for bit in chip_bits if bit != OUT_BIT])
    out_grad = jnp.concatenate(joined(out_grad.astype(bf16), OUT_BIT, out_side))
    out_grad = jnp.concatenate(pair_joined(out_grad, odd)).astype(f32)
    rest = summed_over_chips(both[:cut], [bit for bit in chip_bits if bit != FC_BIT])
    first, second = joined(rest.astype(bf16), FC_BIT, fc_side)
    proj_grad = jnp.concatenate([first[local_width:], second[local_width:]])
    proj_grad = jnp.concatenate(pair_joined(proj_grad, odd)).astype(f32)
    fc_grad = jnp.concatenate([first[:local_width], second[:local_width]], axis=1)
    fc_halves = pair_joined(fc_grad, odd)
    fc_grad = jnp.concatenate(
        [
            fc_halves[h][:, z * half_hidden : (z + 1) * half_hidden]
            for z in range(shards)
            for h in range(2)
        ],
        axis=1,
    ).astype(f32)

    grad = []
    for s in range(seqs):
        normed = after(normed_one[s], normed_parts)
        low = jnp.concatenate([query_low[s], kv_low[s]], axis=1)
        grad.append(dot(normed, low, flat))
    grad = sum(grad).astype(bf16).reshape(shards, local_width, -1)
    for bit in joins[::-1]:
        cut = grad.shape[1] // 2
        mine, sent = parted(grad[:, :cut], grad[:, cut:], (here >> bit) & 1)
        grad = added(mine, swapped(sent, bit))
    grad = lax.all_to_all(grad, "shard", 0, 0, tiled=True)
    grad = jnp.concatenate([grad[z] for z in range(shards)], axis=1)
    for turn, bit in enumerate(joins):
        if turn == 1:
            grad = after(grad, summed)
        grad = jnp.concatenate(joined(grad, bit, (here >> bit) & 1))
    thirds = [
        jnp.concatenate(
            [
                grad[:, (3 * z + third) * group : (3 * z + third + 1) * group]
                for z in range(shards)
            ],
            axis=1,
        )[:, :width]
        for third in range(3)
    ]
    qkv_grad = jnp.concatenate(thirds, axis=1).astype(f32)

    return (
        mirror_late(layer_output.reshape(seqs, piece, width)),
        mirror_late(input_grad.reshape(seqs, piece, width)),
        sums[0],
        sums[1],
        qkv_grad,
        sums[2],
        sums[3],
        proj_grad,
        sums[4],
        sums[5],
        sums[6],
        fc_grad,
        sums[8:].reshape(-1),
        out_grad,
        sums[7],
    )


def solution(mesh):
    tokens = P(None, ("ctx", "shard"), None)
    vector = P("shard")
    matrix = P("shard", None)
    return jax.shard_map(
        body,
        mesh=mesh,
        in_specs=(
            tokens,
            vector,
            vector,
            matrix,
            vector,
            vector,
            matrix,
            vector,
            vector,
            vector,
            matrix,
            vector,
            matrix,
            vector,
            tokens,
        ),
        out_specs=(
            tokens,
            tokens,
            vector,
            vector,
            matrix,
            vector,
            vector,
            matrix,
            vector,
            vector,
            vector,
            matrix,
            vector,
            matrix,
            vector,
        ),
        check_vma=False,
    )
```

```python
import functools

import jax
import jax.numpy as jnp
from jax import lax
from jax.experimental import pallas as pl
from jax.experimental.pallas import tpu as pltpu
from jax.sharding import PartitionSpec as P

HEADS = 12
HEAD = 64
TILE = 512
EXP2_SCALE = 0.125 * 1.4426950408889634
f32 = jnp.float32
bf16 = jnp.bfloat16
FC_BIT = 1
OUT_BIT = 2
VMEM_LIMIT = 56 * 1024 * 1024


def normalized(values):
    centered = values - jnp.mean(values, axis=-1, keepdims=True)
    variance = jnp.mean(centered * centered, axis=-1, keepdims=True)
    return centered * lax.rsqrt(variance + 1e-05)


def layer_norm(values, gain, shift):
    return normalized(values) * gain + shift


def gelu_tanh(values):
    return jax.nn.gelu(values, approximate=True)


def swapped(block, bit):
    n = lax.axis_size("ctx")
    return lax.ppermute(block, "ctx", [(i, i ^ (1 << bit)) for i in range(n)])


def tree_pairs(aparts, bit, later, late, back):
    n = lax.axis_size("ctx")
    reach = [0]
    for other in later:
        reach += [r ^ (1 << other) for r in reach]
    place = (lambda i: n - 1 - i) if late else (lambda i: i)
    pairs = []
    for i in range(n):
        target = i ^ (1 << bit)
        if any(place(i ^ apart) <= place(target ^ r) for r in reach for apart in aparts):
            pairs.append((target, i) if back else (i, target))
    return pairs


def spread(own, order, late, before):
    held, aparts = own[None], [0]
    for bit in order[:-2]:
        pairs = tree_pairs(aparts, bit, order[order.index(bit) + 1 :], late, False)
        held = jnp.concatenate([held, lax.ppermute(held, "ctx", pairs)])
        aparts = aparts + [apart ^ (1 << bit) for apart in aparts]
    bit = order[-2]
    held = after(held, *before)
    received = lax.ppermute(held, "ctx", tree_pairs(aparts, bit, order[-1:], late, False))
    aparts = aparts + [apart ^ (1 << bit) for apart in aparts]
    blocks = [held, received, swapped(held, 0), swapped(received, 0)]
    return blocks, aparts + [apart ^ 1 for apart in aparts]


def added(first, second):
    return (first.astype(f32) + second.astype(f32)).astype(bf16)


def returned(near, middle, far, aparts, order, late, before):
    received = swapped(far, 0)
    count = near.shape[0]
    middle = after(added(middle, received[count:]), *before)
    pairs = tree_pairs(aparts[:count], order[-2], order[-1:], late, True)
    near = added(added(near, received[:count]), lax.ppermute(middle, "ctx", pairs))
    for bit in order[:-2][::-1]:
        count = near.shape[0] // 2
        pairs = tree_pairs(aparts[:count], bit, order[order.index(bit) + 1 :], late, True)
        near = added(near[:count], lax.ppermute(near[count:], "ctx", pairs))
    return near[0]


def after(value, *others):
    return lax.optimization_barrier((value,) + others)[0]


def mirrored(block):
    n = lax.axis_size("ctx")
    return lax.ppermute(block, "ctx", [(i, n - 1 - i) for i in range(n)])


def shifted(block, distance):
    n = lax.axis_size("shard")
    return lax.ppermute(block, "shard", [(i, (i + distance) % n) for i in range(n)])


def dot(a, b, contract):
    return lax.dot_general(a, b, ((contract[0], contract[1]), ((), ())), preferred_element_type=f32)


def summed_over_chips(part, bits):
    for bit in bits:
        low = part.astype(bf16)
        part = low.astype(f32) + swapped(low, bit).astype(f32)
    return part


def joined(half, bit, side):
    other = swapped(half, bit)
    return jnp.where(side, other, half), jnp.where(side, half, other)


def pair_joined(half, odd):
    return joined(half, 0, odd)


def load_blocks(refs, held, sems):
    each = refs[0].shape[0]
    copies = [
        pltpu.make_async_copy(ref, held.at[pl.ds(i * each, each)], sems.at[i])
        for i, ref in enumerate(refs)
    ]
    for copy in copies:
        copy.start()
    return copies


def slot_of(place, here, order):
    apart = place ^ here
    return sum(((apart >> bit) & 1) << k for k, bit in enumerate(order))


def forward_kernel(heads, shards, order, info, q_ref, *refs):
    kv_refs = refs[:4]
    att_ref, out_ref, lse_ref, held, sems, m_ref, l_ref, acc_ref = refs[4:]
    rows, width = q_ref.shape
    piece = rows // shards
    tile = min(TILE, rows)
    per = rows // tile
    copies = load_blocks(kv_refs, held, sems)
    key_places = lax.broadcasted_iota(jnp.int32, (rows, 1), 0)
    query_places = lax.broadcasted_iota(jnp.int32, (1, rows), 1)
    for copy in copies:
        copy.wait()
    for part in range(per):
        span = slice(part * tile, (part + 1) * tile)

        def step(slot, key_part, masked, start):
            keys_at = slice(key_part * tile, (key_part + 1) * tile)
            allowed = key_places[keys_at] <= query_places[:, span] if masked else None
            for h in range(heads):
                lanes = slice(h * HEAD, (h + 1) * HEAD)
                lanes_v = slice(width + h * HEAD, width + (h + 1) * HEAD)
                q = q_ref[span, lanes]
                k = held[slot, keys_at, lanes]
                v = held[slot, keys_at, lanes_v]
                s = dot(k, q, ((1,), (1,))) * EXP2_SCALE
                if masked:
                    s = jnp.where(allowed, s, -1e30)
                m = jnp.max(s, axis=0, keepdims=True)
                if start:
                    p = jnp.exp2(s - m)
                    l_ref[h] = jnp.sum(p, axis=0, keepdims=True)
                    acc_ref[h] = dot(v, p.astype(bf16), ((0,), (0,)))
                else:
                    old = m_ref[h]
                    m = jnp.maximum(old, m)
                    p = jnp.exp2(s - m)
                    factor = jnp.exp2(old - m)
                    l_ref[h] = l_ref[h] * factor + jnp.sum(p, axis=0, keepdims=True)
                    acc_ref[h] = acc_ref[h] * factor + dot(v, p.astype(bf16), ((0,), (0,)))
                m_ref[h] = m

        for key_part in range(per):
            step(slot_of(info[0], info[0], order), key_part, True, key_part == 0)

        @pl.loop(0, info[0])
        def _(j):
            for key_part in range(per):
                step(slot_of(j, info[0], order), key_part, False, False)

        for h in range(heads):
            total = l_ref[h]
            done = acc_ref[h] / total
            out_ref[h * HEAD : (h + 1) * HEAD, span] = done
            lse_ref[h, :, span] = m_ref[h] + jnp.log2(total)
            low = done.astype(bf16)
            for z in range(tile // piece):
                att_ref[part * (tile // piece) + z, h * HEAD : (h + 1) * HEAD, :] = low[
                    :, z * piece : (z + 1) * piece
                ]


def backward_kernel(heads, shards, order, first, info, q_ref, out_ref, lse_ref, go_ref, *refs):
    kv_refs = refs[:4]
    dq_ref, near_ref, middle_ref, far_ref, held, sums, sems, end_sems, acc_ref = refs[4:]
    count = held.shape[0]
    rows, width = q_ref.shape
    piece = rows // shards
    tile = min(TILE, rows)
    per = rows // tile
    copies = load_blocks(kv_refs, held, sems)
    key_places = lax.broadcasted_iota(jnp.int32, (rows, 1), 0)
    query_places = lax.broadcasted_iota(jnp.int32, (1, rows), 1)

    @pl.loop(info[0] + 1, count)
    def _(j):
        sums[slot_of(j, info[0], order)] = jnp.zeros((rows, 2 * width), bf16)

    for copy in copies:
        copy.wait()
    for part in range(per):
        span = slice(part * tile, (part + 1) * tile)
        pieces = range(part * (tile // piece), (part + 1) * (tile // piece))
        go_all = jnp.concatenate(
            [go_ref[z, :, first : first + piece] for z in pieces], axis=1
        )
        deltas = []
        for h in range(heads):
            lanes = slice(h * HEAD, (h + 1) * HEAD)
            deltas.append(
                jnp.sum(go_all[lanes].astype(f32) * out_ref[lanes, span], axis=0, keepdims=True)
            )

        def step(slot, key_part, masked, start):
            keys_at = slice(key_part * tile, (key_part + 1) * tile)
            allowed = key_places[keys_at] <= query_places[:, span] if masked else None
            for h in range(heads):
                lanes = slice(h * HEAD, (h + 1) * HEAD)
                lanes_v = slice(width + h * HEAD, width + (h + 1) * HEAD)
                q = q_ref[span, lanes]
                go = go_all[lanes]
                k = held[slot, keys_at, lanes]
                v = held[slot, keys_at, lanes_v]
                p = jnp.exp2(dot(k, q, ((1,), (1,))) * EXP2_SCALE - lse_ref[h, :, span])
                if masked:
                    p = jnp.where(allowed, p, 0.0)
                pulled = dot(v, go, ((1,), (0,)))
                slopes = (p * (pulled - deltas[h])).astype(bf16)
                dv = dot(p.astype(bf16), go, ((1,), (1,)))
                dk = dot(slopes, q, ((1,), (0,))) * 0.125
                if part:
                    dk = dk + sums[slot, keys_at, lanes].astype(f32)
                    dv = dv + sums[slot, keys_at, lanes_v].astype(f32)
                sums[slot, keys_at, lanes] = dk.astype(bf16)
                sums[slot, keys_at, lanes_v] = dv.astype(bf16)
                dq = dot(k, slopes, ((0,), (0,)))
                if start:
                    acc_ref[h] = dq
                else:
                    acc_ref[h] += dq

        for key_part in range(per):
            step(slot_of(info[0], info[0], order), key_part, True, key_part == 0)

        @pl.loop(0, info[0])
        def _(j):
            for key_part in range(per):
                step(slot_of(j, info[0], order), key_part, False, False)

        for h in range(heads):
            dq_ref[span, h * HEAD : (h + 1) * HEAD] = (acc_ref[h] * 0.125).T.astype(bf16)
    copies = []
    base = 0
    for i, ref in enumerate((near_ref, middle_ref, far_ref)):
        copies.append(
            pltpu.make_async_copy(sums.at[pl.ds(base, ref.shape[0])], ref, end_sems.at[i])
        )
        base += ref.shape[0]
    for copy in copies:
        copy.start()
    for copy in copies:
        copy.wait()


SMEM = pl.BlockSpec(memory_space=pltpu.SMEM)
VMEM = pl.BlockSpec(memory_space=pltpu.VMEM)
ANY = pl.BlockSpec(memory_space=pl.ANY)


def attend(shards, order, info, queries, blocks):
    rows, width = queries.shape
    heads = width // HEAD
    count = 4 * blocks[0].shape[0]
    tile = min(TILE, rows)
    scores = heads * rows * rows * (count + 1) // 2
    return pl.pallas_call(
        functools.partial(forward_kernel, heads, shards, order),
        out_shape=(
            jax.ShapeDtypeStruct((shards, width, rows // shards), bf16),
            jax.ShapeDtypeStruct((width, rows), f32),
            jax.ShapeDtypeStruct((heads, 1, rows), f32),
        ),
        in_specs=[SMEM, VMEM] + [ANY] * 4,
        out_specs=(VMEM, VMEM, VMEM),
        scratch_shapes=[
            pltpu.VMEM((count, rows, 2 * width), bf16),
            pltpu.SemaphoreType.DMA((4,)),
            pltpu.VMEM((heads, 1, tile), f32),
            pltpu.VMEM((heads, 1, tile), f32),
            pltpu.VMEM((heads, HEAD, tile), f32),
        ],
        compiler_params=pltpu.CompilerParams(vmem_limit_bytes=VMEM_LIMIT),
        cost_estimate=pl.CostEstimate(
            flops=scores * 16 * HEAD,
            bytes_accessed=4 * rows * width * (count + 2),
            transcendentals=scores,
        ),
        name="attention_forward",
    )(info, queries, *blocks)


def attend_back(shards, order, first, info, queries, out, lse, grads, blocks):
    rows, width = queries.shape
    heads = width // HEAD
    count = 4 * blocks[0].shape[0]
    tile = min(TILE, rows)
    scores = heads * rows * rows * (count + 1) // 2
    return pl.pallas_call(
        functools.partial(backward_kernel, heads, shards, order, first),
        out_shape=[jax.ShapeDtypeStruct((rows, width), bf16)]
        + [
            jax.ShapeDtypeStruct((share, rows, 2 * width), bf16)
            for share in (count // 4, count // 4, count // 2)
        ],
        in_specs=[SMEM] + [VMEM] * 4 + [ANY] * 4,
        out_specs=[VMEM] + [ANY] * 3,
        scratch_shapes=[
            pltpu.VMEM((count, rows, 2 * width), bf16),
            pltpu.VMEM((count, rows, 2 * width), bf16),
            pltpu.SemaphoreType.DMA((4,)),
            pltpu.SemaphoreType.DMA((3,)),
            pltpu.VMEM((heads, HEAD, tile), f32),
        ],
        compiler_params=pltpu.CompilerParams(vmem_limit_bytes=VMEM_LIMIT),
        cost_estimate=pl.CostEstimate(
            flops=scores * 10 * HEAD,
            bytes_accessed=8 * rows * width * (count + 2),
            transcendentals=scores,
        ),
        name="attention_backward",
    )(info, queries, out, lse, grads, *blocks)


def body(
    layer_input,
    attn_gain,
    attn_shift,
    qkv_weight,
    query_bias,
    value_bias,
    proj_weight,
    proj_bias,
    mlp_gain,
    mlp_shift,
    fc_weight,
    fc_bias,
    out_weight,
    out_bias,
    grad_output,
):
    seqs, piece, width = layer_input.shape
    cycle = lax.axis_size("ctx")
    shards = lax.axis_size("shard")
    here = lax.axis_index("ctx")
    shard_at = lax.axis_index("shard")
    odd = here & 1
    chip_bits = list(range(1, cycle.bit_length() - 1))
    rows = shards * piece
    local_width = qkv_weight.shape[0]
    local_hidden = out_weight.shape[0]
    half_width = local_width // 2
    half_hidden = local_hidden // 2
    quarter = half_hidden // 2
    group = -(-HEADS // shards) * HEAD
    padded = group * shards
    late = [seq >= (seqs + 1) // 2 for seq in range(seqs)]
    tokens = seqs * piece


    def mirror_late(held):
        return jnp.stack([mirrored(held[s]) if late[s] else held[s] for s in range(seqs)])

    layer_input = mirror_late(layer_input)
    grad_output = mirror_late(grad_output)
    gathered = lax.all_gather(layer_input, "shard", axis=0)

    def by_heads(weight):
        parts = []
        for third in range(3):
            part = weight[:, third * width : (third + 1) * width]
            parts.append(jnp.pad(part, ((0, 0), (0, padded - width))))
        return jnp.stack(
            [
                jnp.concatenate([part[:, z * group : (z + 1) * group] for part in parts], axis=1)
                for z in range(shards)
            ]
        )

    joins = chip_bits[::-1] + [0]
    share = local_width // cycle
    weight_share = lax.dynamic_slice_in_dim(
        qkv_weight, sum(((here >> bit) & 1) << k for k, bit in enumerate(joins)) * share, share, 0
    )
    packed = jnp.concatenate(
        [
            jnp.stack(
                [attn_gain, attn_shift, query_bias, value_bias, proj_bias, mlp_gain, mlp_shift, out_bias]
            ),
            fc_bias.reshape(-1, local_width),
        ]
    )
    vector_rows = packed.shape[0]
    packed = jnp.pad(packed, ((0, 16 - vector_rows), (0, 3 * group - local_width)))
    moved = lax.all_to_all(
        jnp.concatenate(
            [by_heads(weight_share), jnp.broadcast_to(packed, (shards,) + packed.shape)], axis=1
        ),
        "shard",
        0,
        0,
        tiled=True,
    )
    small = moved[:, share : share + vector_rows, :local_width].astype(f32)
    qkv_own = moved[:, :share]
    for bit in joins:
        if bit == 0:
            qkv_own, grad_output, _ = lax.optimization_barrier((qkv_own, grad_output, gathered))
        qkv_own = jnp.concatenate(joined(qkv_own, bit, (here >> bit) & 1), axis=1)
    qkv_own = qkv_own.reshape(width, 3 * group)
    q_weight = qkv_own[:, :group]
    kv_weight = qkv_own[:, group:]

    vectors = [small[:, i].reshape(-1) for i in range(8)]
    gain_one, shift_one, query_add, value_add, proj_add, gain_two, shift_two, out_add = vectors
    bias_rows = half_hidden // local_width
    fc_add = lax.dynamic_slice_in_dim(small, 8 + odd * bias_rows, bias_rows, 1).reshape(-1)

    def own_heads(vector):
        return lax.dynamic_slice_in_dim(
            jnp.pad(vector, (0, padded - width)), shard_at * group, group, 0
        )

    kv_add = jnp.concatenate([jnp.zeros((group,), f32), own_heads(value_add)])
    query_add = own_heads(query_add)

    fc_side = (here >> FC_BIT) & 1
    out_side = (here >> OUT_BIT) & 1
    proj_half = lax.dynamic_slice_in_dim(proj_weight, odd * half_width, half_width, 0)
    fc_quarter = jnp.concatenate(
        [
            lax.dynamic_slice_in_dim(
                fc_weight,
                (fc_side * (shards // 2) + z) * local_hidden + odd * half_hidden,
                half_hidden,
                1,
            )
            for z in range(shards // 2)
        ],
        axis=1,
    )
    out_quarter = lax.dynamic_slice_in_dim(
        out_weight, odd * half_hidden + out_side * quarter, quarter, 0
    )
    weights = lax.all_gather(
        jnp.concatenate([proj_half, fc_quarter, out_quarter]), "shard", axis=0
    )

    orders = [chip_bits + [0], chip_bits[::-1] + [0]]
    orders = [orders[s % 2] for s in range(seqs)]
    group_norms, normed_one, own_blocks, queries, infos = [], [], [], [], []
    for s in range(seqs):
        norm = normalized(gathered[:, s].reshape(rows, width).astype(f32))
        normed = (norm * gain_one + shift_one).astype(bf16)
        group_norms.append(norm)
        normed_one.append(normed)
        own_blocks.append((dot(normed, kv_weight, ((1,), (0,))) + kv_add).astype(bf16))
        queries.append((dot(normed, q_weight, ((1,), (0,))) + query_add).astype(bf16))
        infos.append(jnp.reshape(cycle - 1 - here if late[s] else here, (1,)).astype(jnp.int32))
    spreads = [spread(own_blocks[s], orders[s], late[s], queries) for s in range(seqs)]
    blocks = [blocks for blocks, _ in spreads]
    aparts = [apart for _, apart in spreads]
    saved = [None] * seqs
    attended_parts = [None] * seqs
    for s in reversed(range(seqs)):
        attended_parts[s], *saved[s] = attend(shards, orders[s], infos[s], queries[s], blocks[s])
    attended, weights = lax.optimization_barrier(
        (jnp.concatenate(attended_parts, axis=2), weights)
    )
    cut = half_width + local_width
    proj_half, fc_quarter, out_quarter = lax.optimization_barrier(
        (weights[:, :half_width], weights[:, half_width:cut], weights[:, cut:])
    )
    proj_half = pair_joined(proj_half, odd)
    proj_full = jnp.stack(proj_half, axis=1).reshape(width, width)
    fc_quarter = fc_quarter.reshape(width, -1)
    fc_half = jnp.concatenate(joined(fc_quarter, FC_BIT, fc_side), axis=1)
    out_half = jnp.stack(joined(out_quarter, OUT_BIT, out_side), axis=1).reshape(-1, width)
    attended = lax.all_to_all(attended, "shard", 0, 0, tiled=True).reshape(padded, tokens)[:width]

    inputs32 = layer_input.reshape(tokens, width).astype(f32)
    grads_own = grad_output.reshape(tokens, width)
    grads32 = grads_own.astype(f32)
    attended, fc_half = lax.optimization_barrier((attended, fc_half))
    middle = inputs32 + dot(attended, proj_full, ((0,), (0,))) + proj_add
    normed_two = layer_norm(middle, gain_two, shift_two).astype(bf16)

    normed_pair = jnp.concatenate([normed_two, swapped(normed_two, 0)])
    grads_pair = jnp.concatenate([grads_own, swapped(grads_own, 0)])
    preactivation = dot(normed_pair, fc_half, ((1,), (0,))) + fc_add
    hidden = gelu_tanh(preactivation).astype(bf16)
    out_part = dot(hidden, out_half, ((1,), (0,)))
    layer_output = middle + (out_part[:tokens] + swapped(out_part[tokens:], 0)) + out_add
    layer_output = layer_output.astype(bf16)
    grad_hidden = dot(grads_pair, out_half, ((1,), (1,)))
    grad_pre = jax.vjp(gelu_tanh, preactivation)[1](grad_hidden)[0].astype(bf16)
    normed_part = dot(grad_pre, fc_half, ((1,), (1,)))
    grad_normed_two = normed_part[:tokens] + swapped(normed_part[tokens:], 0)
    grad_mid_part, gain_two_grad, shift_two_grad = jax.vjp(
        layer_norm, middle, gain_two, shift_two
    )[1](grad_normed_two)
    grad_middle = grads32 + grad_mid_part
    grad_branch = grad_middle.astype(bf16)

    grad_attended = jnp.pad(
        dot(proj_full, grad_branch, ((1,), (1,))).astype(bf16), ((0, padded - width), (0, 0))
    ).reshape(shards, group, tokens)
    grad_heads = lax.all_to_all(grad_attended, "shard", 0, 0, tiled=True)
    flat = ((0,), (0,))

    def parted(first, second, side):
        return jnp.where(side, second, first), jnp.where(side, first, second)

    hidden, normed_pair, attended = [
        after(held, grad_attended) for held in (hidden, normed_pair, attended)
    ]
    proj_grad = dot(attended, grad_branch, ((1,), (0,))).astype(bf16)
    proj_grad = proj_grad.reshape(shards, 2, half_width, width)
    mine, sent = parted(proj_grad[:, 0], proj_grad[:, 1], odd)
    proj_grad = added(mine, swapped(sent, 0))
    fc_grad = dot(normed_pair, grad_pre, flat).astype(bf16).reshape(shards, local_width, -1)
    column = fc_grad.shape[2] // 2
    fc_mine, fc_sent = parted(
        jnp.concatenate([fc_grad[..., :column], proj_grad[:, : half_width // 2]], axis=1),
        jnp.concatenate([fc_grad[..., column:], proj_grad[:, half_width // 2 :]], axis=1),
        fc_side,
    )
    out_grad = dot(hidden, grads_pair, flat).astype(bf16).reshape(shards, 2, quarter, width)
    out_mine, out_sent = parted(out_grad[:, 0], out_grad[:, 1], out_side)
    fc_received = swapped(fc_sent, FC_BIT)
    out_received = swapped(out_sent, OUT_BIT)

    query_low = [None] * seqs
    kv_parts = [None] * seqs
    grad_heads = after(grad_heads, fc_sent, out_sent)
    for s in range(seqs):
        query_low[s], *kv_parts[s] = attend_back(
            shards, orders[s], s * piece, infos[s], queries[s], *saved[s], grad_heads, blocks[s]
        )

    ended = [parts[0] for parts in kv_parts]
    scattered = jnp.concatenate(
        [added(fc_mine, after(fc_received, *ended)), added(out_mine, after(out_received, *ended))],
        axis=1,
    )
    both = lax.psum_scatter(scattered, "shard", scatter_dimension=0, tiled=False)

    kv_low = [None] * seqs
    normed_parts = []
    gain_one_grad = jnp.zeros((width,), f32)
    shift_one_grad = jnp.zeros((width,), f32)
    for s in range(seqs):
        kv_low[s] = returned(*kv_parts[s], aparts[s], orders[s], late[s], [scattered])
        part = dot(query_low[s], q_weight, ((1,), (1,))) + dot(kv_low[s], kv_weight, ((1,), (1,)))
        gain_one_grad = gain_one_grad + jnp.sum(part * group_norms[s], axis=0)
        shift_one_grad = shift_one_grad + jnp.sum(part, axis=0)
        normed_parts.append(part.astype(bf16).reshape(shards, piece, width))
    fc_add_part = jnp.sum(grad_pre.astype(f32), axis=0).reshape(shards, 1, half_hidden)
    fc_add_part = jnp.where(jnp.arange(2)[None, :, None] == odd, fc_add_part, 0.0)

    def all_heads(vector):
        return lax.dynamic_update_slice_in_dim(
            jnp.zeros((padded,), f32), vector, shard_at * group, 0
        )[:width]

    query_sum = sum(jnp.sum(low.astype(f32), axis=0) for low in query_low)
    value_sum = sum(jnp.sum(low[:, group:].astype(f32), axis=0) for low in kv_low)
    vectors = jnp.stack(
        [
            gain_one_grad,
            shift_one_grad,
            all_heads(query_sum),
            all_heads(value_sum),
            jnp.sum(grad_branch.astype(f32), axis=0),
            gain_two_grad,
            shift_two_grad,
            jnp.sum(grads32, axis=0),
        ]
    )
    vectors = jnp.concatenate(
        [
            vectors.reshape(8, shards, local_width).transpose(1, 0, 2),
            fc_add_part.reshape(shards, -1, local_width),
        ],
        axis=1,
    ).astype(bf16)
    vectors = jnp.pad(vectors, ((0, 0), (0, 16 - vector_rows), (0, width - local_width)))
    vectors = lax.dynamic_update_slice(
        vectors, jnp.broadcast_to(both[:1, :1], (shards, 1, 1)), (0, 15, 0)
    )
    normed_parts = jnp.concatenate(normed_parts + [vectors], axis=1)
    summed = lax.psum_scatter(normed_parts, "shard", scatter_dimension=0, tiled=False).astype(f32)
    pull = jax.vjp(lambda v: normalized(v) * gain_one, inputs32)[1]
    input_grad = (grad_middle + pull(summed[:tokens])[0]).astype(bf16)
    sums = summed[tokens : tokens + vector_rows, :local_width]
    sums = sums + swapped(sums, 0)
    sums = after(sums, input_grad)
    for bit in chip_bits:
        sums = sums + swapped(sums, bit)

    layer_output = after(layer_output, normed_parts).reshape(seqs, piece, width)
    layer_output = mirror_late(layer_output)

    cut = both.shape[0] - quarter
    out_grad = summed_over_chips(both[cut:], [bit for bit in chip_bits if bit != OUT_BIT])
    out_grad = jnp.concatenate(joined(out_grad.astype(bf16), OUT_BIT, out_side))
    out_grad = after(out_grad, summed)
    out_grad = jnp.concatenate(pair_joined(out_grad, odd)).astype(f32)
    rest = summed_over_chips(both[:cut], [bit for bit in chip_bits if bit != FC_BIT])
    first, second = joined(rest.astype(bf16), FC_BIT, fc_side)
    first, second = after(first, summed), after(second, summed)
    proj_grad = jnp.concatenate([first[local_width:], second[local_width:]])
    proj_grad = jnp.concatenate(pair_joined(proj_grad, odd)).astype(f32)
    fc_grad = jnp.concatenate([first[:local_width], second[:local_width]], axis=1)
    fc_halves = pair_joined(fc_grad, odd)
    fc_grad = jnp.concatenate(
        [
            fc_halves[h][:, z * half_hidden : (z + 1) * half_hidden]
            for z in range(shards)
            for h in range(2)
        ],
        axis=1,
    ).astype(f32)

    grad = []
    for s in range(seqs):
        normed = after(normed_one[s], normed_parts)
        low = jnp.concatenate([query_low[s], kv_low[s]], axis=1)
        grad.append(dot(normed, low, flat))
    grad = sum(grad).astype(bf16).reshape(shards, local_width, -1)
    for bit in joins[::-1]:
        cut = grad.shape[1] // 2
        mine, sent = parted(grad[:, :cut], grad[:, cut:], (here >> bit) & 1)
        grad = added(mine, swapped(sent, bit))
    grad = lax.all_to_all(grad, "shard", 0, 0, tiled=True)
    grad = jnp.concatenate([grad[z] for z in range(shards)], axis=1)
    for turn, bit in enumerate(joins):
        if turn == 1:
            grad = after(grad, summed)
        grad = jnp.concatenate(joined(grad, bit, (here >> bit) & 1))
    thirds = [
        jnp.concatenate(
            [
                grad[:, (3 * z + third) * group : (3 * z + third + 1) * group]
                for z in range(shards)
            ],
            axis=1,
        )[:, :width]
        for third in range(3)
    ]
    qkv_grad = jnp.concatenate(thirds, axis=1).astype(f32)

    return (
        layer_output,
        mirror_late(input_grad.reshape(seqs, piece, width)),
        sums[0],
        sums[1],
        qkv_grad,
        sums[2],
        sums[3],
        proj_grad,
        sums[4],
        sums[5],
        sums[6],
        fc_grad,
        sums[8:].reshape(-1),
        out_grad,
        sums[7],
    )


def solution(mesh):
    tokens = P(None, ("ctx", "shard"), None)
    vector = P("shard")
    matrix = P("shard", None)
    return jax.shard_map(
        body,
        mesh=mesh,
        in_specs=(
            tokens,
            vector,
            vector,
            matrix,
            vector,
            vector,
            matrix,
            vector,
            vector,
            vector,
            matrix,
            vector,
            matrix,
            vector,
            tokens,
        ),
        out_specs=(
            tokens,
            tokens,
            vector,
            vector,
            matrix,
            vector,
            vector,
            matrix,
            vector,
            vector,
            vector,
            matrix,
            vector,
            matrix,
            vector,
        ),
        check_vma=False,
    )
```

```python
import functools

import jax
import jax.numpy as jnp
from jax import lax
from jax.experimental import pallas as pl
from jax.experimental.pallas import tpu as pltpu
from jax.sharding import PartitionSpec as P

HEADS = 12
HEAD = 64
TILE = 512
EXP2_SCALE = 0.125 * 1.4426950408889634
f32 = jnp.float32
bf16 = jnp.bfloat16
FC_BIT = 1
OUT_BIT = 2
VMEM_LIMIT = 56 * 1024 * 1024


def normalized(values):
    centered = values - jnp.mean(values, axis=-1, keepdims=True)
    variance = jnp.mean(centered * centered, axis=-1, keepdims=True)
    return centered * lax.rsqrt(variance + 1e-05)


def layer_norm(values, gain, shift):
    return normalized(values) * gain + shift


def gelu_tanh(values):
    return jax.nn.gelu(values, approximate=True)


def swapped(block, bit):
    n = lax.axis_size("ctx")
    return lax.ppermute(block, "ctx", [(i, i ^ (1 << bit)) for i in range(n)])


def tree_pairs(aparts, bit, later, late, back):
    n = lax.axis_size("ctx")
    reach = [0]
    for other in later:
        reach += [r ^ (1 << other) for r in reach]
    place = (lambda i: n - 1 - i) if late else (lambda i: i)
    pairs = []
    for i in range(n):
        target = i ^ (1 << bit)
        if any(place(i ^ apart) <= place(target ^ r) for r in reach for apart in aparts):
            pairs.append((target, i) if back else (i, target))
    return pairs


def spread(own, order, late, before):
    held, aparts = own[None], [0]
    for bit in order[:-2]:
        pairs = tree_pairs(aparts, bit, order[order.index(bit) + 1 :], late, False)
        held = jnp.concatenate([held, lax.ppermute(held, "ctx", pairs)])
        aparts = aparts + [apart ^ (1 << bit) for apart in aparts]
    bit = order[-2]
    held = after(held, *before)
    received = lax.ppermute(held, "ctx", tree_pairs(aparts, bit, order[-1:], late, False))
    aparts = aparts + [apart ^ (1 << bit) for apart in aparts]
    blocks = [held, received, swapped(held, 0), swapped(received, 0)]
    return blocks, aparts + [apart ^ 1 for apart in aparts]


def added(first, second):
    return (first.astype(f32) + second.astype(f32)).astype(bf16)


def returned(near, middle, far, aparts, order, late, before):
    received = swapped(far, 0)
    count = near.shape[0]
    middle = added(middle, received[count:])
    pairs = tree_pairs(aparts[:count], order[-2], order[-1:], late, True)
    near = added(added(near, received[:count]), lax.ppermute(middle, "ctx", pairs))
    for bit in order[:-2][::-1]:
        count = near.shape[0] // 2
        pairs = tree_pairs(aparts[:count], bit, order[order.index(bit) + 1 :], late, True)
        sent = after(near[count:], *before)
        near = added(near[:count], lax.ppermute(sent, "ctx", pairs))
    return near[0]


def after(value, *others):
    return lax.optimization_barrier((value,) + others)[0]


def mirrored(block):
    n = lax.axis_size("ctx")
    return lax.ppermute(block, "ctx", [(i, n - 1 - i) for i in range(n)])


def shifted(block, distance):
    n = lax.axis_size("shard")
    return lax.ppermute(block, "shard", [(i, (i + distance) % n) for i in range(n)])


def dot(a, b, contract):
    return lax.dot_general(a, b, ((contract[0], contract[1]), ((), ())), preferred_element_type=f32)


def summed_over_chips(part, bits):
    for bit in bits:
        low = part.astype(bf16)
        part = low.astype(f32) + swapped(low, bit).astype(f32)
    return part


def joined(half, bit, side):
    other = swapped(half, bit)
    return jnp.where(side, other, half), jnp.where(side, half, other)


def pair_joined(half, odd):
    return joined(half, 0, odd)


def load_blocks(refs, held, sems):
    each = refs[0].shape[0]
    copies = [
        pltpu.make_async_copy(ref, held.at[pl.ds(i * each, each)], sems.at[i])
        for i, ref in enumerate(refs)
    ]
    for copy in copies:
        copy.start()
    return copies


def slot_of(place, here, order):
    apart = place ^ here
    return sum(((apart >> bit) & 1) << k for k, bit in enumerate(order))


def forward_kernel(heads, shards, order, info, q_ref, *refs):
    kv_refs = refs[:4]
    att_ref, out_ref, lse_ref, held, sems, m_ref, l_ref, acc_ref = refs[4:]
    rows, width = q_ref.shape
    piece = rows // shards
    tile = min(TILE, rows)
    per = rows // tile
    copies = load_blocks(kv_refs, held, sems)
    key_places = lax.broadcasted_iota(jnp.int32, (rows, 1), 0)
    query_places = lax.broadcasted_iota(jnp.int32, (1, rows), 1)
    for copy in copies:
        copy.wait()
    for part in range(per):
        span = slice(part * tile, (part + 1) * tile)

        def step(slot, key_part, masked, start):
            keys_at = slice(key_part * tile, (key_part + 1) * tile)
            allowed = key_places[keys_at] <= query_places[:, span] if masked else None
            for h in range(heads):
                lanes = slice(h * HEAD, (h + 1) * HEAD)
                lanes_v = slice(width + h * HEAD, width + (h + 1) * HEAD)
                q = q_ref[span, lanes]
                k = held[slot, keys_at, lanes]
                v = held[slot, keys_at, lanes_v]
                s = dot(k, q, ((1,), (1,))) * EXP2_SCALE
                if masked:
                    s = jnp.where(allowed, s, -1e30)
                m = jnp.max(s, axis=0, keepdims=True)
                if start:
                    p = jnp.exp2(s - m)
                    l_ref[h] = jnp.sum(p, axis=0, keepdims=True)
                    acc_ref[h] = dot(v, p.astype(bf16), ((0,), (0,)))
                else:
                    old = m_ref[h]
                    m = jnp.maximum(old, m)
                    p = jnp.exp2(s - m)
                    factor = jnp.exp2(old - m)
                    l_ref[h] = l_ref[h] * factor + jnp.sum(p, axis=0, keepdims=True)
                    acc_ref[h] = acc_ref[h] * factor + dot(v, p.astype(bf16), ((0,), (0,)))
                m_ref[h] = m

        for key_part in range(per):
            step(slot_of(info[0], info[0], order), key_part, True, key_part == 0)

        @pl.loop(0, info[0])
        def _(j):
            for key_part in range(per):
                step(slot_of(j, info[0], order), key_part, False, False)

        for h in range(heads):
            total = l_ref[h]
            done = acc_ref[h] / total
            out_ref[h * HEAD : (h + 1) * HEAD, span] = done
            lse_ref[h, :, span] = m_ref[h] + jnp.log2(total)
            low = done.astype(bf16)
            for z in range(tile // piece):
                att_ref[part * (tile // piece) + z, h * HEAD : (h + 1) * HEAD, :] = low[
                    :, z * piece : (z + 1) * piece
                ]


def backward_kernel(heads, shards, order, first, info, q_ref, out_ref, lse_ref, go_ref, *refs):
    kv_refs = refs[:4]
    dq_ref, near_ref, middle_ref, far_ref, held, sums, sems, end_sems, acc_ref = refs[4:]
    count = held.shape[0]
    rows, width = q_ref.shape
    piece = rows // shards
    tile = min(TILE, rows)
    per = rows // tile
    copies = load_blocks(kv_refs, held, sems)
    key_places = lax.broadcasted_iota(jnp.int32, (rows, 1), 0)
    query_places = lax.broadcasted_iota(jnp.int32, (1, rows), 1)

    @pl.loop(info[0] + 1, count)
    def _(j):
        sums[slot_of(j, info[0], order)] = jnp.zeros((rows, 2 * width), bf16)

    for copy in copies:
        copy.wait()
    for part in range(per):
        span = slice(part * tile, (part + 1) * tile)
        pieces = range(part * (tile // piece), (part + 1) * (tile // piece))
        go_all = jnp.concatenate(
            [go_ref[z, :, first : first + piece] for z in pieces], axis=1
        )
        deltas = []
        for h in range(heads):
            lanes = slice(h * HEAD, (h + 1) * HEAD)
            deltas.append(
                jnp.sum(go_all[lanes].astype(f32) * out_ref[lanes, span], axis=0, keepdims=True)
            )

        def step(slot, key_part, masked, start):
            keys_at = slice(key_part * tile, (key_part + 1) * tile)
            allowed = key_places[keys_at] <= query_places[:, span] if masked else None
            for h in range(heads):
                lanes = slice(h * HEAD, (h + 1) * HEAD)
                lanes_v = slice(width + h * HEAD, width + (h + 1) * HEAD)
                q = q_ref[span, lanes]
                go = go_all[lanes]
                k = held[slot, keys_at, lanes]
                v = held[slot, keys_at, lanes_v]
                p = jnp.exp2(dot(k, q, ((1,), (1,))) * EXP2_SCALE - lse_ref[h, :, span])
                if masked:
                    p = jnp.where(allowed, p, 0.0)
                pulled = dot(v, go, ((1,), (0,)))
                slopes = (p * (pulled - deltas[h])).astype(bf16)
                dv = dot(p.astype(bf16), go, ((1,), (1,)))
                dk = dot(slopes, q, ((1,), (0,))) * 0.125
                if part:
                    dk = dk + sums[slot, keys_at, lanes].astype(f32)
                    dv = dv + sums[slot, keys_at, lanes_v].astype(f32)
                sums[slot, keys_at, lanes] = dk.astype(bf16)
                sums[slot, keys_at, lanes_v] = dv.astype(bf16)
                dq = dot(k, slopes, ((0,), (0,)))
                if start:
                    acc_ref[h] = dq
                else:
                    acc_ref[h] += dq

        for key_part in range(per):
            step(slot_of(info[0], info[0], order), key_part, True, key_part == 0)

        @pl.loop(0, info[0])
        def _(j):
            for key_part in range(per):
                step(slot_of(j, info[0], order), key_part, False, False)

        for h in range(heads):
            dq_ref[span, h * HEAD : (h + 1) * HEAD] = (acc_ref[h] * 0.125).T.astype(bf16)
    copies = []
    base = 0
    for i, ref in enumerate((near_ref, middle_ref, far_ref)):
        copies.append(
            pltpu.make_async_copy(sums.at[pl.ds(base, ref.shape[0])], ref, end_sems.at[i])
        )
        base += ref.shape[0]
    for copy in copies:
        copy.start()
    for copy in copies:
        copy.wait()


SMEM = pl.BlockSpec(memory_space=pltpu.SMEM)
VMEM = pl.BlockSpec(memory_space=pltpu.VMEM)
ANY = pl.BlockSpec(memory_space=pl.ANY)


def attend(shards, order, info, queries, blocks):
    rows, width = queries.shape
    heads = width // HEAD
    count = 4 * blocks[0].shape[0]
    tile = min(TILE, rows)
    scores = heads * rows * rows * (count + 1) // 2
    return pl.pallas_call(
        functools.partial(forward_kernel, heads, shards, order),
        out_shape=(
            jax.ShapeDtypeStruct((shards, width, rows // shards), bf16),
            jax.ShapeDtypeStruct((width, rows), f32),
            jax.ShapeDtypeStruct((heads, 1, rows), f32),
        ),
        in_specs=[SMEM, VMEM] + [ANY] * 4,
        out_specs=(VMEM, VMEM, VMEM),
        scratch_shapes=[
            pltpu.VMEM((count, rows, 2 * width), bf16),
            pltpu.SemaphoreType.DMA((4,)),
            pltpu.VMEM((heads, 1, tile), f32),
            pltpu.VMEM((heads, 1, tile), f32),
            pltpu.VMEM((heads, HEAD, tile), f32),
        ],
        compiler_params=pltpu.CompilerParams(vmem_limit_bytes=VMEM_LIMIT),
        cost_estimate=pl.CostEstimate(
            flops=scores * 16 * HEAD,
            bytes_accessed=4 * rows * width * (count + 2),
            transcendentals=scores,
        ),
        name="attention_forward",
    )(info, queries, *blocks)


def attend_back(shards, order, first, info, queries, out, lse, grads, blocks):
    rows, width = queries.shape
    heads = width // HEAD
    count = 4 * blocks[0].shape[0]
    tile = min(TILE, rows)
    scores = heads * rows * rows * (count + 1) // 2
    return pl.pallas_call(
        functools.partial(backward_kernel, heads, shards, order, first),
        out_shape=[jax.ShapeDtypeStruct((rows, width), bf16)]
        + [
            jax.ShapeDtypeStruct((share, rows, 2 * width), bf16)
            for share in (count // 4, count // 4, count // 2)
        ],
        in_specs=[SMEM] + [VMEM] * 4 + [ANY] * 4,
        out_specs=[VMEM] + [ANY] * 3,
        scratch_shapes=[
            pltpu.VMEM((count, rows, 2 * width), bf16),
            pltpu.VMEM((count, rows, 2 * width), bf16),
            pltpu.SemaphoreType.DMA((4,)),
            pltpu.SemaphoreType.DMA((3,)),
            pltpu.VMEM((heads, HEAD, tile), f32),
        ],
        compiler_params=pltpu.CompilerParams(vmem_limit_bytes=VMEM_LIMIT),
        cost_estimate=pl.CostEstimate(
            flops=scores * 10 * HEAD,
            bytes_accessed=8 * rows * width * (count + 2),
            transcendentals=scores,
        ),
        name="attention_backward",
    )(info, queries, out, lse, grads, *blocks)


def body(
    layer_input,
    attn_gain,
    attn_shift,
    qkv_weight,
    query_bias,
    value_bias,
    proj_weight,
    proj_bias,
    mlp_gain,
    mlp_shift,
    fc_weight,
    fc_bias,
    out_weight,
    out_bias,
    grad_output,
):
    seqs, piece, width = layer_input.shape
    cycle = lax.axis_size("ctx")
    shards = lax.axis_size("shard")
    here = lax.axis_index("ctx")
    shard_at = lax.axis_index("shard")
    odd = here & 1
    chip_bits = list(range(1, cycle.bit_length() - 1))
    rows = shards * piece
    local_width = qkv_weight.shape[0]
    local_hidden = out_weight.shape[0]
    half_width = local_width // 2
    half_hidden = local_hidden // 2
    quarter = half_hidden // 2
    group = -(-HEADS // shards) * HEAD
    padded = group * shards
    late = [seq >= (seqs + 1) // 2 for seq in range(seqs)]
    tokens = seqs * piece


    def mirror_late(held):
        return jnp.stack([mirrored(held[s]) if late[s] else held[s] for s in range(seqs)])

    layer_input = mirror_late(layer_input)

    def by_heads(weight):
        parts = []
        for third in range(3):
            part = weight[:, third * width : (third + 1) * width]
            parts.append(jnp.pad(part, ((0, 0), (0, padded - width))))
        return jnp.stack(
            [
                jnp.concatenate([part[:, z * group : (z + 1) * group] for part in parts], axis=1)
                for z in range(shards)
            ]
        )

    joins = chip_bits[::-1] + [0]
    share = local_width // cycle
    weight_share = lax.dynamic_slice_in_dim(
        qkv_weight, sum(((here >> bit) & 1) << k for k, bit in enumerate(joins)) * share, share, 0
    )
    packed = jnp.concatenate(
        [
            jnp.stack(
                [attn_gain, attn_shift, query_bias, value_bias, proj_bias, mlp_gain, mlp_shift, out_bias]
            ),
            fc_bias.reshape(-1, local_width),
        ]
    )
    vector_rows = packed.shape[0]
    packed = jnp.pad(packed, ((0, 16 - vector_rows), (0, 3 * group - local_width)))
    moved = jnp.concatenate(
        [by_heads(weight_share), jnp.broadcast_to(packed, (shards,) + packed.shape)], axis=1
    )
    layer_input, grad_output, moved = lax.optimization_barrier((layer_input, grad_output, moved))
    grad_output = mirror_late(grad_output)
    gathered = lax.all_gather(layer_input, "shard", axis=0)
    moved = lax.all_to_all(moved, "shard", 0, 0, tiled=True)
    small = moved[:, share : share + vector_rows, :local_width].astype(f32)
    qkv_own = moved[:, :share]
    for bit in joins:
        if bit == 0:
            qkv_own, grad_output, _ = lax.optimization_barrier((qkv_own, grad_output, gathered))
        qkv_own = jnp.concatenate(joined(qkv_own, bit, (here >> bit) & 1), axis=1)
    qkv_own = qkv_own.reshape(width, 3 * group)
    q_weight = qkv_own[:, :group]
    kv_weight = qkv_own[:, group:]

    vectors = [small[:, i].reshape(-1) for i in range(8)]
    gain_one, shift_one, query_add, value_add, proj_add, gain_two, shift_two, out_add = vectors
    bias_rows = half_hidden // local_width
    fc_add = lax.dynamic_slice_in_dim(small, 8 + odd * bias_rows, bias_rows, 1).reshape(-1)

    def own_heads(vector):
        return lax.dynamic_slice_in_dim(
            jnp.pad(vector, (0, padded - width)), shard_at * group, group, 0
        )

    kv_add = jnp.concatenate([jnp.zeros((group,), f32), own_heads(value_add)])
    query_add = own_heads(query_add)

    fc_side = (here >> FC_BIT) & 1
    out_side = (here >> OUT_BIT) & 1
    proj_half = lax.dynamic_slice_in_dim(proj_weight, odd * half_width, half_width, 0)
    fc_quarter = jnp.concatenate(
        [
            lax.dynamic_slice_in_dim(
                fc_weight,
                (fc_side * (shards // 2) + z) * local_hidden + odd * half_hidden,
                half_hidden,
                1,
            )
            for z in range(shards // 2)
        ],
        axis=1,
    )
    out_quarter = lax.dynamic_slice_in_dim(
        out_weight, odd * half_hidden + out_side * quarter, quarter, 0
    )
    weights = lax.all_gather(
        jnp.concatenate([proj_half, fc_quarter, out_quarter]), "shard", axis=0
    )

    orders = [chip_bits + [0], chip_bits[::-1] + [0]]
    orders = [orders[s % 2] for s in range(seqs)]
    group_norms, normed_one, own_blocks, queries, infos = [], [], [], [], []
    for s in range(seqs):
        norm = normalized(gathered[:, s].reshape(rows, width).astype(f32))
        normed = (norm * gain_one + shift_one).astype(bf16)
        group_norms.append(norm)
        normed_one.append(normed)
        own_blocks.append((dot(normed, kv_weight, ((1,), (0,))) + kv_add).astype(bf16))
        queries.append((dot(normed, q_weight, ((1,), (0,))) + query_add).astype(bf16))
        infos.append(jnp.reshape(cycle - 1 - here if late[s] else here, (1,)).astype(jnp.int32))
    spreads = [spread(own_blocks[s], orders[s], late[s], queries) for s in range(seqs)]
    blocks = [blocks for blocks, _ in spreads]
    aparts = [apart for _, apart in spreads]
    saved = [None] * seqs
    attended_parts = [None] * seqs
    for s in reversed(range(seqs)):
        attended_parts[s], *saved[s] = attend(shards, orders[s], infos[s], queries[s], blocks[s])
    attended, weights = lax.optimization_barrier(
        (jnp.concatenate(attended_parts, axis=2), weights)
    )
    cut = half_width + local_width
    proj_half, fc_quarter, out_quarter = lax.optimization_barrier(
        (weights[:, :half_width], weights[:, half_width:cut], weights[:, cut:])
    )
    proj_half = pair_joined(proj_half, odd)
    proj_full = jnp.stack(proj_half, axis=1).reshape(width, width)
    fc_quarter = fc_quarter.reshape(width, -1)
    fc_half = jnp.concatenate(joined(fc_quarter, FC_BIT, fc_side), axis=1)
    out_half = jnp.stack(joined(out_quarter, OUT_BIT, out_side), axis=1).reshape(-1, width)
    attended = lax.all_to_all(attended, "shard", 0, 0, tiled=True).reshape(padded, tokens)[:width]

    inputs32 = layer_input.reshape(tokens, width).astype(f32)
    grads_own = grad_output.reshape(tokens, width)
    grads32 = grads_own.astype(f32)
    attended, fc_half = lax.optimization_barrier((attended, fc_half))
    middle = inputs32 + dot(attended, proj_full, ((0,), (0,))) + proj_add
    normed_two = layer_norm(middle, gain_two, shift_two).astype(bf16)

    normed_pair = jnp.concatenate([normed_two, swapped(normed_two, 0)])
    grads_pair = jnp.concatenate([grads_own, swapped(grads_own, 0)])
    preactivation = dot(normed_pair, fc_half, ((1,), (0,))) + fc_add
    hidden = gelu_tanh(preactivation).astype(bf16)
    out_part = dot(hidden, out_half, ((1,), (0,)))
    layer_output = middle + (out_part[:tokens] + swapped(out_part[tokens:], 0)) + out_add
    layer_output = layer_output.astype(bf16)
    grad_hidden = dot(grads_pair, out_half, ((1,), (1,)))
    grad_pre = jax.vjp(gelu_tanh, preactivation)[1](grad_hidden)[0].astype(bf16)
    normed_part = dot(grad_pre, fc_half, ((1,), (1,)))
    grad_normed_two = normed_part[:tokens] + swapped(normed_part[tokens:], 0)
    grad_mid_part, gain_two_grad, shift_two_grad = jax.vjp(
        layer_norm, middle, gain_two, shift_two
    )[1](grad_normed_two)
    grad_middle = grads32 + grad_mid_part
    grad_branch = grad_middle.astype(bf16)

    grad_attended = jnp.pad(
        dot(proj_full, grad_branch, ((1,), (1,))).astype(bf16), ((0, padded - width), (0, 0))
    ).reshape(shards, group, tokens)
    grad_heads = lax.all_to_all(grad_attended, "shard", 0, 0, tiled=True)
    flat = ((0,), (0,))

    def parted(first, second, side):
        return jnp.where(side, second, first), jnp.where(side, first, second)

    hidden, normed_pair, attended = [
        after(held, grad_attended) for held in (hidden, normed_pair, attended)
    ]
    proj_grad = dot(attended, grad_branch, ((1,), (0,))).astype(bf16)
    proj_grad = proj_grad.reshape(shards, 2, half_width, width)
    mine, sent = parted(proj_grad[:, 0], proj_grad[:, 1], odd)
    proj_grad = added(mine, swapped(sent, 0))
    fc_grad = dot(normed_pair, grad_pre, flat).astype(bf16).reshape(shards, local_width, -1)
    column = fc_grad.shape[2] // 2
    fc_mine, fc_sent = parted(
        jnp.concatenate([fc_grad[..., :column], proj_grad[:, : half_width // 2]], axis=1),
        jnp.concatenate([fc_grad[..., column:], proj_grad[:, half_width // 2 :]], axis=1),
        fc_side,
    )
    out_grad = dot(hidden, grads_pair, flat).astype(bf16).reshape(shards, 2, quarter, width)
    out_mine, out_sent = parted(out_grad[:, 0], out_grad[:, 1], out_side)
    fc_received = swapped(fc_sent, FC_BIT)
    out_received = swapped(out_sent, OUT_BIT)

    query_low = [None] * seqs
    kv_parts = [None] * seqs
    grad_heads = after(grad_heads, fc_sent, out_sent)
    for s in range(seqs):
        query_low[s], *kv_parts[s] = attend_back(
            shards, orders[s], s * piece, infos[s], queries[s], *saved[s], grad_heads, blocks[s]
        )

    ended = [parts[0] for parts in kv_parts]
    scattered = jnp.concatenate(
        [added(fc_mine, after(fc_received, *ended)), added(out_mine, after(out_received, *ended))],
        axis=1,
    )
    both = lax.psum_scatter(scattered, "shard", scatter_dimension=0, tiled=False)

    kv_low = [None] * seqs
    normed_parts = []
    gain_one_grad = jnp.zeros((width,), f32)
    shift_one_grad = jnp.zeros((width,), f32)
    for s in range(seqs):
        kv_low[s] = returned(*kv_parts[s], aparts[s], orders[s], late[s], [scattered])
        part = dot(query_low[s], q_weight, ((1,), (1,))) + dot(kv_low[s], kv_weight, ((1,), (1,)))
        gain_one_grad = gain_one_grad + jnp.sum(part * group_norms[s], axis=0)
        shift_one_grad = shift_one_grad + jnp.sum(part, axis=0)
        normed_parts.append(part.astype(bf16).reshape(shards, piece, width))
    fc_add_part = jnp.sum(grad_pre.astype(f32), axis=0).reshape(shards, 1, half_hidden)
    fc_add_part = jnp.where(jnp.arange(2)[None, :, None] == odd, fc_add_part, 0.0)

    def all_heads(vector):
        own = jnp.arange(shards)[:, None] == shard_at
        return jnp.where(own, vector[None, :], 0.0).reshape(padded)[:width]

    query_sum = sum(jnp.sum(low.astype(f32), axis=0) for low in query_low)
    value_sum = sum(jnp.sum(low[:, group:].astype(f32), axis=0) for low in kv_low)
    vectors = [
        gain_one_grad,
        shift_one_grad,
        all_heads(query_sum),
        all_heads(value_sum),
        jnp.sum(grad_branch.astype(f32), axis=0),
        gain_two_grad,
        shift_two_grad,
        jnp.sum(grads32, axis=0),
    ]
    vectors = jnp.concatenate(
        [vector.reshape(shards, 1, local_width) for vector in vectors]
        + [fc_add_part.reshape(shards, -1, local_width)],
        axis=1,
    ).astype(bf16)
    vectors = jnp.pad(vectors, ((0, 0), (0, 16 - vector_rows), (0, width - local_width)))
    vectors = lax.dynamic_update_slice(
        vectors, jnp.broadcast_to(both[:1, :1], (shards, 1, 1)), (0, 15, 0)
    )
    normed_parts = jnp.concatenate(normed_parts + [vectors], axis=1)
    summed = lax.psum_scatter(normed_parts, "shard", scatter_dimension=0, tiled=False).astype(f32)
    pull = jax.vjp(lambda v: normalized(v) * gain_one, inputs32)[1]
    input_grad = (grad_middle + pull(summed[:tokens])[0]).astype(bf16)
    sums = summed[tokens : tokens + vector_rows, :local_width]
    sums = sums + swapped(sums, 0)
    sums = after(sums, input_grad)
    for bit in chip_bits:
        sums = sums + swapped(sums, bit)

    results = jnp.stack(
        [part.reshape(seqs, piece, width) for part in (layer_output, input_grad)], axis=1
    )
    results = [mirrored(results[s]) if late[s] else results[s] for s in range(seqs)]

    cut = both.shape[0] - quarter
    out_grad = summed_over_chips(both[cut:], [bit for bit in chip_bits if bit != OUT_BIT])
    out_grad = jnp.concatenate(joined(out_grad.astype(bf16), OUT_BIT, out_side))
    out_grad = after(out_grad, summed)
    out_grad = jnp.concatenate(pair_joined(out_grad, odd)).astype(f32)
    rest = summed_over_chips(both[:cut], [bit for bit in chip_bits if bit != FC_BIT])
    first, second = joined(rest.astype(bf16), FC_BIT, fc_side)
    first, second = after(first, summed), after(second, summed)
    proj_grad = jnp.concatenate([first[local_width:], second[local_width:]])
    proj_grad = jnp.concatenate(pair_joined(proj_grad, odd)).astype(f32)
    fc_grad = jnp.concatenate([first[:local_width], second[:local_width]], axis=1)
    fc_halves = pair_joined(fc_grad, odd)
    fc_grad = jnp.concatenate(
        [
            fc_halves[h][:, z * half_hidden : (z + 1) * half_hidden]
            for z in range(shards)
            for h in range(2)
        ],
        axis=1,
    ).astype(f32)

    grad = []
    for s in range(seqs):
        normed = after(normed_one[s], normed_parts)
        low = jnp.concatenate([query_low[s], kv_low[s]], axis=1)
        grad.append(dot(normed, low, flat))
    grad = sum(grad).astype(bf16).reshape(shards, local_width, -1)
    for bit in joins[::-1]:
        cut = grad.shape[1] // 2
        mine, sent = parted(grad[:, :cut], grad[:, cut:], (here >> bit) & 1)
        grad = added(mine, swapped(sent, bit))
    grad = lax.all_to_all(grad, "shard", 0, 0, tiled=True)
    grad = jnp.concatenate([grad[z] for z in range(shards)], axis=1)
    for turn, bit in enumerate(joins):
        if turn == 1:
            grad = after(grad, summed)
        grad = jnp.concatenate(joined(grad, bit, (here >> bit) & 1))
    thirds = [
        jnp.concatenate(
            [
                grad[:, (3 * z + third) * group : (3 * z + third + 1) * group]
                for z in range(shards)
            ],
            axis=1,
        )[:, :width]
        for third in range(3)
    ]
    qkv_grad = jnp.concatenate(thirds, axis=1).astype(f32)

    return (
        jnp.stack([part[0] for part in results]),
        jnp.stack([part[1] for part in results]),
        sums[0],
        sums[1],
        qkv_grad,
        sums[2],
        sums[3],
        proj_grad,
        sums[4],
        sums[5],
        sums[6],
        fc_grad,
        sums[8:].reshape(-1),
        out_grad,
        sums[7],
    )


def solution(mesh):
    tokens = P(None, ("ctx", "shard"), None)
    vector = P("shard")
    matrix = P("shard", None)
    return jax.shard_map(
        body,
        mesh=mesh,
        in_specs=(
            tokens,
            vector,
            vector,
            matrix,
            vector,
            vector,
            matrix,
            vector,
            vector,
            vector,
            matrix,
            vector,
            matrix,
            vector,
            tokens,
        ),
        out_specs=(
            tokens,
            tokens,
            vector,
            vector,
            matrix,
            vector,
            vector,
            matrix,
            vector,
            vector,
            vector,
            matrix,
            vector,
            matrix,
            vector,
        ),
        check_vma=False,
    )
```

```python
import functools

import jax
import jax.numpy as jnp
from jax import lax
from jax.experimental import pallas as pl
from jax.experimental.pallas import tpu as pltpu
from jax.sharding import PartitionSpec as P

HEADS = 12
HEAD = 64
TILE = 512
EXP2_SCALE = 0.125 * 1.4426950408889634
f32 = jnp.float32
bf16 = jnp.bfloat16
FC_BIT = 1
OUT_BIT = 2
VMEM_LIMIT = 56 * 1024 * 1024


def normalized(values):
    centered = values - jnp.mean(values, axis=-1, keepdims=True)
    variance = jnp.mean(centered * centered, axis=-1, keepdims=True)
    return centered * lax.rsqrt(variance + 1e-05)


def layer_norm(values, gain, shift):
    return normalized(values) * gain + shift


def gelu_tanh(values):
    return jax.nn.gelu(values, approximate=True)


def swapped(block, bit):
    n = lax.axis_size("ctx")
    return lax.ppermute(block, "ctx", [(i, i ^ (1 << bit)) for i in range(n)])


def tree_pairs(aparts, bit, later, late, back):
    n = lax.axis_size("ctx")
    reach = [0]
    for other in later:
        reach += [r ^ (1 << other) for r in reach]
    place = (lambda i: n - 1 - i) if late else (lambda i: i)
    pairs = []
    for i in range(n):
        target = i ^ (1 << bit)
        if any(place(i ^ apart) <= place(target ^ r) for r in reach for apart in aparts):
            pairs.append((target, i) if back else (i, target))
    return pairs


def spread(own, order, late, before):
    held, aparts = own[None], [0]
    for bit in order[:-2]:
        pairs = tree_pairs(aparts, bit, order[order.index(bit) + 1 :], late, False)
        held = jnp.concatenate([held, lax.ppermute(held, "ctx", pairs)])
        aparts = aparts + [apart ^ (1 << bit) for apart in aparts]
    bit = order[-2]
    held = after(held, *before)
    received = lax.ppermute(held, "ctx", tree_pairs(aparts, bit, order[-1:], late, False))
    aparts = aparts + [apart ^ (1 << bit) for apart in aparts]
    blocks = [held, received, swapped(held, 0), swapped(received, 0)]
    return blocks, aparts + [apart ^ 1 for apart in aparts]


def added(first, second):
    return (first.astype(f32) + second.astype(f32)).astype(bf16)


def returned(near, middle, far, aparts, order, late, before):
    received = swapped(far, 0)
    count = near.shape[0]
    middle = added(middle, received[count:])
    pairs = tree_pairs(aparts[:count], order[-2], order[-1:], late, True)
    near = added(added(near, received[:count]), lax.ppermute(middle, "ctx", pairs))
    for bit in order[:-2][::-1]:
        count = near.shape[0] // 2
        pairs = tree_pairs(aparts[:count], bit, order[order.index(bit) + 1 :], late, True)
        sent = after(near[count:], *before)
        near = added(near[:count], lax.ppermute(sent, "ctx", pairs))
    return near[0]


def after(value, *others):
    return lax.optimization_barrier((value,) + others)[0]


def mirrored(block):
    n = lax.axis_size("ctx")
    return lax.ppermute(block, "ctx", [(i, n - 1 - i) for i in range(n)])


def shifted(block, distance):
    n = lax.axis_size("shard")
    return lax.ppermute(block, "shard", [(i, (i + distance) % n) for i in range(n)])


def dot(a, b, contract):
    return lax.dot_general(a, b, ((contract[0], contract[1]), ((), ())), preferred_element_type=f32)


def summed_over_chips(part, bits):
    for bit in bits:
        low = part.astype(bf16)
        part = low.astype(f32) + swapped(low, bit).astype(f32)
    return part


def joined(half, bit, side):
    other = swapped(half, bit)
    return jnp.where(side, other, half), jnp.where(side, half, other)


def pair_joined(half, odd):
    return joined(half, 0, odd)


def load_blocks(refs, held, sems):
    each = refs[0].shape[0]
    copies = [
        pltpu.make_async_copy(ref, held.at[pl.ds(i * each, each)], sems.at[i])
        for i, ref in enumerate(refs)
    ]
    for copy in copies:
        copy.start()
    return copies


def slot_of(place, here, order):
    apart = place ^ here
    return sum(((apart >> bit) & 1) << k for k, bit in enumerate(order))


def forward_kernel(heads, shards, order, info, q_ref, *refs):
    kv_refs = refs[:4]
    att_ref, out_ref, lse_ref, held, sems, m_ref, l_ref, acc_ref = refs[4:]
    rows, width = q_ref.shape
    piece = rows // shards
    tile = min(TILE, rows)
    per = rows // tile
    copies = load_blocks(kv_refs, held, sems)
    key_places = lax.broadcasted_iota(jnp.int32, (rows, 1), 0)
    query_places = lax.broadcasted_iota(jnp.int32, (1, rows), 1)
    for copy in copies:
        copy.wait()
    for part in range(per):
        span = slice(part * tile, (part + 1) * tile)

        def step(slot, key_part, masked, start):
            keys_at = slice(key_part * tile, (key_part + 1) * tile)
            allowed = key_places[keys_at] <= query_places[:, span] if masked else None
            for h in range(heads):
                lanes = slice(h * HEAD, (h + 1) * HEAD)
                lanes_v = slice(width + h * HEAD, width + (h + 1) * HEAD)
                q = q_ref[span, lanes]
                k = held[slot, keys_at, lanes]
                v = held[slot, keys_at, lanes_v]
                s = dot(k, q, ((1,), (1,))) * EXP2_SCALE
                if masked:
                    s = jnp.where(allowed, s, -1e30)
                m = jnp.max(s, axis=0, keepdims=True)
                if start:
                    p = jnp.exp2(s - m)
                    l_ref[h] = jnp.sum(p, axis=0, keepdims=True)
                    acc_ref[h] = dot(v, p.astype(bf16), ((0,), (0,)))
                else:
                    old = m_ref[h]
                    m = jnp.maximum(old, m)
                    p = jnp.exp2(s - m)
                    factor = jnp.exp2(old - m)
                    l_ref[h] = l_ref[h] * factor + jnp.sum(p, axis=0, keepdims=True)
                    acc_ref[h] = acc_ref[h] * factor + dot(v, p.astype(bf16), ((0,), (0,)))
                m_ref[h] = m

        for key_part in range(per):
            step(slot_of(info[0], info[0], order), key_part, True, key_part == 0)

        @pl.loop(0, info[0])
        def _(j):
            for key_part in range(per):
                step(slot_of(j, info[0], order), key_part, False, False)

        for h in range(heads):
            total = l_ref[h]
            done = acc_ref[h] / total
            out_ref[h * HEAD : (h + 1) * HEAD, span] = done
            lse_ref[h, :, span] = m_ref[h] + jnp.log2(total)
            low = done.astype(bf16)
            for z in range(tile // piece):
                att_ref[part * (tile // piece) + z, h * HEAD : (h + 1) * HEAD, :] = low[
                    :, z * piece : (z + 1) * piece
                ]


def backward_kernel(heads, shards, order, first, info, q_ref, out_ref, lse_ref, go_ref, *refs):
    kv_refs = refs[:4]
    dq_ref, near_ref, middle_ref, far_ref, held, sums, sems, end_sems, acc_ref = refs[4:]
    count = held.shape[0]
    rows, width = q_ref.shape
    piece = rows // shards
    tile = min(TILE, rows)
    per = rows // tile
    copies = load_blocks(kv_refs, held, sems)
    key_places = lax.broadcasted_iota(jnp.int32, (rows, 1), 0)
    query_places = lax.broadcasted_iota(jnp.int32, (1, rows), 1)

    @pl.loop(info[0] + 1, count)
    def _(j):
        sums[slot_of(j, info[0], order)] = jnp.zeros((rows, 2 * width), bf16)

    for copy in copies:
        copy.wait()
    for part in range(per):
        span = slice(part * tile, (part + 1) * tile)
        pieces = range(part * (tile // piece), (part + 1) * (tile // piece))
        go_all = jnp.concatenate(
            [go_ref[z, :, first : first + piece] for z in pieces], axis=1
        )
        deltas = []
        for h in range(heads):
            lanes = slice(h * HEAD, (h + 1) * HEAD)
            deltas.append(
                jnp.sum(go_all[lanes].astype(f32) * out_ref[lanes, span], axis=0, keepdims=True)
            )

        def step(slot, key_part, masked, start):
            keys_at = slice(key_part * tile, (key_part + 1) * tile)
            allowed = key_places[keys_at] <= query_places[:, span] if masked else None
            for h in range(heads):
                lanes = slice(h * HEAD, (h + 1) * HEAD)
                lanes_v = slice(width + h * HEAD, width + (h + 1) * HEAD)
                q = q_ref[span, lanes]
                go = go_all[lanes]
                k = held[slot, keys_at, lanes]
                v = held[slot, keys_at, lanes_v]
                p = jnp.exp2(dot(k, q, ((1,), (1,))) * EXP2_SCALE - lse_ref[h, :, span])
                if masked:
                    p = jnp.where(allowed, p, 0.0)
                pulled = dot(v, go, ((1,), (0,)))
                slopes = (p * (pulled - deltas[h])).astype(bf16)
                dv = dot(p.astype(bf16), go, ((1,), (1,)))
                dk = dot(slopes, q, ((1,), (0,))) * 0.125
                if part:
                    dk = dk + sums[slot, keys_at, lanes].astype(f32)
                    dv = dv + sums[slot, keys_at, lanes_v].astype(f32)
                sums[slot, keys_at, lanes] = dk.astype(bf16)
                sums[slot, keys_at, lanes_v] = dv.astype(bf16)
                dq = dot(k, slopes, ((0,), (0,)))
                if start:
                    acc_ref[h] = dq
                else:
                    acc_ref[h] += dq

        for key_part in range(per):
            step(slot_of(info[0], info[0], order), key_part, True, key_part == 0)

        @pl.loop(0, info[0])
        def _(j):
            for key_part in range(per):
                step(slot_of(j, info[0], order), key_part, False, False)

        for h in range(heads):
            dq_ref[span, h * HEAD : (h + 1) * HEAD] = (acc_ref[h] * 0.125).T.astype(bf16)
    copies = []
    base = 0
    for i, ref in enumerate((near_ref, middle_ref, far_ref)):
        copies.append(
            pltpu.make_async_copy(sums.at[pl.ds(base, ref.shape[0])], ref, end_sems.at[i])
        )
        base += ref.shape[0]
    for copy in copies:
        copy.start()
    for copy in copies:
        copy.wait()


SMEM = pl.BlockSpec(memory_space=pltpu.SMEM)
VMEM = pl.BlockSpec(memory_space=pltpu.VMEM)
ANY = pl.BlockSpec(memory_space=pl.ANY)


def attend(shards, order, info, queries, blocks):
    rows, width = queries.shape
    heads = width // HEAD
    count = 4 * blocks[0].shape[0]
    tile = min(TILE, rows)
    scores = heads * rows * rows * (count + 1) // 2
    return pl.pallas_call(
        functools.partial(forward_kernel, heads, shards, order),
        out_shape=(
            jax.ShapeDtypeStruct((shards, width, rows // shards), bf16),
            jax.ShapeDtypeStruct((width, rows), f32),
            jax.ShapeDtypeStruct((heads, 1, rows), f32),
        ),
        in_specs=[SMEM, VMEM] + [ANY] * 4,
        out_specs=(VMEM, VMEM, VMEM),
        scratch_shapes=[
            pltpu.VMEM((count, rows, 2 * width), bf16),
            pltpu.SemaphoreType.DMA((4,)),
            pltpu.VMEM((heads, 1, tile), f32),
            pltpu.VMEM((heads, 1, tile), f32),
            pltpu.VMEM((heads, HEAD, tile), f32),
        ],
        compiler_params=pltpu.CompilerParams(vmem_limit_bytes=VMEM_LIMIT),
        cost_estimate=pl.CostEstimate(
            flops=scores * 16 * HEAD,
            bytes_accessed=4 * rows * width * (count + 2),
            transcendentals=scores,
        ),
        name="attention_forward",
    )(info, queries, *blocks)


def attend_back(shards, order, first, info, queries, out, lse, grads, blocks):
    rows, width = queries.shape
    heads = width // HEAD
    count = 4 * blocks[0].shape[0]
    tile = min(TILE, rows)
    scores = heads * rows * rows * (count + 1) // 2
    return pl.pallas_call(
        functools.partial(backward_kernel, heads, shards, order, first),
        out_shape=[jax.ShapeDtypeStruct((rows, width), bf16)]
        + [
            jax.ShapeDtypeStruct((share, rows, 2 * width), bf16)
            for share in (count // 4, count // 4, count // 2)
        ],
        in_specs=[SMEM] + [VMEM] * 4 + [ANY] * 4,
        out_specs=[VMEM] + [ANY] * 3,
        scratch_shapes=[
            pltpu.VMEM((count, rows, 2 * width), bf16),
            pltpu.VMEM((count, rows, 2 * width), bf16),
            pltpu.SemaphoreType.DMA((4,)),
            pltpu.SemaphoreType.DMA((3,)),
            pltpu.VMEM((heads, HEAD, tile), f32),
        ],
        compiler_params=pltpu.CompilerParams(vmem_limit_bytes=VMEM_LIMIT),
        cost_estimate=pl.CostEstimate(
            flops=scores * 10 * HEAD,
            bytes_accessed=8 * rows * width * (count + 2),
            transcendentals=scores,
        ),
        name="attention_backward",
    )(info, queries, out, lse, grads, *blocks)


def body(
    layer_input,
    attn_gain,
    attn_shift,
    qkv_weight,
    query_bias,
    value_bias,
    proj_weight,
    proj_bias,
    mlp_gain,
    mlp_shift,
    fc_weight,
    fc_bias,
    out_weight,
    out_bias,
    grad_output,
):
    seqs, piece, width = layer_input.shape
    cycle = lax.axis_size("ctx")
    shards = lax.axis_size("shard")
    here = lax.axis_index("ctx")
    shard_at = lax.axis_index("shard")
    odd = here & 1
    chip_bits = list(range(1, cycle.bit_length() - 1))
    rows = shards * piece
    local_width = qkv_weight.shape[0]
    local_hidden = out_weight.shape[0]
    half_width = local_width // 2
    half_hidden = local_hidden // 2
    quarter = half_hidden // 2
    group = -(-HEADS // shards) * HEAD
    padded = group * shards
    late = [seq >= (seqs + 1) // 2 for seq in range(seqs)]
    tokens = seqs * piece


    def mirror_late(held):
        return jnp.stack([mirrored(held[s]) if late[s] else held[s] for s in range(seqs)])

    layer_input = mirror_late(layer_input)

    def by_heads(weight):
        parts = []
        for third in range(3):
            part = weight[:, third * width : (third + 1) * width]
            parts.append(jnp.pad(part, ((0, 0), (0, padded - width))))
        return jnp.stack(
            [
                jnp.concatenate([part[:, z * group : (z + 1) * group] for part in parts], axis=1)
                for z in range(shards)
            ]
        )

    joins = chip_bits[::-1] + [0]
    share = local_width // cycle
    weight_share = lax.dynamic_slice_in_dim(
        qkv_weight, sum(((here >> bit) & 1) << k for k, bit in enumerate(joins)) * share, share, 0
    )
    packed = jnp.concatenate(
        [
            jnp.stack(
                [attn_gain, attn_shift, query_bias, value_bias, proj_bias, mlp_gain, mlp_shift, out_bias]
            ),
            fc_bias.reshape(-1, local_width),
        ]
    )
    vector_rows = packed.shape[0]
    packed = jnp.pad(packed, ((0, 16 - vector_rows), (0, 3 * group - local_width)))
    moved = jnp.concatenate(
        [by_heads(weight_share), jnp.broadcast_to(packed, (shards,) + packed.shape)], axis=1
    )
    layer_input, grad_output, moved = lax.optimization_barrier((layer_input, grad_output, moved))
    grad_output = mirror_late(grad_output)
    gathered = lax.all_gather(layer_input, "shard", axis=0)
    moved = lax.all_to_all(moved, "shard", 0, 0, tiled=True)
    small = moved[:, share : share + vector_rows, :local_width].astype(f32)
    qkv_own = moved[:, :share]
    for bit in joins:
        if bit == 0:
            qkv_own, grad_output, _ = lax.optimization_barrier((qkv_own, grad_output, gathered))
        qkv_own = jnp.concatenate(joined(qkv_own, bit, (here >> bit) & 1), axis=1)
    qkv_own = qkv_own.reshape(width, 3 * group)
    q_weight = qkv_own[:, :group]
    kv_weight = qkv_own[:, group:]

    vectors = [small[:, i].reshape(-1) for i in range(8)]
    gain_one, shift_one, query_add, value_add, proj_add, gain_two, shift_two, out_add = vectors
    bias_rows = half_hidden // local_width
    fc_add = lax.dynamic_slice_in_dim(small, 8 + odd * bias_rows, bias_rows, 1).reshape(-1)

    def own_heads(vector):
        return lax.dynamic_slice_in_dim(
            jnp.pad(vector, (0, padded - width)), shard_at * group, group, 0
        )

    kv_add = jnp.concatenate([jnp.zeros((group,), f32), own_heads(value_add)])
    query_add = own_heads(query_add)

    fc_side = (here >> FC_BIT) & 1
    out_side = (here >> OUT_BIT) & 1
    proj_half = lax.dynamic_slice_in_dim(proj_weight, odd * half_width, half_width, 0)
    fc_quarter = jnp.concatenate(
        [
            lax.dynamic_slice_in_dim(
                fc_weight,
                (fc_side * (shards // 2) + z) * local_hidden + odd * half_hidden,
                half_hidden,
                1,
            )
            for z in range(shards // 2)
        ],
        axis=1,
    )
    out_quarter = lax.dynamic_slice_in_dim(
        out_weight, odd * half_hidden + out_side * quarter, quarter, 0
    )
    weights = lax.all_gather(
        jnp.concatenate([proj_half, fc_quarter, out_quarter]), "shard", axis=0
    )

    orders = [chip_bits + [0], chip_bits[::-1] + [0]]
    orders = [orders[s % 2] for s in range(seqs)]
    group_norms, normed_one, own_blocks, queries, infos = [], [], [], [], []
    for s in range(seqs):
        norm = normalized(gathered[:, s].reshape(rows, width).astype(f32))
        normed = (norm * gain_one + shift_one).astype(bf16)
        group_norms.append(norm)
        normed_one.append(normed)
        own_blocks.append((dot(normed, kv_weight, ((1,), (0,))) + kv_add).astype(bf16))
        queries.append((dot(normed, q_weight, ((1,), (0,))) + query_add).astype(bf16))
        infos.append(jnp.reshape(cycle - 1 - here if late[s] else here, (1,)).astype(jnp.int32))
    spreads = [spread(own_blocks[s], orders[s], late[s], queries) for s in range(seqs)]
    blocks = [blocks for blocks, _ in spreads]
    aparts = [apart for _, apart in spreads]
    saved = [None] * seqs
    attended_parts = [None] * seqs
    for s in reversed(range(seqs)):
        attended_parts[s], *saved[s] = attend(shards, orders[s], infos[s], queries[s], blocks[s])
    attended, weights = lax.optimization_barrier(
        (jnp.concatenate(attended_parts, axis=2), weights)
    )
    cut = half_width + local_width
    proj_half, fc_quarter, out_quarter = lax.optimization_barrier(
        (weights[:, :half_width], weights[:, half_width:cut], weights[:, cut:])
    )
    proj_half = pair_joined(proj_half, odd)
    proj_full = jnp.stack(proj_half, axis=1).reshape(width, width)
    fc_quarter = fc_quarter.reshape(width, -1)
    fc_half = jnp.concatenate(joined(fc_quarter, FC_BIT, fc_side), axis=1)
    out_half = jnp.stack(joined(out_quarter, OUT_BIT, out_side), axis=1).reshape(-1, width)
    attended = lax.all_to_all(attended, "shard", 0, 0, tiled=True).reshape(padded, tokens)[:width]

    inputs32 = layer_input.reshape(tokens, width).astype(f32)
    grads_own = grad_output.reshape(tokens, width)
    grads32 = grads_own.astype(f32)
    attended, fc_half = lax.optimization_barrier((attended, fc_half))
    middle = inputs32 + dot(attended, proj_full, ((0,), (0,))) + proj_add
    normed_two = layer_norm(middle, gain_two, shift_two).astype(bf16)

    normed_pair = jnp.concatenate([normed_two, swapped(normed_two, 0)])
    grads_pair = jnp.concatenate([grads_own, swapped(grads_own, 0)])
    preactivation = dot(normed_pair, fc_half, ((1,), (0,))) + fc_add
    hidden = gelu_tanh(preactivation).astype(bf16)
    out_part = dot(hidden, out_half, ((1,), (0,)))
    layer_output = middle + (out_part[:tokens] + swapped(out_part[tokens:], 0)) + out_add
    layer_output = layer_output.astype(bf16)
    grad_hidden = dot(grads_pair, out_half, ((1,), (1,)))
    grad_pre = jax.vjp(gelu_tanh, preactivation)[1](grad_hidden)[0].astype(bf16)
    normed_part = dot(grad_pre, fc_half, ((1,), (1,)))
    grad_normed_two = normed_part[:tokens] + swapped(normed_part[tokens:], 0)
    grad_mid_part, gain_two_grad, shift_two_grad = jax.vjp(
        layer_norm, middle, gain_two, shift_two
    )[1](grad_normed_two)
    grad_middle = grads32 + grad_mid_part
    grad_branch = grad_middle.astype(bf16)

    grad_attended = jnp.pad(
        dot(proj_full, grad_branch, ((1,), (1,))).astype(bf16), ((0, padded - width), (0, 0))
    ).reshape(shards, group, tokens)
    grad_heads = lax.all_to_all(grad_attended, "shard", 0, 0, tiled=True)
    flat = ((0,), (0,))

    def parted(first, second, side):
        return jnp.where(side, second, first), jnp.where(side, first, second)

    hidden, normed_pair, attended = [
        after(held, grad_attended) for held in (hidden, normed_pair, attended)
    ]
    proj_grad = dot(attended, grad_branch, ((1,), (0,))).astype(bf16)
    proj_grad = proj_grad.reshape(shards, 2, half_width, width)
    mine, sent = parted(proj_grad[:, 0], proj_grad[:, 1], odd)
    proj_grad = added(mine, swapped(sent, 0))
    fc_grad = dot(normed_pair, grad_pre, flat).astype(bf16).reshape(shards, local_width, -1)
    column = fc_grad.shape[2] // 2
    fc_mine, fc_sent = parted(
        jnp.concatenate([fc_grad[..., :column], proj_grad[:, : half_width // 2]], axis=1),
        jnp.concatenate([fc_grad[..., column:], proj_grad[:, half_width // 2 :]], axis=1),
        fc_side,
    )
    out_grad = dot(hidden, grads_pair, flat).astype(bf16).reshape(shards, 2, quarter, width)
    out_mine, out_sent = parted(out_grad[:, 0], out_grad[:, 1], out_side)
    fc_received = swapped(fc_sent, FC_BIT)
    out_received = swapped(out_sent, OUT_BIT)

    query_low = [None] * seqs
    kv_parts = [None] * seqs
    grad_heads = after(grad_heads, fc_sent, out_sent)
    for s in range(seqs):
        query_low[s], *kv_parts[s] = attend_back(
            shards, orders[s], s * piece, infos[s], queries[s], *saved[s], grad_heads, blocks[s]
        )

    ended = [parts[0] for parts in kv_parts]
    scattered = jnp.concatenate(
        [added(fc_mine, after(fc_received, *ended)), added(out_mine, after(out_received, *ended))],
        axis=1,
    )
    both = lax.psum_scatter(scattered, "shard", scatter_dimension=0, tiled=False)

    kv_low = [None] * seqs
    normed_parts = []
    gain_one_grad = jnp.zeros((width,), f32)
    shift_one_grad = jnp.zeros((width,), f32)
    for s in range(seqs):
        kv_low[s] = returned(*kv_parts[s], aparts[s], orders[s], late[s], [scattered])
        part = dot(query_low[s], q_weight, ((1,), (1,))) + dot(kv_low[s], kv_weight, ((1,), (1,)))
        gain_one_grad = gain_one_grad + jnp.sum(part * group_norms[s], axis=0)
        shift_one_grad = shift_one_grad + jnp.sum(part, axis=0)
        normed_parts.append(part.astype(bf16).reshape(shards, piece, width))
    fc_add_part = jnp.sum(grad_pre.astype(f32), axis=0).reshape(shards, 1, half_hidden)
    fc_add_part = jnp.where(jnp.arange(2)[None, :, None] == odd, fc_add_part, 0.0)

    def all_heads(vector):
        own = jnp.arange(shards)[:, None] == shard_at
        return jnp.where(own, vector[None, :], 0.0).reshape(padded)[:width]

    query_sum = sum(jnp.sum(low.astype(f32), axis=0) for low in query_low)
    value_sum = sum(jnp.sum(low[:, group:].astype(f32), axis=0) for low in kv_low)
    vectors = [
        gain_one_grad,
        shift_one_grad,
        all_heads(query_sum),
        all_heads(value_sum),
        jnp.sum(grad_branch.astype(f32), axis=0),
        gain_two_grad,
        shift_two_grad,
        jnp.sum(grads32, axis=0),
    ]
    vectors = jnp.concatenate(
        [vector.reshape(shards, 1, local_width) for vector in vectors]
        + [fc_add_part.reshape(shards, -1, local_width)],
        axis=1,
    ).astype(bf16)
    vectors = jnp.pad(vectors, ((0, 0), (0, 16 - vector_rows), (0, width - local_width)))
    vectors = lax.dynamic_update_slice(
        vectors, jnp.broadcast_to(both[:1, :1], (shards, 1, 1)), (0, 15, 0)
    )
    normed_parts = jnp.concatenate(normed_parts + [vectors], axis=1)
    summed = lax.psum_scatter(normed_parts, "shard", scatter_dimension=0, tiled=False).astype(f32)
    pull = jax.vjp(lambda v: normalized(v) * gain_one, inputs32)[1]
    input_grad = (grad_middle + pull(summed[:tokens])[0]).astype(bf16)
    sums = summed[tokens : tokens + vector_rows, :local_width]
    sums = sums + swapped(sums, 0)
    sums = after(sums, input_grad)
    for bit in chip_bits:
        sums = sums + swapped(sums, bit)

    results = jnp.stack(
        [part.reshape(seqs, piece, width) for part in (layer_output, input_grad)], axis=1
    )
    results = [mirrored(results[s]) if late[s] else results[s] for s in range(seqs)]

    cut = both.shape[0] - quarter
    out_grad = summed_over_chips(both[cut:], [bit for bit in chip_bits if bit != OUT_BIT])
    out_grad = jnp.concatenate(joined(out_grad.astype(bf16), OUT_BIT, out_side))
    out_grad = jnp.concatenate(pair_joined(out_grad, odd)).astype(f32)
    rest = summed_over_chips(both[:cut], [bit for bit in chip_bits if bit != FC_BIT])
    first, second = joined(rest.astype(bf16), FC_BIT, fc_side)
    proj_grad = jnp.concatenate([first[local_width:], second[local_width:]])
    proj_grad = jnp.concatenate(pair_joined(proj_grad, odd)).astype(f32)
    fc_grad = jnp.concatenate([first[:local_width], second[:local_width]], axis=1)
    fc_halves = pair_joined(fc_grad, odd)
    fc_grad = jnp.concatenate(
        [
            fc_halves[h][:, z * half_hidden : (z + 1) * half_hidden]
            for z in range(shards)
            for h in range(2)
        ],
        axis=1,
    ).astype(f32)

    grad = []
    for s in range(seqs):
        normed = after(normed_one[s], normed_parts)
        low = jnp.concatenate([query_low[s], kv_low[s]], axis=1)
        grad.append(dot(normed, low, flat))
    grad = sum(grad).astype(bf16).reshape(shards, local_width, -1)
    for bit in joins[::-1]:
        cut = grad.shape[1] // 2
        mine, sent = parted(grad[:, :cut], grad[:, cut:], (here >> bit) & 1)
        grad = added(mine, swapped(sent, bit))
    grad = lax.all_to_all(grad, "shard", 0, 0, tiled=True)
    grad = jnp.concatenate([grad[z] for z in range(shards)], axis=1)
    for turn, bit in enumerate(joins):
        if turn == 1:
            grad = after(grad, summed)
        grad = jnp.concatenate(joined(grad, bit, (here >> bit) & 1))
    thirds = [
        jnp.concatenate(
            [
                grad[:, (3 * z + third) * group : (3 * z + third + 1) * group]
                for z in range(shards)
            ],
            axis=1,
        )[:, :width]
        for third in range(3)
    ]
    qkv_grad = jnp.concatenate(thirds, axis=1).astype(f32)

    return (
        jnp.stack([part[0] for part in results]),
        jnp.stack([part[1] for part in results]),
        sums[0],
        sums[1],
        qkv_grad,
        sums[2],
        sums[3],
        proj_grad,
        sums[4],
        sums[5],
        sums[6],
        fc_grad,
        sums[8:].reshape(-1),
        out_grad,
        sums[7],
    )


def solution(mesh):
    tokens = P(None, ("ctx", "shard"), None)
    vector = P("shard")
    matrix = P("shard", None)
    return jax.shard_map(
        body,
        mesh=mesh,
        in_specs=(
            tokens,
            vector,
            vector,
            matrix,
            vector,
            vector,
            matrix,
            vector,
            vector,
            vector,
            matrix,
            vector,
            matrix,
            vector,
            tokens,
        ),
        out_specs=(
            tokens,
            tokens,
            vector,
            vector,
            matrix,
            vector,
            vector,
            matrix,
            vector,
            vector,
            vector,
            matrix,
            vector,
            matrix,
            vector,
        ),
        check_vma=False,
    )
```
